256 devices in a mesh: grp: 128 (over z, y, x), sub: 2 (over core).
Axes of the slice: x: 4, y: 4, z: 8, core: 2. Of those that a mesh axis runs over, the one named last changes fastest.
Arguments:
- fine_rows: bfloat16 [131072, 192], P(('grp', 'sub')), may hold values from -6 to 6
- qkv_weight: bfloat16 [192, 576], replicated, may hold values from -0.4375 to 0.4375
- out_weight: bfloat16 [192, 192], replicated, may hold values from -0.4375 to 0.4375
- pool_weight: bfloat16 [1536, 384], replicated, may hold values from -0.15625 to 0.15625
- coarse_qkv_weight: bfloat16 [3, 384, 384], P(None, None, 'sub'), may hold values from -0.3125 to 0.3125
- coarse_out_weight: bfloat16 [384, 384], P('sub'), may hold values from -0.3125 to 0.3125
- parent_index: int32 [131072], P(('grp', 'sub')), may hold values from 0 to 32767, as said below
- child_slot: int32 [131072], P(('grp', 'sub')), may hold values from 0 to 7
- out_grad: bfloat16 [32768, 384], P(('grp', 'sub')), may hold values from -6 to 6
Outputs:
- coarse_rows: bfloat16 [32768, 384], P(('grp', 'sub'))
- row_grad: bfloat16 [131072, 192], P(('grp', 'sub'))
- grad_qkv: float32 [192, 576], replicated
- grad_out: float32 [192, 192], replicated
- grad_pool: float32 [1536, 384], replicated
- grad_coarse_qkv: float32 [3, 384, 384], P(None, None, 'sub')
- grad_coarse_out: float32 [384, 384], P('sub')
The draws below stay inside these ranges and needn't reach their ends.
Inputs may be any that keep to these rules, and one draw needn't show every extreme that they name: parent_index never falls, the octants of one parent are consecutive, and every parent has 1 to 7 children with distinct, rising child_slot values. Parent p belongs to the device holding rows p // 128 * 512 onward: each device's rows belong to its own 128 parents, except its first 1 to 3 rows (none on the first device), which belong to the last parent of the device before it.
All inputs are finite; a program needn't handle non-finite values.
Results may differ from the reference program's by a relative error of at most 0.024.
Values may be sent and summed in bfloat16 or wider, within the bound.
No kernel may reach another device: no remote copies, remote signals or barrier semaphores. Data moves between devices by JAX's collectives and lax.ppermute only.
A program may use at most 64 MiB of HBM per device.

```python
import jax
import jax.numpy as jnp
from jax import lax

C1 = 192
C2 = 384
HD = 16
WINDOW_OCTANTS = 32
DILATION_STRIDE = 4
TOK_DEV = 512
PAR_DEV = 128
TOKENS = 131072
PARENTS = 32768
N_GRP = 128


def parent_layout(key):
    offset_key, boundary_key, slot_key = jax.random.split(key, 3)
    interior = jax.random.randint(offset_key, (PARENTS + 1,), 0, 4)
    boundary = jax.random.randint(boundary_key, (PARENTS + 1,), 1, 4)
    position = jnp.arange(PARENTS + 1, dtype=jnp.int32)
    offset = jnp.where(position % PAR_DEV == 0, boundary, interior)
    offset = jnp.where((position == 0) | (position == PARENTS), 0, offset)
    length = 4 + offset[1:] - offset[:-1]
    slot_gap = jax.random.randint(slot_key, (PARENTS,), 0, 9 - length)
    return (offset, slot_gap)


def parent_of_children(offset):
    children = jnp.arange(TOKENS, dtype=jnp.int32)
    nearest = children // 4
    first_child = 4 * nearest + offset[:-1][nearest]
    return (children, jnp.where(children >= first_child, nearest, nearest - 1).astype(jnp.int32))


def draw_parent_index(key, part):
    offset, slot_gap = parent_layout(key)
    children, parent = parent_of_children(offset)
    return parent


def draw_child_slot(key, part):
    offset, slot_gap = parent_layout(key)
    children, parent = parent_of_children(offset)
    first_child = 4 * parent + offset[parent]
    return (children - first_child + slot_gap[parent]).astype(jnp.int32)


def steps_of(rng, shape, shards, least, top_value):
    def one(axis_at, shards_of):
        draws = jax.random.uniform(jax.random.fold_in(jax.random.fold_in(rng, 6), axis_at), (shards_of,), jnp.float32, least / len(shards), top_value / len(shards))
        return jnp.repeat(jnp.exp(draws), shape[axis_at] // shards_of).reshape((-1,) + (1,) * (len(shape) - axis_at - 1))

    gain = one(*shards[0])
    for cut in shards[1:]:
        gain = gain * one(*cut)
    return gain


def gaussian(key, shape, spread, reach, cuts=(), held_as=jnp.bfloat16):
    gain = steps_of(key, shape, cuts, -0.22, 0.18) if cuts else 1.0
    entries = jax.random.normal(key, shape, jnp.float32) * spread * gain
    return jnp.minimum(jnp.maximum(entries, -reach), reach).astype(held_as)


def setup_inputs(seed: int = 0) -> dict:
    seeds = jax.random.split(jax.random.key(seed), 10)
    return {
        "fine_rows": gaussian(seeds[0], (TOKENS, C1), 1.0, 6.0, ((0, 256),)),
        "qkv_weight": gaussian(seeds[1], (C1, 3 * C1), C1 ** -0.5, 0.4375),
        "out_weight": gaussian(seeds[2], (C1, C1), C1 ** -0.5, 0.4375),
        "pool_weight": gaussian(seeds[3], (8 * C1, C2), (8 * C1) ** -0.5, 0.15625),
        "coarse_qkv_weight": gaussian(seeds[4], (3, C2, C2), C2 ** -0.5, 0.3125, ((2, 2),)),
        "coarse_out_weight": gaussian(seeds[5], (C2, C2), C2 ** -0.5, 0.3125, ((0, 2),)),
        "parent_index": draw_parent_index(jax.random.fold_in(seeds[9], 71), 0),
        "child_slot": draw_child_slot(jax.random.fold_in(seeds[9], 71), 0),
        "out_grad": gaussian(seeds[8], (PARENTS, C2), 1.0, 6.0, ((0, 256),)),
    }


EPSILON = 1e-05

def bround(value):
    return value.astype(jnp.bfloat16)

def multiply(form, left, right):
    return jnp.einsum(form, left.astype(jnp.float32), right.astype(jnp.float32))

def layer_norm(value):
    center = value - lax.optimization_barrier(jnp.mean(value, -1, keepdims=True))
    inverse = lax.rsqrt(lax.optimization_barrier(jnp.mean(center * center, -1, keepdims=True)) + EPSILON)
    return (center * inverse, inverse)

def layer_norm_back(normed, inverse, upstream):
    return inverse * (upstream - lax.optimization_barrier(jnp.mean(upstream, -1, keepdims=True)) - normed * lax.optimization_barrier(jnp.mean(upstream * normed, -1, keepdims=True)))

def split_heads(input_tensor, head_count):
    return input_tensor.reshape(input_tensor.shape[0], input_tensor.shape[1], head_count, input_tensor.shape[2] // head_count)

def to_windows(input_tensor):
    block_list = input_tensor.shape[0] // (WINDOW_OCTANTS * DILATION_STRIDE)
    channel_width = input_tensor.shape[-1]
    return input_tensor.reshape(block_list, WINDOW_OCTANTS, DILATION_STRIDE, channel_width).transpose(0, 2, 1, 3).reshape(block_list * DILATION_STRIDE, WINDOW_OCTANTS, channel_width)

def from_windows(input_tensor):
    channel_width = input_tensor.shape[-1]
    block_list = input_tensor.shape[0] // DILATION_STRIDE
    return input_tensor.reshape(block_list, DILATION_STRIDE, WINDOW_OCTANTS, channel_width).transpose(0, 2, 1, 3).reshape(block_list * WINDOW_OCTANTS * DILATION_STRIDE, channel_width)

def attention_probs(query_heads, key_heads, query_form, key_form):
    scaling = query_heads.shape[-1] ** (-0.5)
    exponent = jnp.exp(multiply(query_form + ',' + key_form + '->whjk', query_heads, key_heads) * scaling)
    return exponent / lax.optimization_barrier(jnp.sum(exponent, -1, keepdims=True))

def attend(queries, key_rows, values, head_count, layout):
    query_form = layout + 'hd'
    key_form = query_form.replace('j', 'k')
    query_heads = split_heads(queries, head_count)
    key_heads = split_heads(key_rows, head_count)
    value_heads = split_heads(values, head_count)
    attn_prob = attention_probs(query_heads, key_heads, query_form, key_form)
    mixed = multiply('whjk,' + key_form + '->' + query_form, bround(attn_prob), value_heads)
    return bround(mixed).reshape(queries.shape)

def attend_back(queries, key_rows, values, upstream, head_count, layout):
    query_form = layout + 'hd'
    key_form = query_form.replace('j', 'k')
    query_heads = split_heads(queries, head_count)
    key_heads = split_heads(key_rows, head_count)
    value_heads = split_heads(values, head_count)
    scaling = query_heads.shape[-1] ** (-0.5)
    attn_prob = attention_probs(query_heads, key_heads, query_form, key_form)
    up_heads = split_heads(upstream, head_count)
    grad_values = multiply('whjk,' + query_form + '->' + key_form, bround(attn_prob), up_heads)
    grad_prob = multiply(query_form + ',' + key_form + '->whjk', up_heads, value_heads)
    grad_score = bround(attn_prob * (grad_prob - lax.optimization_barrier(jnp.sum(attn_prob * grad_prob, -1, keepdims=True))) * scaling)
    grad_query = multiply('whjk,' + key_form + '->' + query_form, grad_score, key_heads)
    grad_keys = multiply('whjk,' + query_form + '->' + key_form, grad_score, query_heads)
    row_dimensions = queries.shape
    return (bround(grad_query).reshape(row_dimensions), bround(grad_keys).reshape(row_dimensions), bround(grad_values).reshape(row_dimensions))

def reference(fine_rows, qkv_weight, out_weight, pool_weight, coarse_qkv_weight, coarse_out_weight, parent_index, child_slot, out_grad):
    fine_heads = C1 // HD
    coarse_heads = C2 // HD
    rows_float = fine_rows.astype(jnp.float32)
    normed, inverse = layer_norm(rows_float)
    attn_input = bround(normed)
    qkv = bround(jnp.dot(attn_input, qkv_weight, preferred_element_type=jnp.float32))
    qkv_slabs = qkv.reshape(-1, TOK_DEV, 3 * C1)

    def fine_block(slab):
        block = to_windows(slab)
        return from_windows(attend(block[..., :C1], block[..., C1:2 * C1], block[..., 2 * C1:], fine_heads, 'wj'))
    mixed = lax.map(fine_block, qkv_slabs).reshape(TOKENS, C1)
    hidden = bround(rows_float + jnp.dot(mixed, out_weight, preferred_element_type=jnp.float32))
    pooled = jnp.zeros((PARENTS, 8, C1), jnp.bfloat16).at[parent_index, child_slot].set(hidden)
    pooled_flat = pooled.reshape(PARENTS, 8 * C1)
    parents = bround(jnp.dot(pooled_flat, pool_weight, preferred_element_type=jnp.float32))
    parents_float = parents.astype(jnp.float32)
    coarse_normed, coarse_inverse = layer_norm(parents_float)
    coarse_input = bround(coarse_normed)
    coarse_parts = [bround(jnp.dot(coarse_input, coarse_qkv_weight[which], preferred_element_type=jnp.float32)) for which in range(3)]
    coarse_blocks = jnp.stack(coarse_parts, 0).reshape(3, N_GRP, -1, WINDOW_OCTANTS, C2)

    def pooled_window_block(block):
        return attend(block[0], block[1], block[2], coarse_heads, 'wj')
    coarse_mixed = lax.map(pooled_window_block, jnp.moveaxis(coarse_blocks, 1, 0)).reshape(PARENTS, C2)
    coarse_pre = parents_float + jnp.dot(coarse_mixed, coarse_out_weight, preferred_element_type=jnp.float32)
    coarse_rows = bround(coarse_pre)
    coarse_scale = PARENTS ** (-0.5)
    fine_scale = TOKENS ** (-0.5)
    grad_coarse_out = jnp.dot(coarse_mixed.T, out_grad, preferred_element_type=jnp.float32) * coarse_scale
    grad_cmixed = bround(jnp.dot(out_grad, coarse_out_weight.T, preferred_element_type=jnp.float32))
    cmixed_blocks = grad_cmixed.reshape(N_GRP, -1, WINDOW_OCTANTS, C2)

    def coarse_back(pair):
        block, upstream = pair
        return jnp.stack(attend_back(block[0], block[1], block[2], upstream, coarse_heads, 'wj'), 0)
    grad_cqkv = lax.map(coarse_back, (jnp.moveaxis(coarse_blocks, 1, 0), cmixed_blocks))
    grad_cqkv = jnp.moveaxis(grad_cqkv, 1, 0).reshape(3, PARENTS, C2)
    grad_coarse_qkv = jnp.stack([jnp.dot(coarse_input.T, grad_cqkv[which], preferred_element_type=jnp.float32) for which in range(3)], 0) * coarse_scale
    grad_cnormed = jnp.dot(grad_cqkv[0], coarse_qkv_weight[0].T, preferred_element_type=jnp.float32) + jnp.dot(grad_cqkv[1], coarse_qkv_weight[1].T, preferred_element_type=jnp.float32) + jnp.dot(grad_cqkv[2], coarse_qkv_weight[2].T, preferred_element_type=jnp.float32)
    parent_gradient = bround(out_grad.astype(jnp.float32) + layer_norm_back(coarse_normed, coarse_inverse, grad_cnormed))
    grad_pool = jnp.dot(pooled_flat.T, parent_gradient, preferred_element_type=jnp.float32) * coarse_scale
    grad_pooled = bround(jnp.dot(parent_gradient, pool_weight.T, preferred_element_type=jnp.float32))
    grad_hidden = grad_pooled.reshape(PARENTS, 8, C1)[parent_index, child_slot]
    grad_out = jnp.dot(mixed.T, grad_hidden, preferred_element_type=jnp.float32) * fine_scale
    grad_mixed = bround(jnp.dot(grad_hidden, out_weight.T, preferred_element_type=jnp.float32))

    def fine_back(pair):
        slab, upstream = pair
        block = to_windows(slab)
        parts = attend_back(block[..., :C1], block[..., C1:2 * C1], block[..., 2 * C1:], to_windows(upstream), fine_heads, 'wj')
        return from_windows(jnp.concatenate(parts, -1))
    grad_qkv_rows = lax.map(fine_back, (qkv_slabs, grad_mixed.reshape(-1, TOK_DEV, C1))).reshape(TOKENS, 3 * C1)
    grad_qkv = jnp.dot(attn_input.T, grad_qkv_rows, preferred_element_type=jnp.float32) * fine_scale
    grad_normed = jnp.dot(grad_qkv_rows, qkv_weight.T, preferred_element_type=jnp.float32)
    row_grad = bround(grad_hidden.astype(jnp.float32) + layer_norm_back(normed, inverse, grad_normed))
    return (coarse_rows, row_grad, grad_qkv, grad_out, grad_pool, grad_coarse_qkv, grad_coarse_out)
```

```python
import functools

import jax
import jax.numpy as jnp
from jax import lax
from jax.experimental import pallas as pl
from jax.experimental.pallas import tpu as pltpu
from jax.sharding import Mesh, PartitionSpec as P

HD = 16
WINDOW_OCTANTS = 32
DILATION_STRIDE = 4
SLOTS = 8
LANES = 128
SPILL = 16
EPSILON = 1e-05
AXES = ("z", "y", "x", "sub")
VMEM_BYTES = 48 * 1024 * 1024
FAR = -1e30


def passed_along(shard, by):
    count = 1
    for name in AXES:
        count *= lax.axis_size(name)
    pairs = [(i, i + by) for i in range(count) if 0 <= i + by < count]
    return lax.ppermute(shard, AXES, pairs)


def swap_cores(shard):
    return lax.ppermute(shard, "sub", [(0, 1), (1, 0)])


def bround(value):
    return value.astype(jnp.bfloat16)


def product(left, right, left_dim, right_dim):
    return lax.dot_general(
        left, right, (((left_dim,), (right_dim,)), ((), ())), preferred_element_type=jnp.float32
    )


def nn(left, right):
    return product(left, right, 1, 0)


def nt(left, right):
    return product(left, right, 1, 1)


def tn(left, right):
    return product(left, right, 0, 0)


def indicator(condition):
    return bround(jnp.where(condition, 1.0, 0.0))


def layer_norm(value):
    center = value - jnp.mean(value, 0, keepdims=True)
    inverse = lax.rsqrt(jnp.mean(center * center, 0, keepdims=True) + EPSILON)
    return (center * inverse, inverse)


def layer_norm_back(normed, inverse, upstream):
    return inverse * (
        upstream
        - jnp.mean(upstream, 0, keepdims=True)
        - normed * jnp.mean(upstream * normed, 0, keepdims=True)
    )


def window_bias(same_window):
    key = lax.broadcasted_iota(jnp.int32, (LANES, LANES), 0)
    query = lax.broadcasted_iota(jnp.int32, (LANES, LANES), 1)
    return jnp.where(same_window(key) == same_window(query), 0.0, FAR)


def attention_probs(query, key, bias):
    score = tn(key, query * jnp.bfloat16(HD**-0.5)) + bias
    exponent = jnp.exp(score - jnp.max(score, 0, keepdims=True))
    return exponent * (1.0 / jnp.sum(exponent, 0, keepdims=True))


def attend_back(query, key, value, prob, upstream):
    grad_prob = tn(value, upstream * jnp.bfloat16(HD**-0.5))
    grad_score = bround(prob * (grad_prob - jnp.sum(prob * grad_prob, 0, keepdims=True)))
    grad_value = nt(upstream, bround(prob))
    grad_query = nn(key, grad_score)
    grad_key = nt(query, grad_score)
    return (bround(grad_query), bround(grad_key), bround(grad_value))


def fine_forward(
    rows, qkv_weight, out_weight, codes, hidden, mixed, qkv, probs, spill
):
    channels = rows.shape[1]
    rows_float = rows[...].astype(jnp.float32).T
    normed, _ = layer_norm(rows_float)
    qkv[...] = bround(tn(qkv_weight[...], bround(normed)))
    bias = window_bias(lambda at: at % DILATION_STRIDE)
    heads = channels // HD
    for block in range(rows.shape[0] // LANES):
        lanes = slice(block * LANES, (block + 1) * LANES)
        for head in range(heads):
            at = head * HD
            query = qkv[at : at + HD, lanes]
            key = qkv[channels + at : channels + at + HD, lanes]
            value = qkv[2 * channels + at : 2 * channels + at + HD, lanes]
            prob = bround(attention_probs(query, key, bias))
            probs[block * heads + head] = prob
            mixed[at : at + HD, lanes] = bround(nn(value, prob))
    total = bround(rows_float + tn(out_weight[...], mixed[...]))
    hidden[...] = total
    slot = lax.broadcasted_iota(jnp.int32, (SPILL, LANES), 0)
    leading = indicator(codes[:, :LANES] == slot - SLOTS)
    spill[...] = bround(nt(leading, total[:, :LANES]))


def coarse_both(
    core_ref,
    hidden,
    codes,
    spill,
    pool_weight,
    own_qkv,
    other_qkv,
    own_out,
    other_out,
    out_grad,
    coarse_rows,
    grad_hidden,
    spill_grad,
    keep,
    give,
    pooled,
    mixed,
    grads,
):
    core = core_ref[0]
    owned, wide = out_grad.shape
    channels, row_count = hidden.shape
    part = own_out.shape[0]
    parent = lax.broadcasted_iota(jnp.int32, (owned, row_count), 0)
    slot_of = codes[...] - parent * SLOTS
    spill_slot = lax.broadcasted_iota(jnp.int32, (SPILL, owned), 0)
    last = lax.broadcasted_iota(jnp.int32, (SPILL, owned), 1) == owned - 1
    total = jnp.zeros((owned, wide), jnp.float32)
    for slot in range(SLOTS):
        edge = indicator(last & (spill_slot == slot))
        children = nt(hidden[...], indicator(slot_of == slot)) + tn(spill[...], edge)
        pooled[slot] = bround(children)
        total += tn(bround(children), pool_weight[slot * channels : (slot + 1) * channels])
    parents = bround(total).astype(jnp.float32)
    normed, inverse = layer_norm(parents.T)
    coarse_input = bround(normed)
    upstream = out_grad[...]
    bias = window_bias(lambda at: at // WINDOW_OCTANTS)
    weights = ((own_qkv, own_out), (other_qkv, other_out))
    grad_normed = jnp.zeros((wide, owned), jnp.float32)
    summed = jnp.zeros((owned, wide), jnp.float32)
    for half, (qkv_weight, out_weight) in enumerate(weights):
        queries, keys, values = (
            bround(tn(qkv_weight[which], coarse_input)) for which in range(3)
        )
        grad_mixed = bround(nt(out_weight[...], upstream))
        for head in range(part // HD):
            at = slice(head * HD, (head + 1) * HD)
            prob = attention_probs(queries[at], keys[at], bias)
            mixed[at] = bround(nn(values[at], bround(prob)))
            back = attend_back(queries[at], keys[at], values[at], prob, grad_mixed[at])
            for which in range(3):
                start = which * part + head * HD
                grads[start : start + HD] = back[which]
        summed += tn(mixed[...], out_weight[...])
        for which in range(3):
            grad_normed += nn(qkv_weight[which], grads[which * part : (which + 1) * part])
        target = give if half else keep
        grad_qkv = bround(nt(coarse_input, grads[...]))
        whole = 3 * part // LANES
        for panel in range(whole):
            target[panel * wide : (panel + 1) * wide] = grad_qkv[
                :, panel * LANES : (panel + 1) * LANES
            ]
        tail = grad_qkv[:, whole * LANES :]
        base = whole * wide
        target[base : base + part] = jnp.concatenate([tail[:part], tail[part:]], 1)
        base += part
        grad_out = bround(nn(mixed[...], upstream))
        for panel in range(wide // LANES):
            target[base + panel * part : base + (panel + 1) * part] = grad_out[
                :, panel * LANES : (panel + 1) * LANES
            ]
    coarse_rows[...] = bround(parents + summed)
    grad_parents = bround(
        upstream.astype(jnp.float32).T + layer_norm_back(normed, inverse, grad_normed)
    )
    base = 4 * part * wide // LANES
    panels = wide // LANES
    for target, first in ((keep, core), (give, 1 - core)):
        for step in range(SLOTS // 2):
            grad_pool = bround(nt(pooled[first * (SLOTS // 2) + step], grad_parents))
            for panel in range(panels):
                start = base + (step * panels + panel) * channels
                target[start : start + channels] = grad_pool[
                    :, panel * LANES : (panel + 1) * LANES
                ]
    grad_total = jnp.zeros((channels, row_count), jnp.float32)
    edge_total = jnp.zeros((SPILL, channels), jnp.float32)
    for slot in range(SLOTS):
        weight = pool_weight[slot * channels : (slot + 1) * channels]
        grad_pooled = bround(nn(weight, grad_parents))
        grad_total += nn(grad_pooled, indicator(slot_of == slot))
        edge_total += nt(indicator(last & (spill_slot == slot)), grad_pooled)
    grad_hidden[...] = bround(grad_total)
    spill_grad[...] = bround(edge_total)


def fine_back(
    core_ref,
    rows,
    grad_hidden,
    spill_grad,
    codes,
    probs,
    qkv,
    mixed,
    qkv_weight,
    out_weight,
    row_grad,
    keep,
    give,
    upstream,
    grads,
):
    core = core_ref[0]
    row_count, channels = rows.shape
    normed, inverse = layer_norm(rows[...].astype(jnp.float32).T)
    slot = lax.broadcasted_iota(jnp.int32, (SPILL, LANES), 0)
    leading = indicator(codes[:, :LANES] == slot - SLOTS)
    upstream[...] = grad_hidden[...]
    upstream[:, :LANES] = bround(
        grad_hidden[:, :LANES].astype(jnp.float32) + tn(spill_grad[...], leading)
    )
    grad_mixed = bround(nn(out_weight[...], upstream[...]))
    heads = channels // HD
    for block in range(row_count // LANES):
        lanes = slice(block * LANES, (block + 1) * LANES)
        for head in range(heads):
            at = [which * channels + head * HD for which in range(3)]
            query, key, value = (qkv[start : start + HD, lanes] for start in at)
            prob = probs[block * heads + head].astype(jnp.float32)
            back = attend_back(
                query, key, value, prob, grad_mixed[head * HD : (head + 1) * HD, lanes]
            )
            for which in range(3):
                grads[at[which] : at[which] + HD, lanes] = back[which]
    grad_normed = nn(qkv_weight[...], grads[...])
    total = upstream[...].astype(jnp.float32) + layer_norm_back(normed, inverse, grad_normed)
    row_grad[...] = bround(total.T)
    grad_qkv = bround(nt(bround(normed), grads[...]))
    grad_out = bround(nt(mixed[...], upstream[...]))
    whole = 3 * channels // LANES
    panels = [grad_qkv[:, i * LANES : (i + 1) * LANES] for i in range(whole)]
    panels.append(jnp.concatenate([grad_qkv[:, whole * LANES :], grad_out[:, LANES:]], 1))
    panels.append(grad_out[:, :LANES])
    half = len(panels) // 2
    for i in range(half):
        at = slice(i * channels, (i + 1) * channels)
        keep[at] = jnp.where(core == 0, panels[i], panels[half + i])
        give[at] = jnp.where(core == 0, panels[half + i], panels[i])


def assemble(
    fine_scale,
    coarse_scale,
    core_ref,
    mine,
    other,
    grad_qkv,
    grad_out,
    grad_pool,
    grad_coarse_qkv,
    grad_coarse_out,
):
    core = core_ref[0]
    channels = grad_out.shape[0]
    part, wide = grad_coarse_out.shape
    edge = part % LANES

    def coarse(start, count):
        return mine[start : start + count].astype(jnp.float32) * coarse_scale

    panels = [coarse(i * wide, wide) for i in range(4)]
    base = 4 * wide
    tail = coarse(base, part)
    grad_coarse_qkv[0, :, :LANES] = panels[0]
    grad_coarse_qkv[0, :, LANES:] = panels[1][:, :edge]
    grad_coarse_qkv[1] = jnp.concatenate([panels[1][:, edge:], panels[2]], 1)
    grad_coarse_qkv[2, :, :LANES] = panels[3]
    grad_coarse_qkv[2, :part, LANES:] = tail[:, :edge]
    grad_coarse_qkv[2, part:, LANES:] = tail[:, edge:]
    base += part
    for panel in range(wide // LANES):
        grad_coarse_out[:, panel * LANES : (panel + 1) * LANES] = coarse(base, part)
        base += part
    first = base
    pool_panels = wide // LANES
    half_rows = SLOTS // 2 * channels
    for source, start, half in ((mine, first, core), (other, 0, 1 - core)):
        for step in range(SLOTS // 2):
            row = pl.multiple_of(half * half_rows + step * channels, 8)
            for panel in range(pool_panels):
                at = start + (step * pool_panels + panel) * channels
                grad_pool[pl.ds(row, channels), panel * LANES : (panel + 1) * LANES] = (
                    source[at : at + channels].astype(jnp.float32) * coarse_scale
                )
    skip = half_rows * pool_panels
    fine = []
    for half in range(2):
        for i in range(3):
            at = skip + i * channels
            near = mine[first + at : first + at + channels].astype(jnp.float32)
            far = other[at : at + channels].astype(jnp.float32)
            fine.append(jnp.where(core == half, near, far) * fine_scale)
    for i in range(4):
        grad_qkv[:, i * LANES : (i + 1) * LANES] = fine[i]
    grad_qkv[:, 4 * LANES :] = fine[4][:, :edge]
    grad_out[:, :LANES] = fine[5]
    grad_out[:, LANES:] = fine[4][:, edge:]


def call(kernel, outs, scratch, *operands, scalars=1, cost=0):
    specs = [pl.BlockSpec(memory_space=pltpu.SMEM)] * scalars
    specs += [pl.BlockSpec(memory_space=pltpu.VMEM)] * (len(operands) - scalars)
    return pl.pallas_call(
        kernel,
        out_shape=[jax.ShapeDtypeStruct(shape, dtype) for shape, dtype in outs],
        in_specs=specs,
        out_specs=[pl.BlockSpec(memory_space=pltpu.VMEM)] * len(outs),
        scratch_shapes=[pltpu.VMEM(shape, jnp.bfloat16) for shape in scratch],
        compiler_params=pltpu.CompilerParams(vmem_limit_bytes=VMEM_BYTES),
        cost_estimate=pl.CostEstimate(
            flops=cost, bytes_accessed=4 * 1024 * 1024, transcendentals=0
        ),
    )(*operands)


def float_sum(stacked):
    return bround(jnp.sum(stacked.astype(jnp.float32), 0))


def sum_over_chips(parts):
    plane = lax.all_to_all(parts, ("y", "x"), 0, 0, tiled=True)
    slab = float_sum(plane)
    copies = jnp.broadcast_to(slab, (lax.axis_size("z"),) + slab.shape)
    slab = float_sum(lax.all_to_all(copies, "z", 0, 0, tiled=True))
    copies = jnp.broadcast_to(slab, parts.shape)
    return lax.all_to_all(copies, ("y", "x"), 0, 0, tiled=True)


def on_device(
    fine_rows,
    qkv_weight,
    out_weight,
    pool_weight,
    coarse_qkv_weight,
    coarse_out_weight,
    parent_index,
    child_slot,
    out_grad,
):
    bf16, f32 = jnp.bfloat16, jnp.float32
    devices = 1
    for name in AXES:
        devices *= lax.axis_size(name)
    row_count, channels = fine_rows.shape
    owned, wide = out_grad.shape
    part = coarse_out_weight.shape[0]
    blocks = row_count // LANES
    heads = channels // HD
    core = lax.axis_index("sub").astype(jnp.int32).reshape(1)
    other_qkv = swap_cores(coarse_qkv_weight)
    other_out = swap_cores(coarse_out_weight)
    first_parent = lax.axis_index(AXES) * owned
    codes = ((parent_index - first_parent) * SLOTS + child_slot).reshape(1, row_count)
    coarse_count = 4 * part * wide // LANES
    pool_count = SLOTS // 2 * channels * wide // LANES
    fine_count = 2 * channels * channels // LANES

    hidden, mixed, qkv, probs, spill = call(
        fine_forward,
        [
            ((channels, row_count), bf16),
            ((channels, row_count), bf16),
            ((3 * channels, row_count), bf16),
            ((blocks * heads, LANES, LANES), bf16),
            ((SPILL, channels), bf16),
        ],
        [],
        fine_rows,
        qkv_weight,
        out_weight,
        codes,
        scalars=0,
        cost=10**10,
    )
    spill_in = passed_along(spill, -1)
    coarse_rows, grad_hidden, spill_grad, keep, give = call(
        coarse_both,
        [
            ((owned, wide), bf16),
            ((channels, row_count), bf16),
            ((SPILL, channels), bf16),
            ((coarse_count + pool_count, LANES), bf16),
            ((coarse_count + pool_count, LANES), bf16),
        ],
        [(SLOTS, channels, owned), (part, owned), (3 * part, owned)],
        core,
        hidden,
        codes,
        spill_in,
        pool_weight,
        coarse_qkv_weight,
        other_qkv,
        coarse_out_weight,
        other_out,
        out_grad,
        cost=10**10,
    )
    spill_back = passed_along(spill_grad, 1)
    got = swap_cores(give)
    row_grad, fine_keep, fine_give = call(
        fine_back,
        [
            ((row_count, channels), bf16),
            ((fine_count, LANES), bf16),
            ((fine_count, LANES), bf16),
        ],
        [(channels, row_count), (3 * channels, row_count)],
        core,
        fine_rows,
        grad_hidden,
        spill_back,
        codes,
        probs,
        qkv,
        mixed,
        qkv_weight,
        out_weight,
        cost=10**10,
    )
    fine_got = swap_cores(fine_give)
    plane = lax.axis_size("y") * lax.axis_size("x")
    count = coarse_count + pool_count + fine_count
    unit = plane * 8
    padded = -(-count // unit) * unit
    rows = jnp.concatenate(
        [
            bround(keep.astype(f32) + got.astype(f32)),
            bround(fine_keep.astype(f32) + fine_got.astype(f32)),
            jnp.zeros((padded - count, LANES), bf16),
        ],
        0,
    )
    total = sum_over_chips(rows.reshape(plane, padded // plane, LANES)).reshape(padded, LANES)
    other = swap_cores(total[coarse_count:count])
    grad_qkv, grad_out, grad_pool, grad_coarse_qkv, grad_coarse_out = call(
        functools.partial(
            assemble, (row_count * devices) ** (-0.5), (owned * devices) ** (-0.5)
        ),
        [
            ((channels, 3 * channels), f32),
            ((channels, channels), f32),
            ((SLOTS * channels, wide), f32),
            ((3, wide, part), f32),
            ((part, wide), f32),
        ],
        [],
        core,
        total,
        other,
    )
    return (
        coarse_rows,
        row_grad,
        grad_qkv,
        grad_out,
        grad_pool,
        grad_coarse_qkv,
        grad_coarse_out,
    )


def solution(mesh):
    torus = Mesh(mesh.devices.reshape(-1, 4, 4, mesh.shape["sub"]), AXES)
    in_specs = (
        P(AXES, None),
        P(),
        P(),
        P(),
        P(None, None, "sub"),
        P("sub", None),
        P(AXES),
        P(AXES),
        P(AXES, None),
    )
    out_specs = (
        P(AXES, None),
        P(AXES, None),
        P(),
        P(),
        P(),
        P(None, None, "sub"),
        P("sub", None),
    )
    return jax.shard_map(
        on_device, mesh=torus, in_specs=in_specs, out_specs=out_specs, check_vma=False
    )
```

```python
import functools

import jax
import jax.numpy as jnp
from jax import lax
from jax.experimental import pallas as pl
from jax.experimental.pallas import tpu as pltpu
from jax.sharding import Mesh, PartitionSpec as P

HD = 16
WINDOW_OCTANTS = 32
DILATION_STRIDE = 4
SLOTS = 8
LANES = 128
SPILL = 16
EPSILON = 1e-05
NEAR = ("zl", "y", "x")
AXES = ("zh",) + NEAR + ("sub",)
VMEM_BYTES = 20 * 1024 * 1024
FAR = -1e30


def passed_along(shard, by):
    count = 1
    for name in AXES:
        count *= lax.axis_size(name)
    pairs = [(i, i + by) for i in range(count) if 0 <= i + by < count]
    return lax.ppermute(shard, AXES, pairs)


def swap_cores(shard):
    return lax.ppermute(shard, "sub", [(0, 1), (1, 0)])


def bround(value):
    return value.astype(jnp.bfloat16)


def product(left, right, left_dim, right_dim):
    return lax.dot_general(
        left, right, (((left_dim,), (right_dim,)), ((), ())), preferred_element_type=jnp.float32
    )


def nn(left, right):
    return product(left, right, 1, 0)


def nt(left, right):
    return product(left, right, 1, 1)


def tn(left, right):
    return product(left, right, 0, 0)


def indicator(condition):
    return bround(jnp.where(condition, 1.0, 0.0))


def layer_norm(value, axis):
    center = value - jnp.mean(value, axis, keepdims=True)
    inverse = lax.rsqrt(jnp.mean(center * center, axis, keepdims=True) + EPSILON)
    return (center * inverse, inverse)


def layer_norm_back(normed, inverse, upstream, axis):
    return inverse * (
        upstream
        - jnp.mean(upstream, axis, keepdims=True)
        - normed * jnp.mean(upstream * normed, axis, keepdims=True)
    )


def window_rows(window_of):
    row = lax.broadcasted_iota(jnp.int32, (SPILL, LANES), 0)
    lane = lax.broadcasted_iota(jnp.int32, (SPILL, LANES), 1)
    return indicator(window_of(lane) == row)


def mask_rows(window_of, heads):
    row = lax.broadcasted_iota(jnp.int32, (SPILL, LANES), 0)
    lane = lax.broadcasted_iota(jnp.int32, (SPILL, LANES), 1)
    other = (window_of(lane) != row) & (row < LANES // WINDOW_OCTANTS)
    return jnp.concatenate([bround(jnp.where(other, FAR, 0.0))] * heads, 1)


def fine_window(at):
    return at % DILATION_STRIDE


def coarse_window(at):
    return at // WINDOW_OCTANTS


def spread(wide, rows, heads):
    for head in range(heads):
        at = slice(head * HD, (head + 1) * HD)
        wide[at, head * LANES : (head + 1) * LANES] = rows[at]


def softmax_parts(score):
    exponent = jnp.exp(score - jnp.max(score, 0, keepdims=True))
    return (bround(exponent), 1.0 / jnp.sum(exponent, 0, keepdims=True))


def attend_back(query, key, upstream, exponent, inverse, grad_prob):
    weighted = exponent.astype(jnp.float32)
    mean = inverse * jnp.sum(weighted * grad_prob, 0, keepdims=True)
    grad_score = bround(weighted * (grad_prob - mean))
    grad_value = nt(bround(upstream.astype(jnp.float32) * inverse), exponent)
    grad_query = nn(key, grad_score)
    grad_key = nt(query, grad_score)
    return (bround(grad_query), bround(grad_key), bround(grad_value))


def scaled(value):
    return value * jnp.bfloat16(HD**-0.5)


def fine_attention(qkv, wide, classes, heads, mixed, store):
    channels = heads * HD
    spread(wide, scaled(qkv[:channels]), heads)
    keys = jnp.concatenate([qkv[channels : 2 * channels], classes], 0)
    scores = tn(keys, wide[...])
    for head in range(heads):
        exponent, inverse = softmax_parts(scores[:, head * LANES : (head + 1) * LANES])
        value = qkv[2 * channels + head * HD : 2 * channels + (head + 1) * HD]
        mixed[head * HD : (head + 1) * HD] = bround(nn(value, exponent) * inverse)
        if store is not None:
            store(head, exponent, inverse)


def clear_wide(wide, heads, window_of):
    wide[...] = jnp.zeros(wide.shape, wide.dtype)
    for slot in range(wide.shape[0]):
        wide[slot, heads * HD :] = mask_rows(window_of, heads)


def fine_forward(
    rows_in,
    qkv_in,
    out_in,
    rows,
    qkv_weight,
    out_weight,
    hidden,
    mixed,
    qkv,
    exponents,
    inverses,
    wide,
    arrived,
):
    pairs = ((rows_in, rows), (qkv_in, qkv_weight), (out_in, out_weight))
    copies = [
        pltpu.make_async_copy(source, target, arrived.at[i])
        for i, (source, target) in enumerate(pairs)
    ]
    for copy in copies:
        copy.start()
    channels, count = hidden.shape
    heads = channels // HD
    clear_wide(wide, heads, fine_window)
    classes = window_rows(fine_window)
    copies[0].wait()
    copies[1].wait()
    rows_float = rows[...].astype(jnp.float32)
    normed, _ = layer_norm(rows_float, 0)
    qkv[...] = bround(tn(qkv_weight[...], bround(normed)))
    for block in range(count // LANES):
        lanes = slice(block * LANES, (block + 1) * LANES)

        def store(head, exponent, inverse):
            exponents[block, :, head * LANES : (head + 1) * LANES] = exponent
            at = block * heads + head
            inverses[at : at + 1] = inverse

        fine_attention(
            qkv[:, lanes],
            wide.at[block % wide.shape[0]],
            classes,
            heads,
            mixed.at[:, lanes],
            store,
        )
    copies[2].wait()
    hidden[...] = bround(rows_float + tn(out_weight[...], mixed[...]))


def leading_slots(parent_index, child_slot, first_parent):
    slot = lax.broadcasted_iota(jnp.int32, (SPILL, LANES), 0)
    before = parent_index[:, :LANES] < first_parent[0]
    return indicator(before & (child_slot[:, :LANES] == slot))


def slot_numbers(parent_index, child_slot, first_parent, owned):
    parent = lax.broadcasted_iota(jnp.int32, (owned, parent_index.shape[1]), 0)
    mine = parent_index - first_parent[0] == parent
    return jnp.where(mine, child_slot, -1)


def coarse_both(
    first_parent,
    own_hidden,
    parent_index,
    child_slot,
    next_rows,
    next_parent,
    next_slot,
    fine_qkv,
    fine_out,
    pool_weight,
    own_qkv,
    other_qkv,
    own_out,
    other_out,
    out_grad,
    coarse_rows,
    spill_grad,
    grad_parents,
    pooled,
    grad_pooled,
    coarse_input,
    mixed,
    grads,
    hidden,
    next_mixed,
    wide_next,
    wide_query,
    wide_grad,
):
    owned, width = out_grad.shape
    channels, row_count = own_hidden.shape
    part = own_out.shape[0]
    heads = part // HD
    fine_heads = channels // HD
    clear_wide(wide_next, fine_heads, fine_window)
    rows_float = next_rows[:, :LANES].astype(jnp.float32)
    normed, _ = layer_norm(rows_float, 0)
    fine_attention(
        bround(tn(fine_qkv[...], bround(normed))),
        wide_next.at[0],
        window_rows(fine_window),
        fine_heads,
        next_mixed,
        None,
    )
    hidden[:, :row_count] = own_hidden[...]
    hidden[:, row_count:] = bround(rows_float + tn(fine_out[...], next_mixed[...]))
    slot_of = slot_numbers(
        jnp.concatenate([parent_index[...], next_parent[:, :LANES]], 1),
        jnp.concatenate([child_slot[...], next_slot[:, :LANES]], 1),
        first_parent,
        owned,
    )
    total = jnp.zeros((owned, width), jnp.float32)
    for slot in range(0, SLOTS, 2):
        both = jnp.concatenate([indicator(slot_of == slot), indicator(slot_of == slot + 1)], 0)
        children = bround(nt(hidden[...], both))
        for i in range(2):
            chosen = children[:, i * owned : (i + 1) * owned]
            pooled[slot + i] = chosen
            at = (slot + i) * channels
            total += tn(chosen, pool_weight[at : at + channels])
    parents = bround(total).astype(jnp.float32)
    normed, inverse = layer_norm(parents, 1)
    coarse_input[...] = bround(normed)
    upstream = out_grad[...]
    classes = window_rows(coarse_window)
    grad_normed = jnp.zeros((owned, width), jnp.float32)
    summed = jnp.zeros((owned, width), jnp.float32)
    for wide in (wide_query, wide_grad):
        wide[...] = jnp.zeros(wide.shape, wide.dtype)
    weights = ((own_qkv, own_out), (other_qkv, other_out))
    for half, (qkv_weight, out_weight) in enumerate(weights):
        qkv = bround(nt(qkv_weight[...], coarse_input[...]))
        upward = bround(nt(out_weight[...], upstream))
        wide_query[half, part:] = mask_rows(coarse_window, heads)
        spread(wide_query.at[half], scaled(qkv[:part]), heads)
        keys = jnp.concatenate([qkv[part : 2 * part], classes], 0)
        scores = tn(keys, wide_query[half])
        parts = []
        for head in range(heads):
            at = slice(head * HD, (head + 1) * HD)
            exponent, scale = softmax_parts(scores[:, head * LANES : (head + 1) * LANES])
            parts.append((exponent, scale))
            value = qkv[2 * part + head * HD : 2 * part + (head + 1) * HD]
            mixed[half, at] = bround(nn(value, exponent) * scale)
            weighted = scaled(upward[at]).astype(jnp.float32) * scale
            wide_grad[half, at, head * LANES : (head + 1) * LANES] = bround(weighted)
        grad_probs = tn(qkv[2 * part :], wide_grad[half])
        for head in range(heads):
            at = [slice(i * part + head * HD, i * part + (head + 1) * HD) for i in range(3)]
            back = attend_back(
                qkv[at[0]],
                qkv[at[1]],
                upward[at[0]],
                *parts[head],
                grad_probs[:, head * LANES : (head + 1) * LANES],
            )
            for which in range(3):
                grads[half, at[which]] = back[which]
        summed += tn(mixed[half], out_weight[...])
        grad_normed += tn(grads[half], qkv_weight[...])
    coarse_rows[...] = bround(parents + summed)
    upstream_total = bround(
        upstream.astype(jnp.float32) + layer_norm_back(normed, inverse, grad_normed, 1)
    )
    grad_parents[...] = upstream_total
    spill_slot = lax.broadcasted_iota(jnp.int32, (SPILL, owned), 0)
    last = lax.broadcasted_iota(jnp.int32, (SPILL, owned), 1) == owned - 1
    edge_total = jnp.zeros((SPILL, channels), jnp.float32)
    for slot in range(SLOTS):
        weight = pool_weight[slot * channels : (slot + 1) * channels]
        grad_slot = bround(nt(weight, upstream_total))
        grad_pooled[slot] = grad_slot
        edge_total += nt(indicator(last & (spill_slot == slot)), grad_slot)
    spill_grad[...] = bround(edge_total)


def coarse_weights(
    core_ref,
    first_parent,
    parent_index,
    child_slot,
    grad_parents,
    pooled,
    grad_pooled,
    coarse_input,
    mixed,
    grads,
    out_grad,
    grad_hidden,
    keep,
    give,
):
    core = core_ref[0]
    owned, width = out_grad.shape
    channels, row_count = grad_hidden.shape
    part = mixed.shape[1]
    panels = width // LANES

    def store(target, start, value):
        for panel in range(panels):
            at = start + panel * value.shape[0]
            target[at : at + value.shape[0]] = bround(
                value[:, panel * LANES : (panel + 1) * LANES]
            )

    for half, target in enumerate((keep, give)):
        store(target, 0, nn(grads[half], coarse_input[...]))
        store(target, 3 * part * panels, nn(mixed[half], out_grad[...]))
    base = 4 * part * panels
    for target, first in ((keep, core), (give, 1 - core)):
        for step in range(SLOTS // 2):
            grad_pool = nn(pooled[first * (SLOTS // 2) + step], grad_parents[...])
            store(target, base + step * panels * channels, grad_pool)
    slot_of = slot_numbers(parent_index[...], child_slot[...], first_parent, owned)
    grad_total = jnp.zeros((channels, row_count), jnp.float32)
    for slot in range(SLOTS):
        grad_total += nn(grad_pooled[slot], indicator(slot_of == slot))
    grad_hidden[...] = bround(grad_total)


def fine_back(
    first_block,
    core_ref,
    first_parent,
    rows,
    grad_hidden,
    exponents,
    inverses,
    qkv,
    mixed,
    qkv_weight,
    out_weight,
    *rest,
):
    if first_block:
        row_grad, qkv_total, out_total, grads, wide = rest
        spill_grad = None
    else:
        spill_grad, parent_index, child_slot, row_rest, qkv_rest, out_rest = rest[:6]
        row_grad, keep, give, grads, wide = rest[6:]
    channels, count = grads.shape[0] // 3, grads.shape[1]
    heads = channels // HD
    span = slice(first_block * LANES, first_block * LANES + count)
    normed, inverse = layer_norm(rows[:, span].astype(jnp.float32), 0)
    upstream = grad_hidden[:, span]
    if spill_grad is not None:
        leading = leading_slots(parent_index, child_slot, first_parent)
        upstream = bround(upstream.astype(jnp.float32) + tn(spill_grad[...], leading))
    upward = bround(nn(out_weight[...], upstream))
    wide[...] = jnp.zeros(wide.shape, wide.dtype)
    for block in range(count // LANES):
        lanes = slice(block * LANES, (block + 1) * LANES)
        whole = first_block + block
        outer = slice(whole * LANES, (whole + 1) * LANES)
        grad_rows = wide.at[block % wide.shape[0]]
        scales = [
            inverses[whole * heads + head : whole * heads + head + 1] for head in range(heads)
        ]
        for head in range(heads):
            at = slice(head * HD, (head + 1) * HD)
            weighted = scaled(upward[at, lanes]).astype(jnp.float32) * scales[head]
            grad_rows[at, head * LANES : (head + 1) * LANES] = bround(weighted)
        grad_probs = tn(qkv[2 * channels :, outer], grad_rows[...])
        for head in range(heads):
            at = [slice(i * channels + head * HD, i * channels + (head + 1) * HD) for i in range(3)]
            out = slice(head * LANES, (head + 1) * LANES)
            back = attend_back(
                qkv[at[0], outer],
                qkv[at[1], outer],
                upward[at[0], lanes],
                exponents[whole, :, out],
                scales[head],
                grad_probs[:, out],
            )
            for which in range(3):
                grads[at[which], lanes] = back[which]
    grad_normed = nn(qkv_weight[...], grads[...])
    total = upstream.astype(jnp.float32) + layer_norm_back(normed, inverse, grad_normed, 0)
    grad_qkv = nt(bround(normed), grads[...])
    grad_out = nt(mixed[:, span], upstream)
    if first_block:
        row_grad[...] = bround(total)
        qkv_total[...] = grad_qkv
        out_total[...] = grad_out
        return
    row_grad[:, span] = bround(total)
    row_grad[:, count:] = row_rest[...]
    grad_qkv = bround(grad_qkv + qkv_rest[...])
    grad_out = bround(grad_out + out_rest[...])
    core = core_ref[0]
    whole = 3 * channels // LANES
    panels = [grad_qkv[:, i * LANES : (i + 1) * LANES] for i in range(whole)]
    panels.append(jnp.concatenate([grad_qkv[:, whole * LANES :], grad_out[:, LANES:]], 1))
    panels.append(grad_out[:, :LANES])
    half = len(panels) // 2
    for i in range(half):
        at = slice(i * channels, (i + 1) * channels)
        keep[at] = jnp.where(core == 0, panels[i], panels[half + i])
        give[at] = jnp.where(core == 0, panels[half + i], panels[i])


def merge(keep, got, fine_keep, fine_got, total):
    first, second = keep.shape[0], fine_keep.shape[0]
    total[:first] = keep[...] + got[...]
    total[first : first + second] = fine_keep[...] + fine_got[...]
    pad = total.shape[0] - first - second
    total[first + second :] = jnp.zeros((pad, LANES), total.dtype)


def assemble(
    fine_scale,
    coarse_scale,
    core_ref,
    mine,
    other,
    grad_qkv,
    grad_out,
    grad_pool,
    grad_coarse_qkv,
    grad_coarse_out,
):
    core = core_ref[0]
    channels = grad_out.shape[0]
    part, width = grad_coarse_out.shape
    panels = width // LANES
    edge = channels % LANES

    def coarse(start, count):
        return mine[start : start + count].astype(jnp.float32) * coarse_scale

    first = 3 * part * panels
    for panel in range(panels):
        lanes = slice(panel * LANES, (panel + 1) * LANES)
        for which in range(3):
            grad_coarse_qkv[which, :, lanes] = coarse((3 * panel + which) * part, part)
        grad_coarse_out[:, lanes] = coarse(first + panel * part, part)
    first += panels * part
    half_rows = SLOTS // 2 * channels
    for source, start, half in ((mine, first, core), (other, 0, 1 - core)):
        for step in range(SLOTS // 2):
            row = pl.multiple_of(half * half_rows + step * channels, 8)
            for panel in range(panels):
                at = start + (step * panels + panel) * channels
                grad_pool[pl.ds(row, channels), panel * LANES : (panel + 1) * LANES] = (
                    source[at : at + channels].astype(jnp.float32) * coarse_scale
                )
    skip = half_rows * panels
    fine = []
    for half in range(2):
        for i in range(3):
            at = skip + i * channels
            near = mine[first + at : first + at + channels].astype(jnp.float32)
            far = other[at : at + channels].astype(jnp.float32)
            fine.append(jnp.where(core == half, near, far) * fine_scale)
    for i in range(4):
        grad_qkv[:, i * LANES : (i + 1) * LANES] = fine[i]
    grad_qkv[:, 4 * LANES :] = fine[4][:, :edge]
    grad_out[:, :LANES] = fine[5]
    grad_out[:, LANES:] = fine[4][:, edge:]


def call(kernel, outs, scratch, *operands, scalars=1, micros=1, hbm=0, copies=0):
    spaces = [pltpu.SMEM] * scalars + [pltpu.HBM] * hbm
    spaces += [pltpu.VMEM] * (len(operands) - len(spaces))
    return pl.pallas_call(
        kernel,
        out_shape=[jax.ShapeDtypeStruct(shape, dtype) for shape, dtype in outs],
        in_specs=[pl.BlockSpec(memory_space=space) for space in spaces],
        out_specs=[pl.BlockSpec(memory_space=pltpu.VMEM)] * len(outs),
        scratch_shapes=[pltpu.VMEM(shape, jnp.bfloat16) for shape in scratch]
        + ([pltpu.SemaphoreType.DMA((copies,))] if copies else []),
        compiler_params=pltpu.CompilerParams(vmem_limit_bytes=VMEM_BYTES),
        cost_estimate=pl.CostEstimate(
            flops=int(micros * 10**9), bytes_accessed=int(micros * 10**6), transcendentals=0
        ),
    )(*operands)


def float_sum(stacked):
    return bround(jnp.sum(stacked.astype(jnp.float32), 0))


def sum_over_chips(parts):
    plane = lax.all_to_all(parts, NEAR, 0, 0, tiled=True)
    slab = float_sum(plane)
    copies = jnp.broadcast_to(slab, (lax.axis_size("zh"),) + slab.shape)
    slab = float_sum(lax.all_to_all(copies, "zh", 0, 0, tiled=True))
    copies = jnp.broadcast_to(slab, parts.shape)
    return lax.all_to_all(copies, NEAR, 0, 0, tiled=True)


def on_device(
    fine_rows,
    qkv_weight,
    out_weight,
    pool_weight,
    coarse_qkv_weight,
    coarse_out_weight,
    parent_index,
    child_slot,
    out_grad,
):
    bf16, f32 = jnp.bfloat16, jnp.float32
    devices = 1
    for name in AXES:
        devices *= lax.axis_size(name)
    row_count, channels = fine_rows.shape
    owned, width = out_grad.shape
    part = coarse_out_weight.shape[0]
    blocks = row_count // LANES
    heads = channels // HD
    coarse_heads = part // HD
    coarse_count = 4 * part * width // LANES
    pool_count = SLOTS // 2 * channels * width // LANES
    fine_count = 2 * channels * channels // LANES
    core = lax.axis_index("sub").astype(jnp.int32).reshape(1)
    first_parent = (lax.axis_index(AXES) * owned).astype(jnp.int32).reshape(1)
    rows = fine_rows.T
    parent_row = parent_index.reshape(1, row_count)
    slot_row = child_slot.reshape(1, row_count)
    own_qkv = coarse_qkv_weight.transpose(0, 2, 1).reshape(3 * part, width)
    other_qkv = swap_cores(own_qkv)
    other_out = swap_cores(coarse_out_weight)
    next_rows = passed_along(rows, -1)
    next_parent = passed_along(parent_row, -1)
    next_slot = passed_along(slot_row, -1)
    wide_rows = heads * LANES
    rows, fine_qkv, fine_out, hidden, mixed_fine, qkv, exponents, inverses = call(
        fine_forward,
        [
            ((channels, row_count), bf16),
            ((channels, 3 * channels), bf16),
            ((channels, channels), bf16),
            ((channels, row_count), bf16),
            ((channels, row_count), bf16),
            ((3 * channels, row_count), bf16),
            ((blocks, LANES, wide_rows), bf16),
            ((blocks * heads, LANES), f32),
        ],
        [(2, channels + SPILL, wide_rows)],
        *(
            pltpu.with_memory_space_constraint(array, pltpu.HBM)
            for array in (rows, qkv_weight, out_weight)
        ),
        scalars=0,
        hbm=3,
        copies=3,
        micros=4,
    )
    coarse_rows, spill_grad, grad_parents, pooled, grad_pooled, coarse_input, mixed, grads = call(
        coarse_both,
        [
            ((owned, width), bf16),
            ((SPILL, channels), bf16),
            ((owned, width), bf16),
            ((SLOTS, channels, owned), bf16),
            ((SLOTS, channels, owned), bf16),
            ((owned, width), bf16),
            ((2, part, owned), bf16),
            ((2, 3 * part, owned), bf16),
        ],
        [
            (channels, row_count + LANES),
            (channels, LANES),
            (1, channels + SPILL, wide_rows),
            (2, part + SPILL, coarse_heads * LANES),
            (2, part, coarse_heads * LANES),
        ],
        first_parent,
        hidden,
        parent_row,
        slot_row,
        next_rows,
        next_parent,
        next_slot,
        fine_qkv,
        fine_out,
        pool_weight,
        own_qkv,
        other_qkv,
        coarse_out_weight,
        other_out,
        out_grad,
        micros=9,
    )
    spill_back = passed_along(spill_grad, 1)
    grad_hidden, keep, give = call(
        coarse_weights,
        [
            ((channels, row_count), bf16),
            ((coarse_count + pool_count, LANES), bf16),
            ((coarse_count + pool_count, LANES), bf16),
        ],
        [],
        core,
        first_parent,
        parent_row,
        slot_row,
        grad_parents,
        pooled,
        grad_pooled,
        coarse_input,
        mixed,
        grads,
        out_grad,
        scalars=2,
        micros=1e-4,
    )
    got = swap_cores(give)
    shared = (
        core,
        first_parent,
        rows,
        grad_hidden,
        exponents,
        inverses,
        qkv,
        mixed_fine,
        fine_qkv,
        fine_out,
    )
    rest_count = row_count - LANES
    row_rest, qkv_rest, out_rest = call(
        functools.partial(fine_back, 1),
        [
            ((channels, rest_count), bf16),
            ((channels, 3 * channels), f32),
            ((channels, channels), f32),
        ],
        [(3 * channels, rest_count), (2, channels, wide_rows)],
        *shared,
        scalars=2,
        micros=1e-4,
    )
    row_grad, fine_keep, fine_give = call(
        functools.partial(fine_back, 0),
        [
            ((channels, row_count), bf16),
            ((fine_count, LANES), bf16),
            ((fine_count, LANES), bf16),
        ],
        [(3 * channels, LANES), (1, channels, wide_rows)],
        *shared,
        spill_back,
        parent_row,
        slot_row,
        row_rest,
        qkv_rest,
        out_rest,
        scalars=2,
        micros=2,
    )
    fine_got = swap_cores(fine_give)
    plane = lax.axis_size("zl") * lax.axis_size("y") * lax.axis_size("x")
    count = coarse_count + pool_count + fine_count
    unit = plane * 8
    padded = -(-count // unit) * unit
    (merged,) = call(
        merge, [((padded, LANES), bf16)], [], keep, got, fine_keep, fine_got, scalars=0, micros=1
    )
    total = sum_over_chips(merged.reshape(plane, padded // plane, LANES)).reshape(padded, LANES)
    other = swap_cores(total[coarse_count:count])
    grad_qkv, grad_out, grad_pool, grad_coarse_qkv, grad_coarse_out = call(
        functools.partial(
            assemble, (row_count * devices) ** (-0.5), (owned * devices) ** (-0.5)
        ),
        [
            ((channels, 3 * channels), f32),
            ((channels, channels), f32),
            ((SLOTS * channels, width), f32),
            ((3, part, width), f32),
            ((part, width), f32),
        ],
        [],
        core,
        total,
        other,
        micros=2,
    )
    return (
        coarse_rows,
        row_grad.T,
        grad_qkv,
        grad_out,
        grad_pool,
        grad_coarse_qkv.transpose(0, 2, 1),
        grad_coarse_out,
    )


def solution(mesh):
    torus = Mesh(mesh.devices.reshape(-1, 2, 4, 4, mesh.shape["sub"]), AXES)
    in_specs = (
        P(AXES, None),
        P(),
        P(),
        P(),
        P(None, None, "sub"),
        P("sub", None),
        P(AXES),
        P(AXES),
        P(AXES, None),
    )
    out_specs = (
        P(AXES, None),
        P(AXES, None),
        P(),
        P(),
        P(),
        P(None, None, "sub"),
        P("sub", None),
    )
    return jax.shard_map(
        on_device, mesh=torus, in_specs=in_specs, out_specs=out_specs, check_vma=False
    )
```

```python
import functools

import jax
import jax.numpy as jnp
from jax import lax
from jax.experimental import pallas as pl
from jax.experimental.pallas import tpu as pltpu
from jax.sharding import Mesh, PartitionSpec as P

HD = 16
WINDOW_OCTANTS = 32
DILATION_STRIDE = 4
SLOTS = 8
LANES = 128
SPILL = 16
EPSILON = 1e-05
NEAR = ("zl", "y", "x")
AXES = ("zh",) + NEAR + ("sub",)
VMEM_BYTES = 20 * 1024 * 1024
FAR = -1e30


def passed_along(shard, by):
    count = 1
    for name in AXES:
        count *= lax.axis_size(name)
    pairs = [(i, i + by) for i in range(count) if 0 <= i + by < count]
    return lax.ppermute(shard, AXES, pairs)


def swap_cores(shard):
    return lax.ppermute(shard, "sub", [(0, 1), (1, 0)])


def bround(value):
    return value.astype(jnp.bfloat16)


def product(left, right, left_dim, right_dim):
    return lax.dot_general(
        left, right, (((left_dim,), (right_dim,)), ((), ())), preferred_element_type=jnp.float32
    )


def nn(left, right):
    return product(left, right, 1, 0)


def nt(left, right):
    return product(left, right, 1, 1)


def tn(left, right):
    return product(left, right, 0, 0)


def indicator(condition):
    return bround(jnp.where(condition, 1.0, 0.0))


def layer_norm(value, axis):
    center = value - jnp.mean(value, axis, keepdims=True)
    inverse = lax.rsqrt(jnp.mean(center * center, axis, keepdims=True) + EPSILON)
    return (center * inverse, inverse)


def layer_norm_back(normed, inverse, upstream, axis):
    return inverse * (
        upstream
        - jnp.mean(upstream, axis, keepdims=True)
        - normed * jnp.mean(upstream * normed, axis, keepdims=True)
    )


def window_rows(window_of):
    row = lax.broadcasted_iota(jnp.int32, (SPILL, LANES), 0)
    lane = lax.broadcasted_iota(jnp.int32, (SPILL, LANES), 1)
    return indicator(window_of(lane) == row)


def mask_rows(window_of, heads):
    row = lax.broadcasted_iota(jnp.int32, (SPILL, LANES), 0)
    lane = lax.broadcasted_iota(jnp.int32, (SPILL, LANES), 1)
    other = (window_of(lane) != row) & (row < LANES // WINDOW_OCTANTS)
    return jnp.concatenate([bround(jnp.where(other, FAR, 0.0))] * heads, 1)


def fine_window(at):
    return at % DILATION_STRIDE


def coarse_window(at):
    return at // WINDOW_OCTANTS


def spread(wide, rows, heads):
    for head in range(heads):
        at = slice(head * HD, (head + 1) * HD)
        wide[at, head * LANES : (head + 1) * LANES] = rows[at]


def softmax_parts(score):
    exponent = jnp.exp(score - jnp.max(score, 0, keepdims=True))
    return (bround(exponent), 1.0 / jnp.sum(exponent, 0, keepdims=True))


def attend_back(query, key, upstream, exponent, inverse, grad_prob):
    weighted = exponent.astype(jnp.float32)
    mean = inverse * jnp.sum(weighted * grad_prob, 0, keepdims=True)
    grad_score = bround(weighted * (grad_prob - mean))
    grad_value = nt(bround(upstream.astype(jnp.float32) * inverse), exponent)
    grad_query = nn(key, grad_score)
    grad_key = nt(query, grad_score)
    return (bround(grad_query), bround(grad_key), bround(grad_value))


def scaled(value):
    return value * jnp.bfloat16(HD**-0.5)


def fine_attention(qkv, wide, classes, heads, mixed, store):
    channels = heads * HD
    spread(wide, scaled(qkv[:channels]), heads)
    keys = jnp.concatenate([qkv[channels : 2 * channels], classes], 0)
    scores = tn(keys, wide[...])
    for head in range(heads):
        exponent, inverse = softmax_parts(scores[:, head * LANES : (head + 1) * LANES])
        value = qkv[2 * channels + head * HD : 2 * channels + (head + 1) * HD]
        mixed[head * HD : (head + 1) * HD] = bround(nn(value, exponent) * inverse)
        if store is not None:
            store(head, exponent, inverse)


def clear_wide(wide, heads, window_of):
    wide[...] = jnp.zeros(wide.shape, wide.dtype)
    for slot in range(wide.shape[0]):
        wide[slot, heads * HD :] = mask_rows(window_of, heads)


def fetch(pairs, arrived):
    copies = [
        pltpu.make_async_copy(source, target, arrived.at[i])
        for i, (source, target) in enumerate(pairs)
    ]
    for copy in copies:
        copy.start()
    return copies


def fine_blocks(
    first, rows, qkv_weight, out_weight, hidden, mixed, qkv, exponents, inverses, wide, wait
):
    channels, count = hidden.shape
    heads = channels // HD
    clear_wide(wide, heads, fine_window)
    classes = window_rows(fine_window)
    wait(0)
    wait(1)
    rows_float = rows[:, first * LANES : first * LANES + count].astype(jnp.float32)
    normed, _ = layer_norm(rows_float, 0)
    qkv[...] = bround(tn(qkv_weight[...], bround(normed)))
    for block in range(count // LANES):
        lanes = slice(block * LANES, (block + 1) * LANES)

        def store(head, exponent, inverse):
            exponents[block, :, head * LANES : (head + 1) * LANES] = exponent
            at = block * heads + head
            inverses[at : at + 1] = inverse

        fine_attention(
            qkv[:, lanes],
            wide.at[block % wide.shape[0]],
            classes,
            heads,
            mixed.at[:, lanes],
            store,
        )
    wait(2)
    hidden[...] = bround(rows_float + tn(out_weight[...], mixed[...]))


def fine_first(first_parent, *refs):
    sources, targets = refs[:5], refs[5:10]
    hidden, mixed, qkv, exponents, inverses, spill, wide, arrived = refs[10:]
    rows, qkv_weight, out_weight, parent_index, child_slot = targets
    copies = fetch(tuple(zip(sources, targets)), arrived)
    fine_blocks(
        0,
        rows,
        qkv_weight,
        out_weight,
        hidden,
        mixed,
        qkv,
        exponents,
        inverses,
        wide,
        lambda i: copies[i].wait(),
    )
    copies[3].wait()
    copies[4].wait()
    spill[...] = bround(nt(leading_slots(parent_index, child_slot, first_parent), hidden[...]))


def fine_rest(*refs):
    sources, (rows, qkv_weight, out_weight) = refs[:4], refs[4:7]
    targets = refs[7:11]
    hidden, mixed, qkv, exponents, inverses, wide, arrived = refs[11:]
    copies = fetch(tuple(zip(sources, targets)), arrived)
    fine_blocks(
        1,
        rows,
        qkv_weight,
        out_weight,
        hidden,
        mixed,
        qkv,
        exponents,
        inverses,
        wide,
        lambda i: None,
    )
    for copy in copies:
        copy.wait()


def leading_slots(parent_index, child_slot, first_parent):
    slot = lax.broadcasted_iota(jnp.int32, (SPILL, LANES), 0)
    before = parent_index[:, :LANES] < first_parent[0]
    return indicator(before & (child_slot[:, :LANES] == slot))


def slot_numbers(parent_index, child_slot, first_parent, owned):
    parent = lax.broadcasted_iota(jnp.int32, (owned, parent_index.shape[1]), 0)
    mine = parent_index - first_parent[0] == parent
    return jnp.where(mine, child_slot, -1)


def pool(
    first_parent,
    first_hidden,
    rest_hidden,
    parent_index,
    child_slot,
    own_out,
    other_out,
    out_grad,
    children,
    upward,
    hidden,
):
    owned = out_grad.shape[0]
    hidden[:, :LANES] = first_hidden[...]
    hidden[:, LANES:] = rest_hidden[...]
    slot_of = slot_numbers(parent_index[...], child_slot[...], first_parent, owned)
    for slot in range(0, SLOTS, 2):
        both = jnp.concatenate([indicator(slot_of == slot), indicator(slot_of == slot + 1)], 0)
        pair = bround(nt(hidden[...], both))
        children[slot] = pair[:, :owned]
        children[slot + 1] = pair[:, owned:]
    for half, out_weight in enumerate((own_out, other_out)):
        upward[half] = bround(nt(out_weight[...], out_grad[...]))


def coarse_both(
    children,
    upward,
    spill,
    pool_weight,
    own_qkv,
    other_qkv,
    own_out,
    other_out,
    out_grad,
    coarse_rows,
    spill_grad,
    grad_parents,
    pooled,
    grad_pooled,
    coarse_input,
    mixed,
    grads,
    wide_query,
    wide_grad,
):
    owned, width = out_grad.shape
    channels = children.shape[1]
    part = own_out.shape[0]
    heads = part // HD
    spill_slot = lax.broadcasted_iota(jnp.int32, (SPILL, owned), 0)
    last = lax.broadcasted_iota(jnp.int32, (SPILL, owned), 1) == owned - 1
    total = jnp.zeros((owned, width), jnp.float32)
    for slot in range(SLOTS):
        edge = tn(spill[...], indicator(last & (spill_slot == slot)))
        chosen = children[slot] + bround(edge)
        pooled[slot] = chosen
        total += tn(chosen, pool_weight[slot * channels : (slot + 1) * channels])
    parents = bround(total).astype(jnp.float32)
    normed, inverse = layer_norm(parents, 1)
    coarse_input[...] = bround(normed)
    upstream = out_grad[...]
    classes = window_rows(coarse_window)
    grad_normed = jnp.zeros((owned, width), jnp.float32)
    summed = jnp.zeros((owned, width), jnp.float32)
    for wide in (wide_query, wide_grad):
        wide[...] = jnp.zeros(wide.shape, wide.dtype)
    weights = ((own_qkv, own_out), (other_qkv, other_out))
    for half, (qkv_weight, out_weight) in enumerate(weights):
        qkv = bround(nt(qkv_weight[...], coarse_input[...]))
        wide_query[half, part:] = mask_rows(coarse_window, heads)
        spread(wide_query.at[half], scaled(qkv[:part]), heads)
        keys = jnp.concatenate([qkv[part : 2 * part], classes], 0)
        scores = tn(keys, wide_query[half])
        parts = []
        for head in range(heads):
            at = slice(head * HD, (head + 1) * HD)
            exponent, scale = softmax_parts(scores[:, head * LANES : (head + 1) * LANES])
            parts.append((exponent, scale))
            value = qkv[2 * part + head * HD : 2 * part + (head + 1) * HD]
            mixed[half, at] = bround(nn(value, exponent) * scale)
            weighted = scaled(upward[half, at]).astype(jnp.float32) * scale
            wide_grad[half, at, head * LANES : (head + 1) * LANES] = bround(weighted)
        grad_probs = tn(qkv[2 * part :], wide_grad[half])
        for head in range(heads):
            at = [slice(i * part + head * HD, i * part + (head + 1) * HD) for i in range(3)]
            back = attend_back(
                qkv[at[0]],
                qkv[at[1]],
                upward[half, at[0]],
                *parts[head],
                grad_probs[:, head * LANES : (head + 1) * LANES],
            )
            for which in range(3):
                grads[half, at[which]] = back[which]
        summed += tn(mixed[half], out_weight[...])
        grad_normed += tn(grads[half], qkv_weight[...])
    coarse_rows[...] = bround(parents + summed)
    upstream_total = bround(
        upstream.astype(jnp.float32) + layer_norm_back(normed, inverse, grad_normed, 1)
    )
    grad_parents[...] = upstream_total
    edge_total = jnp.zeros((SPILL, channels), jnp.float32)
    for slot in range(SLOTS):
        weight = pool_weight[slot * channels : (slot + 1) * channels]
        grad_slot = bround(nt(weight, upstream_total))
        grad_pooled[slot] = grad_slot
        edge_total += nt(indicator(last & (spill_slot == slot)), grad_slot)
    spill_grad[...] = bround(edge_total)


def coarse_weights(
    core_ref,
    grad_parents,
    pooled,
    coarse_input,
    mixed,
    grads,
    out_grad,
    keep,
    give,
):
    core = core_ref[0]
    width = out_grad.shape[1]
    channels = pooled.shape[1]
    part = mixed.shape[1]
    panels = width // LANES

    def store(target, start, value):
        for panel in range(panels):
            at = start + panel * value.shape[0]
            target[at : at + value.shape[0]] = bround(
                value[:, panel * LANES : (panel + 1) * LANES]
            )

    for half, target in enumerate((keep, give)):
        store(target, 0, nn(grads[half], coarse_input[...]))
        store(target, 3 * part * panels, nn(mixed[half], out_grad[...]))
    base = 4 * part * panels
    for target, first in ((keep, core), (give, 1 - core)):
        for step in range(SLOTS // 2):
            grad_pool = nn(pooled[first * (SLOTS // 2) + step], grad_parents[...])
            store(target, base + step * panels * channels, grad_pool)


def fine_back(
    first_block,
    core_ref,
    first_parent,
    rows,
    grad_pooled,
    parent_index,
    child_slot,
    qkv_weight,
    out_weight,
    exponents,
    inverses,
    qkv,
    mixed,
    *rest,
):
    if first_block:
        row_grad, qkv_total, out_total, grads, wide = rest
    else:
        spill_grad, row_rest, qkv_rest, out_rest = rest[:4]
        row_grad, keep, give, grads, wide = rest[4:]
    channels, count = mixed.shape
    owned = grad_pooled.shape[2]
    heads = channels // HD
    span = slice(first_block * LANES, first_block * LANES + count)
    normed, inverse = layer_norm(rows[:, span].astype(jnp.float32), 0)
    slot_of = slot_numbers(parent_index[:, span], child_slot[:, span], first_parent, owned)
    upstream = jnp.zeros((channels, count), jnp.float32)
    for slot in range(SLOTS):
        upstream += nn(grad_pooled[slot], indicator(slot_of == slot))
    if not first_block:
        leading = leading_slots(parent_index, child_slot, first_parent)
        upstream += tn(spill_grad[...], leading)
    upstream = bround(upstream)
    upward = bround(nn(out_weight[...], upstream))
    wide[...] = jnp.zeros(wide.shape, wide.dtype)
    for block in range(count // LANES):
        lanes = slice(block * LANES, (block + 1) * LANES)
        grad_rows = wide.at[block % wide.shape[0]]
        scales = [
            inverses[block * heads + head : block * heads + head + 1] for head in range(heads)
        ]
        for head in range(heads):
            at = slice(head * HD, (head + 1) * HD)
            weighted = scaled(upward[at, lanes]).astype(jnp.float32) * scales[head]
            grad_rows[at, head * LANES : (head + 1) * LANES] = bround(weighted)
        grad_probs = tn(qkv[2 * channels :, lanes], grad_rows[...])
        for head in range(heads):
            at = [slice(i * channels + head * HD, i * channels + (head + 1) * HD) for i in range(3)]
            out = slice(head * LANES, (head + 1) * LANES)
            back = attend_back(
                qkv[at[0], lanes],
                qkv[at[1], lanes],
                upward[at[0], lanes],
                exponents[block, :, out],
                scales[head],
                grad_probs[:, out],
            )
            for which in range(3):
                grads[at[which], lanes] = back[which]
    grad_normed = nn(qkv_weight[...], grads[...])
    total = upstream.astype(jnp.float32) + layer_norm_back(normed, inverse, grad_normed, 0)
    grad_qkv = nt(bround(normed), grads[...])
    grad_out = nt(mixed[...], upstream)
    if first_block:
        row_grad[...] = bround(total)
        qkv_total[...] = grad_qkv
        out_total[...] = grad_out
        return
    row_grad[:, span] = bround(total)
    row_grad[:, count:] = row_rest[...]
    grad_qkv = bround(grad_qkv + qkv_rest[...])
    grad_out = bround(grad_out + out_rest[...])
    core = core_ref[0]
    whole = 3 * channels // LANES
    panels = [grad_qkv[:, i * LANES : (i + 1) * LANES] for i in range(whole)]
    panels.append(jnp.concatenate([grad_qkv[:, whole * LANES :], grad_out[:, LANES:]], 1))
    panels.append(grad_out[:, :LANES])
    half = len(panels) // 2
    for i in range(half):
        at = slice(i * channels, (i + 1) * channels)
        keep[at] = jnp.where(core == 0, panels[i], panels[half + i])
        give[at] = jnp.where(core == 0, panels[half + i], panels[i])


def fine_and_weights(core_ref, first_parent, *refs):
    fine_in, weight_in, refs = refs[:10], refs[10:16], refs[16:]
    fine_back(1, core_ref, first_parent, *fine_in, *refs[:3], *refs[5:])
    coarse_weights(core_ref, *weight_in, *refs[3:5])


def merge(keep, got, fine_keep, fine_got, total):
    first, second = keep.shape[0], fine_keep.shape[0]
    total[:first] = keep[...] + got[...]
    total[first : first + second] = fine_keep[...] + fine_got[...]
    pad = total.shape[0] - first - second
    total[first + second :] = jnp.zeros((pad, LANES), total.dtype)


def assemble(
    fine_scale,
    coarse_scale,
    core_ref,
    mine,
    other,
    grad_qkv,
    grad_out,
    grad_pool,
    grad_coarse_qkv,
    grad_coarse_out,
):
    core = core_ref[0]
    channels = grad_out.shape[0]
    part, width = grad_coarse_out.shape
    panels = width // LANES
    edge = channels % LANES

    def coarse(start, count):
        return mine[start : start + count].astype(jnp.float32) * coarse_scale

    first = 3 * part * panels
    for panel in range(panels):
        lanes = slice(panel * LANES, (panel + 1) * LANES)
        for which in range(3):
            grad_coarse_qkv[which, :, lanes] = coarse((3 * panel + which) * part, part)
        grad_coarse_out[:, lanes] = coarse(first + panel * part, part)
    first += panels * part
    half_rows = SLOTS // 2 * channels
    for source, start, half in ((mine, first, core), (other, 0, 1 - core)):
        for step in range(SLOTS // 2):
            row = pl.multiple_of(half * half_rows + step * channels, 8)
            for panel in range(panels):
                at = start + (step * panels + panel) * channels
                grad_pool[pl.ds(row, channels), panel * LANES : (panel + 1) * LANES] = (
                    source[at : at + channels].astype(jnp.float32) * coarse_scale
                )
    skip = half_rows * panels
    fine = []
    for half in range(2):
        for i in range(3):
            at = skip + i * channels
            near = mine[first + at : first + at + channels].astype(jnp.float32)
            far = other[at : at + channels].astype(jnp.float32)
            fine.append(jnp.where(core == half, near, far) * fine_scale)
    for i in range(4):
        grad_qkv[:, i * LANES : (i + 1) * LANES] = fine[i]
    grad_qkv[:, 4 * LANES :] = fine[4][:, :edge]
    grad_out[:, :LANES] = fine[5]
    grad_out[:, LANES:] = fine[4][:, edge:]


def call(kernel, outs, scratch, *operands, scalars=1, micros=1, hbm=0, copies=0):
    spaces = [pltpu.SMEM] * scalars + [pltpu.HBM] * hbm
    spaces += [pltpu.VMEM] * (len(operands) - len(spaces))
    return pl.pallas_call(
        kernel,
        out_shape=[jax.ShapeDtypeStruct(shape, dtype) for shape, dtype in outs],
        in_specs=[pl.BlockSpec(memory_space=space) for space in spaces],
        out_specs=[pl.BlockSpec(memory_space=pltpu.VMEM)] * len(outs),
        scratch_shapes=[pltpu.VMEM(shape, jnp.bfloat16) for shape in scratch]
        + ([pltpu.SemaphoreType.DMA((copies,))] if copies else []),
        compiler_params=pltpu.CompilerParams(vmem_limit_bytes=VMEM_BYTES),
        cost_estimate=pl.CostEstimate(
            flops=int(micros * 10**9), bytes_accessed=int(micros * 10**6), transcendentals=0
        ),
    )(*operands)


def float_sum(stacked):
    return bround(jnp.sum(stacked.astype(jnp.float32), 0))


def sum_over_chips(parts):
    plane = lax.all_to_all(parts, NEAR, 0, 0, tiled=True)
    slab = float_sum(plane)
    copies = jnp.broadcast_to(slab, (lax.axis_size("zh"),) + slab.shape)
    slab = float_sum(lax.all_to_all(copies, "zh", 0, 0, tiled=True))
    copies = jnp.broadcast_to(slab, parts.shape)
    return lax.all_to_all(copies, NEAR, 0, 0, tiled=True)


def on_device(
    fine_rows,
    qkv_weight,
    out_weight,
    pool_weight,
    coarse_qkv_weight,
    coarse_out_weight,
    parent_index,
    child_slot,
    out_grad,
):
    bf16, f32 = jnp.bfloat16, jnp.float32
    devices = 1
    for name in AXES:
        devices *= lax.axis_size(name)
    row_count, channels = fine_rows.shape
    owned, width = out_grad.shape
    part = coarse_out_weight.shape[0]
    blocks = row_count // LANES
    heads = channels // HD
    coarse_heads = part // HD
    coarse_count = 4 * part * width // LANES
    pool_count = SLOTS // 2 * channels * width // LANES
    fine_count = 2 * channels * channels // LANES
    core = lax.axis_index("sub").astype(jnp.int32).reshape(1)
    first_parent = (lax.axis_index(AXES) * owned).astype(jnp.int32).reshape(1)
    rows = fine_rows.T
    parent_row = parent_index.reshape(1, row_count)
    slot_row = child_slot.reshape(1, row_count)
    own_qkv = coarse_qkv_weight.transpose(0, 2, 1).reshape(3 * part, width)
    other_qkv = swap_cores(own_qkv)
    other_out = swap_cores(coarse_out_weight)
    wide_rows = heads * LANES

    def in_hbm(*arrays):
        return [pltpu.with_memory_space_constraint(array, pltpu.HBM) for array in arrays]

    def like(*arrays):
        return [(array.shape, array.dtype) for array in arrays]

    def block_outs(count):
        return [
            ((channels, count * LANES), bf16),
            ((channels, count * LANES), bf16),
            ((3 * channels, count * LANES), bf16),
            ((count, LANES, wide_rows), bf16),
            ((count * heads, LANES), f32),
        ]

    sources = (rows, qkv_weight, out_weight, parent_row, slot_row)
    first = call(
        fine_first,
        like(*sources) + block_outs(1) + [((SPILL, channels), bf16)],
        [(1, channels + SPILL, wide_rows)],
        first_parent,
        *in_hbm(*sources),
        hbm=5,
        copies=5,
        micros=3,
    )
    rows, fine_qkv, fine_out, parent_row, slot_row = first[:5]
    hidden_first, *saved_first, spill = first[5:]
    spill_in = passed_along(spill, -1)
    sources = (pool_weight, own_qkv, coarse_out_weight, out_grad)
    second = call(
        fine_rest,
        like(*sources) + block_outs(blocks - 1),
        [(2, channels + SPILL, wide_rows)],
        *in_hbm(*sources),
        rows,
        fine_qkv,
        fine_out,
        scalars=0,
        hbm=4,
        copies=4,
        micros=2,
    )
    pool_weight, own_qkv, own_out, out_grad = second[:4]
    hidden_rest, *saved_rest = second[4:]
    children, upward = call(
        pool,
        [((SLOTS, channels, owned), bf16), ((2, part, owned), bf16)],
        [(channels, row_count)],
        first_parent,
        hidden_first,
        hidden_rest,
        parent_row,
        slot_row,
        own_out,
        other_out,
        out_grad,
        micros=2,
    )
    coarse_rows, spill_grad, grad_parents, pooled, grad_pooled, coarse_input, mixed, grads = call(
        coarse_both,
        [
            ((owned, width), bf16),
            ((SPILL, channels), bf16),
            ((owned, width), bf16),
            ((SLOTS, channels, owned), bf16),
            ((SLOTS, channels, owned), bf16),
            ((owned, width), bf16),
            ((2, part, owned), bf16),
            ((2, 3 * part, owned), bf16),
        ],
        [
            (2, part + SPILL, coarse_heads * LANES),
            (2, part, coarse_heads * LANES),
        ],
        children,
        upward,
        spill_in,
        pool_weight,
        own_qkv,
        other_qkv,
        own_out,
        other_out,
        out_grad,
        scalars=0,
        micros=8,
    )
    spill_back = passed_along(spill_grad, 1)
    shared = (core, first_parent, rows, grad_pooled, parent_row, slot_row, fine_qkv, fine_out)
    rest_count = row_count - LANES
    row_rest, qkv_rest, out_rest, keep, give = call(
        fine_and_weights,
        [
            ((channels, rest_count), bf16),
            ((channels, 3 * channels), f32),
            ((channels, channels), f32),
            ((coarse_count + pool_count, LANES), bf16),
            ((coarse_count + pool_count, LANES), bf16),
        ],
        [(3 * channels, rest_count), (2, channels, wide_rows)],
        *shared,
        *saved_rest[2:],
        saved_rest[1],
        saved_rest[0],
        grad_parents,
        pooled,
        coarse_input,
        mixed,
        grads,
        out_grad,
        scalars=2,
        micros=5,
    )
    spill_back, give = lax.optimization_barrier((spill_back, give))
    got = swap_cores(give)
    row_grad, fine_keep, fine_give = call(
        functools.partial(fine_back, 0),
        [
            ((channels, row_count), bf16),
            ((fine_count, LANES), bf16),
            ((fine_count, LANES), bf16),
        ],
        [(3 * channels, LANES), (1, channels, wide_rows)],
        *shared,
        *saved_first[2:],
        saved_first[1],
        saved_first[0],
        spill_back,
        row_rest,
        qkv_rest,
        out_rest,
        scalars=2,
        micros=2,
    )
    fine_got = swap_cores(fine_give)
    plane = lax.axis_size("zl") * lax.axis_size("y") * lax.axis_size("x")
    count = coarse_count + pool_count + fine_count
    unit = plane * 8
    padded = -(-count // unit) * unit
    (merged,) = call(
        merge, [((padded, LANES), bf16)], [], keep, got, fine_keep, fine_got, scalars=0, micros=1
    )
    total = sum_over_chips(merged.reshape(plane, padded // plane, LANES)).reshape(padded, LANES)
    other = swap_cores(total[coarse_count:count])
    grad_qkv, grad_out, grad_pool, grad_coarse_qkv, grad_coarse_out = call(
        functools.partial(
            assemble, (row_count * devices) ** (-0.5), (owned * devices) ** (-0.5)
        ),
        [
            ((channels, 3 * channels), f32),
            ((channels, channels), f32),
            ((SLOTS * channels, width), f32),
            ((3, part, width), f32),
            ((part, width), f32),
        ],
        [],
        core,
        total,
        other,
        micros=2,
    )
    return (
        coarse_rows,
        row_grad.T,
        grad_qkv,
        grad_out,
        grad_pool,
        grad_coarse_qkv.transpose(0, 2, 1),
        grad_coarse_out,
    )


def solution(mesh):
    torus = Mesh(mesh.devices.reshape(-1, 2, 4, 4, mesh.shape["sub"]), AXES)
    in_specs = (
        P(AXES, None),
        P(),
        P(),
        P(),
        P(None, None, "sub"),
        P("sub", None),
        P(AXES),
        P(AXES),
        P(AXES, None),
    )
    out_specs = (
        P(AXES, None),
        P(AXES, None),
        P(),
        P(),
        P(),
        P(None, None, "sub"),
        P("sub", None),
    )
    return jax.shard_map(
        on_device, mesh=torus, in_specs=in_specs, out_specs=out_specs, check_vma=False
    )
```

```python
import functools

import jax
import jax.numpy as jnp
from jax import lax
from jax.experimental import pallas as pl
from jax.experimental.pallas import tpu as pltpu
from jax.sharding import Mesh, PartitionSpec as P

HD = 16
WINDOW_OCTANTS = 32
DILATION_STRIDE = 4
SLOTS = 8
LANES = 128
SPILL = 16
EPSILON = 1e-05
NEAR = ("zl", "y", "x")
AXES = ("zh",) + NEAR + ("sub",)
VMEM_BYTES = 20 * 1024 * 1024
FAR = -1e30


def passed_along(shard, by):
    count = 1
    for name in AXES:
        count *= lax.axis_size(name)
    pairs = [(i, i + by) for i in range(count) if 0 <= i + by < count]
    return lax.ppermute(shard, AXES, pairs)


def swap_cores(shard):
    return lax.ppermute(shard, "sub", [(0, 1), (1, 0)])


def bround(value):
    return value.astype(jnp.bfloat16)


def product(left, right, left_dim, right_dim):
    return lax.dot_general(
        left, right, (((left_dim,), (right_dim,)), ((), ())), preferred_element_type=jnp.float32
    )


def nn(left, right):
    return product(left, right, 1, 0)


def nt(left, right):
    return product(left, right, 1, 1)


def tn(left, right):
    return product(left, right, 0, 0)


def indicator(condition):
    return bround(jnp.where(condition, 1.0, 0.0))


def layer_norm(value, axis):
    center = value - jnp.mean(value, axis, keepdims=True)
    inverse = lax.rsqrt(jnp.mean(center * center, axis, keepdims=True) + EPSILON)
    return (center * inverse, inverse)


def layer_norm_back(normed, inverse, upstream, axis):
    return inverse * (
        upstream
        - jnp.mean(upstream, axis, keepdims=True)
        - normed * jnp.mean(upstream * normed, axis, keepdims=True)
    )


def window_rows(window_of):
    row = lax.broadcasted_iota(jnp.int32, (SPILL, LANES), 0)
    lane = lax.broadcasted_iota(jnp.int32, (SPILL, LANES), 1)
    return indicator(window_of(lane) == row)


def mask_rows(window_of, heads):
    row = lax.broadcasted_iota(jnp.int32, (SPILL, LANES), 0)
    lane = lax.broadcasted_iota(jnp.int32, (SPILL, LANES), 1)
    other = (window_of(lane) != row) & (row < LANES // WINDOW_OCTANTS)
    return jnp.concatenate([bround(jnp.where(other, FAR, 0.0))] * heads, 1)


def fine_window(at):
    return at % DILATION_STRIDE


def coarse_window(at):
    return at // WINDOW_OCTANTS


def spread(wide, rows, heads):
    for head in range(heads):
        at = slice(head * HD, (head + 1) * HD)
        wide[at, head * LANES : (head + 1) * LANES] = rows[at]


def softmax_parts(score):
    exponent = jnp.exp(score - jnp.max(score, 0, keepdims=True))
    return (bround(exponent), 1.0 / jnp.sum(exponent, 0, keepdims=True))


def attend_back(query, key, upstream, exponent, inverse, grad_prob):
    weighted = exponent.astype(jnp.float32)
    mean = inverse * jnp.sum(weighted * grad_prob, 0, keepdims=True)
    grad_score = bround(weighted * (grad_prob - mean))
    grad_value = nt(bround(upstream.astype(jnp.float32) * inverse), exponent)
    grad_query = nn(key, grad_score)
    grad_key = nt(query, grad_score)
    return (bround(grad_query), bround(grad_key), bround(grad_value))


def scaled(value):
    return value * jnp.bfloat16(HD**-0.5)


def fine_attention(qkv, wide, classes, heads, mixed, store):
    channels = heads * HD
    spread(wide, scaled(qkv[:channels]), heads)
    keys = jnp.concatenate([qkv[channels : 2 * channels], classes], 0)
    scores = tn(keys, wide[...])
    for head in range(heads):
        exponent, inverse = softmax_parts(scores[:, head * LANES : (head + 1) * LANES])
        value = qkv[2 * channels + head * HD : 2 * channels + (head + 1) * HD]
        mixed[head * HD : (head + 1) * HD] = bround(nn(value, exponent) * inverse)
        if store is not None:
            store(head, exponent, inverse)


def clear_wide(wide, heads, window_of):
    wide[...] = jnp.zeros(wide.shape, wide.dtype)
    for slot in range(wide.shape[0]):
        wide[slot, heads * HD :] = mask_rows(window_of, heads)


def fetch(pairs, arrived):
    copies = [
        pltpu.make_async_copy(source, target, arrived.at[i])
        for i, (source, target) in enumerate(pairs)
    ]
    for copy in copies:
        copy.start()
    return copies


def fine_blocks(
    first, rows, qkv_weight, out_weight, hidden, mixed, qkv, exponents, inverses, wide, wait
):
    channels, count = hidden.shape
    heads = channels // HD
    clear_wide(wide, heads, fine_window)
    classes = window_rows(fine_window)
    wait(0)
    wait(1)
    rows_float = rows[:, first * LANES : first * LANES + count].astype(jnp.float32)
    normed, _ = layer_norm(rows_float, 0)
    qkv[...] = bround(tn(qkv_weight[...], bround(normed)))
    for block in range(count // LANES):
        lanes = slice(block * LANES, (block + 1) * LANES)

        def store(head, exponent, inverse):
            exponents[block, :, head * LANES : (head + 1) * LANES] = exponent
            at = block * heads + head
            inverses[at : at + 1] = inverse

        fine_attention(
            qkv[:, lanes],
            wide.at[block % wide.shape[0]],
            classes,
            heads,
            mixed.at[:, lanes],
            store,
        )
    wait(2)
    hidden[...] = bround(rows_float + tn(out_weight[...], mixed[...]))


def fine_first(first_parent, *refs):
    sources, targets = refs[:5], refs[5:10]
    hidden, mixed, qkv, exponents, inverses, spill, wide, arrived = refs[10:]
    rows, qkv_weight, out_weight, parent_index, child_slot = targets
    copies = fetch(tuple(zip(sources, targets)), arrived)
    fine_blocks(
        0,
        rows,
        qkv_weight,
        out_weight,
        hidden,
        mixed,
        qkv,
        exponents,
        inverses,
        wide,
        lambda i: copies[i].wait(),
    )
    copies[3].wait()
    copies[4].wait()
    spill[...] = bround(nt(leading_slots(parent_index, child_slot, first_parent), hidden[...]))


def fine_rest(*refs):
    sources, (rows, qkv_weight, out_weight) = refs[:4], refs[4:7]
    targets = refs[7:11]
    hidden, mixed, qkv, exponents, inverses, wide, arrived = refs[11:]
    copies = fetch(tuple(zip(sources, targets)), arrived)
    fine_blocks(
        1,
        rows,
        qkv_weight,
        out_weight,
        hidden,
        mixed,
        qkv,
        exponents,
        inverses,
        wide,
        lambda i: None,
    )
    for copy in copies:
        copy.wait()


def leading_slots(parent_index, child_slot, first_parent):
    slot = lax.broadcasted_iota(jnp.int32, (SPILL, LANES), 0)
    before = parent_index[:, :LANES] < first_parent[0]
    return indicator(before & (child_slot[:, :LANES] == slot))


def slot_numbers(parent_index, child_slot, first_parent, owned):
    parent = lax.broadcasted_iota(jnp.int32, (owned, parent_index.shape[1]), 0)
    mine = parent_index - first_parent[0] == parent
    return jnp.where(mine, child_slot, -1)


def pool(
    first_parent,
    first_hidden,
    rest_hidden,
    parent_index,
    child_slot,
    own_out,
    other_out,
    out_grad,
    pool_weight,
    children,
    upward,
    partial,
    hidden,
):
    owned = out_grad.shape[0]
    hidden[:, :LANES] = first_hidden[...]
    hidden[:, LANES:] = rest_hidden[...]
    slot_of = slot_numbers(parent_index[...], child_slot[...], first_parent, owned)
    for slot in range(0, SLOTS, 2):
        both = jnp.concatenate([indicator(slot_of == slot), indicator(slot_of == slot + 1)], 0)
        pair = bround(nt(hidden[...], both))
        children[slot] = pair[:, :owned]
        children[slot + 1] = pair[:, owned:]
    channels = hidden.shape[0]
    total = jnp.zeros(partial.shape, jnp.float32)
    for slot in range(SLOTS):
        total += tn(children[slot], pool_weight[slot * channels : (slot + 1) * channels])
    partial[...] = total
    for half, out_weight in enumerate((own_out, other_out)):
        upward[half] = bround(nt(out_weight[...], out_grad[...]))


def coarse_both(
    partial,
    upward,
    spill,
    pool_weight,
    own_qkv,
    other_qkv,
    own_out,
    other_out,
    out_grad,
    coarse_rows,
    spill_grad,
    grad_parents,
    grad_pooled,
    coarse_input,
    mixed,
    grads,
    wide_query,
    wide_grad,
):
    owned, width = out_grad.shape
    channels = spill.shape[1]
    part = own_out.shape[0]
    heads = part // HD
    halves = range(2)
    qkv_weights, out_weights = (own_qkv, other_qkv), (own_out, other_out)
    for wide in (wide_query, wide_grad):
        wide[...] = jnp.zeros(wide.shape, wide.dtype)
    for half in halves:
        wide_query[half, part:] = mask_rows(coarse_window, heads)
    spill_row = lax.broadcasted_iota(jnp.int32, (SPILL, channels), 0)
    late = jnp.zeros((SPILL, width), jnp.float32)
    for slot in range(SLOTS):
        chosen = jnp.where(spill_row == slot, spill[...], jnp.zeros_like(spill))
        late += nn(chosen, pool_weight[slot * channels : (slot + 1) * channels])
    late = jnp.sum(late, 0, keepdims=True)
    at_last = lax.broadcasted_iota(jnp.int32, (owned, width), 0) == owned - 1
    parents = bround(partial[...] + jnp.where(at_last, late, 0.0)).astype(jnp.float32)
    normed, inverse = layer_norm(parents, 1)
    coarse_input[...] = bround(normed)
    upstream = out_grad[...]
    classes = window_rows(coarse_window)
    qkvs = [bround(nt(qkv_weights[half][...], coarse_input[...])) for half in halves]
    for half in halves:
        spread(wide_query.at[half], scaled(qkvs[half][:part]), heads)
    scores = [
        tn(jnp.concatenate([qkvs[half][part : 2 * part], classes], 0), wide_query[half])
        for half in halves
    ]
    parts = {}
    for half in halves:
        for head in range(heads):
            at = slice(head * HD, (head + 1) * HD)
            lanes = slice(head * LANES, (head + 1) * LANES)
            exponent, scale = softmax_parts(scores[half][:, lanes])
            parts[half, head] = (exponent, scale)
            value = qkvs[half][2 * part + head * HD : 2 * part + (head + 1) * HD]
            mixed[half, at] = bround(nn(value, exponent) * scale)
            weighted = scaled(upward[half, at]).astype(jnp.float32) * scale
            wide_grad[half, at, lanes] = bround(weighted)
    grad_probs = [tn(qkvs[half][2 * part :], wide_grad[half]) for half in halves]
    for half in halves:
        for head in range(heads):
            at = [slice(i * part + head * HD, i * part + (head + 1) * HD) for i in range(3)]
            back = attend_back(
                qkvs[half][at[0]],
                qkvs[half][at[1]],
                upward[half, at[0]],
                *parts[half, head],
                grad_probs[half][:, head * LANES : (head + 1) * LANES],
            )
            for which in range(3):
                grads[half, at[which]] = back[which]
    grad_normed = sum(tn(grads[half], qkv_weights[half][...]) for half in halves)
    upstream_total = bround(
        upstream.astype(jnp.float32) + layer_norm_back(normed, inverse, grad_normed, 1)
    )
    grad_parents[...] = upstream_total
    grad_all = bround(nt(pool_weight[...], upstream_total))
    last = lax.broadcasted_iota(jnp.int32, (SPILL, owned), 1) == owned - 1
    spill_slot = lax.broadcasted_iota(jnp.int32, (SPILL, owned), 0)
    edge_total = jnp.zeros((SPILL, channels), jnp.float32)
    for slot in range(SLOTS):
        grad_slot = grad_all[slot * channels : (slot + 1) * channels]
        grad_pooled[slot // 2, :, slot % 2 * owned : (slot % 2 + 1) * owned] = grad_slot
        edge_total += nt(indicator(last & (spill_slot == slot)), grad_slot)
    spill_grad[...] = bround(edge_total)
    summed = sum(tn(mixed[half], out_weights[half][...]) for half in halves)
    coarse_rows[...] = bround(parents + summed)


def coarse_weights(
    core_ref,
    grad_parents,
    children,
    spill,
    coarse_input,
    mixed,
    grads,
    out_grad,
    keep,
    give,
    pooled,
):
    core = core_ref[0]
    width = out_grad.shape[1]
    owned, channels = out_grad.shape[0], pooled.shape[1]
    part = mixed.shape[1]
    last = lax.broadcasted_iota(jnp.int32, (SPILL, owned), 1) == owned - 1
    spill_slot = lax.broadcasted_iota(jnp.int32, (SPILL, owned), 0)
    for slot in range(0, SLOTS, 2):
        edges = [indicator(last & (spill_slot == at)) for at in (slot, slot + 1)]
        edge = bround(tn(spill[...], jnp.concatenate(edges, 1)))
        pooled[slot] = children[slot] + edge[:, :owned]
        pooled[slot + 1] = children[slot + 1] + edge[:, owned:]
    panels = width // LANES

    def store(target, start, value):
        for panel in range(panels):
            at = start + panel * value.shape[0]
            target[at : at + value.shape[0]] = bround(
                value[:, panel * LANES : (panel + 1) * LANES]
            )

    for half, target in enumerate((keep, give)):
        store(target, 0, nn(grads[half], coarse_input[...]))
        store(target, 3 * part * panels, nn(mixed[half], out_grad[...]))
    base = 4 * part * panels
    for target, first in ((keep, core), (give, 1 - core)):
        for step in range(SLOTS // 2):
            grad_pool = nn(pooled[first * (SLOTS // 2) + step], grad_parents[...])
            store(target, base + step * panels * channels, grad_pool)


def fine_back(
    first_block,
    core_ref,
    first_parent,
    rows,
    grad_pooled,
    parent_index,
    child_slot,
    qkv_weight,
    out_weight,
    exponents,
    inverses,
    qkv,
    mixed,
    *rest,
):
    if first_block:
        row_grad, qkv_total, out_total, grads, wide = rest
    else:
        spill_grad, row_rest, qkv_rest, out_rest = rest[:4]
        row_grad, keep, give, grads, wide = rest[4:]
    channels, count = mixed.shape
    owned = grad_pooled.shape[2] // 2
    heads = channels // HD
    span = slice(first_block * LANES, first_block * LANES + count)
    normed, inverse = layer_norm(rows[:, span].astype(jnp.float32), 0)
    slot_of = slot_numbers(parent_index[:, span], child_slot[:, span], first_parent, owned)
    upstream = jnp.zeros((channels, count), jnp.float32)
    for slot in range(0, SLOTS, 2):
        both = jnp.concatenate([indicator(slot_of == slot), indicator(slot_of == slot + 1)], 0)
        upstream += nn(grad_pooled[slot // 2], both)
    if not first_block:
        leading = leading_slots(parent_index, child_slot, first_parent)
        upstream += tn(spill_grad[...], leading)
    upstream = bround(upstream)
    upward = bround(nn(out_weight[...], upstream))
    wide[...] = jnp.zeros(wide.shape, wide.dtype)
    for block in range(count // LANES):
        lanes = slice(block * LANES, (block + 1) * LANES)
        grad_rows = wide.at[block % wide.shape[0]]
        scales = [
            inverses[block * heads + head : block * heads + head + 1] for head in range(heads)
        ]
        for head in range(heads):
            at = slice(head * HD, (head + 1) * HD)
            weighted = scaled(upward[at, lanes]).astype(jnp.float32) * scales[head]
            grad_rows[at, head * LANES : (head + 1) * LANES] = bround(weighted)
        grad_probs = tn(qkv[2 * channels :, lanes], grad_rows[...])
        for head in range(heads):
            at = [slice(i * channels + head * HD, i * channels + (head + 1) * HD) for i in range(3)]
            out = slice(head * LANES, (head + 1) * LANES)
            back = attend_back(
                qkv[at[0], lanes],
                qkv[at[1], lanes],
                upward[at[0], lanes],
                exponents[block, :, out],
                scales[head],
                grad_probs[:, out],
            )
            for which in range(3):
                grads[at[which], lanes] = back[which]
    grad_normed = nn(qkv_weight[...], grads[...])
    total = upstream.astype(jnp.float32) + layer_norm_back(normed, inverse, grad_normed, 0)
    grad_qkv = nt(bround(normed), grads[...])
    grad_out = nt(mixed[...], upstream)
    if first_block:
        row_grad[...] = bround(total)
        qkv_total[...] = grad_qkv
        out_total[...] = grad_out
        return
    row_grad[:, span] = bround(total)
    row_grad[:, count:] = row_rest[...]
    grad_qkv = bround(grad_qkv + qkv_rest[...])
    grad_out = bround(grad_out + out_rest[...])
    core = core_ref[0]
    whole = 3 * channels // LANES
    panels = [grad_qkv[:, i * LANES : (i + 1) * LANES] for i in range(whole)]
    panels.append(jnp.concatenate([grad_qkv[:, whole * LANES :], grad_out[:, LANES:]], 1))
    panels.append(grad_out[:, :LANES])
    half = len(panels) // 2
    for i in range(half):
        at = slice(i * channels, (i + 1) * channels)
        keep[at] = jnp.where(core == 0, panels[i], panels[half + i])
        give[at] = jnp.where(core == 0, panels[half + i], panels[i])


def fine_and_weights(core_ref, first_parent, *refs):
    fine_in, weight_in, refs = refs[:10], refs[10:17], refs[17:]
    fine_back(1, core_ref, first_parent, *fine_in, *refs[:3], *refs[5:7])
    coarse_weights(core_ref, *weight_in, *refs[3:5], *refs[7:])


def merge(keep, got, fine_keep, fine_got, total):
    first, second = keep.shape[0], fine_keep.shape[0]
    total[:first] = keep[...] + got[...]
    total[first : first + second] = fine_keep[...] + fine_got[...]
    pad = total.shape[0] - first - second
    total[first + second :] = jnp.zeros((pad, LANES), total.dtype)


def unpack_pool(source, start, target, scale):
    panels = target.shape[1] // LANES
    channels = target.shape[0] * 2 // SLOTS
    for step in range(SLOTS // 2):
        for panel in range(panels):
            at = start + (step * panels + panel) * channels
            rows = slice(step * channels, (step + 1) * channels)
            target[rows, panel * LANES : (panel + 1) * LANES] = (
                source[at : at + channels].astype(jnp.float32) * scale
            )


def place_half(half, staged, target, arrived):
    rows = staged.shape[0]
    start = pl.multiple_of(half * rows, 8)
    return pltpu.make_async_copy(staged, target.at[pl.ds(start, rows)], arrived.at[0])


def assemble_own(
    scale, core_ref, mine, grad_coarse_qkv, grad_coarse_out, grad_pool, staged, arrived
):
    part, width = grad_coarse_out.shape
    panels = width // LANES
    unpack_pool(mine, 4 * part * panels, staged, scale)
    copy = place_half(core_ref[0], staged, grad_pool, arrived)
    copy.start()

    def coarse(start):
        return mine[start : start + part].astype(jnp.float32) * scale

    first = 3 * part * panels
    for panel in range(panels):
        lanes = slice(panel * LANES, (panel + 1) * LANES)
        for which in range(3):
            grad_coarse_qkv[which, :, lanes] = coarse((3 * panel + which) * part)
        grad_coarse_out[:, lanes] = coarse(first + panel * part)
    copy.wait()


def assemble_other(
    fine_scale,
    coarse_scale,
    base,
    core_ref,
    pool_in,
    mine,
    other,
    grad_pool,
    grad_qkv,
    grad_out,
    staged,
    arrived,
):
    core = core_ref[0]
    channels = grad_out.shape[0]
    edge = channels % LANES
    unpack_pool(other, 0, staged, coarse_scale)
    copy = place_half(1 - core, staged, grad_pool, arrived)
    copy.start()
    skip = staged.shape[0] * staged.shape[1] // LANES
    fine = []
    for half in range(2):
        for i in range(3):
            at = skip + i * channels
            near = mine[base + at : base + at + channels].astype(jnp.float32)
            far = other[at : at + channels].astype(jnp.float32)
            fine.append(jnp.where(core == half, near, far) * fine_scale)
    for i in range(4):
        grad_qkv[:, i * LANES : (i + 1) * LANES] = fine[i]
    grad_qkv[:, 4 * LANES :] = fine[4][:, :edge]
    grad_out[:, :LANES] = fine[5]
    grad_out[:, LANES:] = fine[4][:, edge:]
    copy.wait()


def call(
    kernel,
    outs,
    scratch,
    *operands,
    scalars=1,
    micros=1,
    hbm=0,
    copies=0,
    staged=(),
    in_place=None,
):
    spaces = [pltpu.SMEM] * scalars + [pltpu.HBM] * hbm
    spaces += [pltpu.VMEM] * (len(operands) - len(spaces))
    out_spaces = [pltpu.VMEM] * len(outs)
    if in_place is not None:
        out_spaces[in_place] = pltpu.HBM
    return pl.pallas_call(
        kernel,
        out_shape=[jax.ShapeDtypeStruct(shape, dtype) for shape, dtype in outs],
        in_specs=[pl.BlockSpec(memory_space=space) for space in spaces],
        out_specs=[pl.BlockSpec(memory_space=space) for space in out_spaces],
        input_output_aliases={scalars: in_place} if in_place is not None and hbm else {},
        scratch_shapes=[pltpu.VMEM(shape, jnp.bfloat16) for shape in scratch]
        + [pltpu.VMEM(shape, jnp.float32) for shape in staged]
        + ([pltpu.SemaphoreType.DMA((copies,))] if copies else []),
        compiler_params=pltpu.CompilerParams(vmem_limit_bytes=VMEM_BYTES),
        cost_estimate=pl.CostEstimate(
            flops=int(micros * 10**9), bytes_accessed=int(micros * 10**6), transcendentals=0
        ),
    )(*operands)


def float_sum(stacked):
    return bround(jnp.sum(stacked.astype(jnp.float32), 0))


def sum_over_chips(parts):
    plane = lax.all_to_all(parts, NEAR, 0, 0, tiled=True)
    slab = float_sum(plane)
    copies = jnp.broadcast_to(slab, (lax.axis_size("zh"),) + slab.shape)
    slab = float_sum(lax.all_to_all(copies, "zh", 0, 0, tiled=True))
    copies = jnp.broadcast_to(slab, parts.shape)
    return lax.all_to_all(copies, NEAR, 0, 0, tiled=True)


def on_device(
    fine_rows,
    qkv_weight,
    out_weight,
    pool_weight,
    coarse_qkv_weight,
    coarse_out_weight,
    parent_index,
    child_slot,
    out_grad,
):
    bf16, f32 = jnp.bfloat16, jnp.float32
    devices = 1
    for name in AXES:
        devices *= lax.axis_size(name)
    row_count, channels = fine_rows.shape
    owned, width = out_grad.shape
    part = coarse_out_weight.shape[0]
    blocks = row_count // LANES
    heads = channels // HD
    coarse_heads = part // HD
    coarse_count = 4 * part * width // LANES
    pool_count = SLOTS // 2 * channels * width // LANES
    fine_count = 2 * channels * channels // LANES
    core = lax.axis_index("sub").astype(jnp.int32).reshape(1)
    first_parent = (lax.axis_index(AXES) * owned).astype(jnp.int32).reshape(1)
    rows = fine_rows.T
    parent_row = parent_index.reshape(1, row_count)
    slot_row = child_slot.reshape(1, row_count)
    own_qkv = coarse_qkv_weight.transpose(0, 2, 1).reshape(3 * part, width)
    other_qkv = swap_cores(own_qkv)
    other_out = swap_cores(coarse_out_weight)
    wide_rows = heads * LANES

    def in_hbm(*arrays):
        return [pltpu.with_memory_space_constraint(array, pltpu.HBM) for array in arrays]

    def like(*arrays):
        return [(array.shape, array.dtype) for array in arrays]

    def block_outs(count):
        return [
            ((channels, count * LANES), bf16),
            ((channels, count * LANES), bf16),
            ((3 * channels, count * LANES), bf16),
            ((count, LANES, wide_rows), bf16),
            ((count * heads, LANES), f32),
        ]

    sources = (rows, qkv_weight, out_weight, parent_row, slot_row)
    first = call(
        fine_first,
        like(*sources) + block_outs(1) + [((SPILL, channels), bf16)],
        [(1, channels + SPILL, wide_rows)],
        first_parent,
        *in_hbm(*sources),
        hbm=5,
        copies=5,
        micros=3,
    )
    rows, fine_qkv, fine_out, parent_row, slot_row = first[:5]
    hidden_first, *saved_first, spill = first[5:]
    spill_in = passed_along(spill, -1)
    sources = (pool_weight, own_qkv, coarse_out_weight, out_grad)
    second = call(
        fine_rest,
        like(*sources) + block_outs(blocks - 1),
        [(2, channels + SPILL, wide_rows)],
        *in_hbm(*sources),
        rows,
        fine_qkv,
        fine_out,
        scalars=0,
        hbm=4,
        copies=4,
        micros=2,
    )
    pool_weight, own_qkv, own_out, out_grad = second[:4]
    hidden_rest, *saved_rest = second[4:]
    children, upward, partial = call(
        pool,
        [((SLOTS, channels, owned), bf16), ((2, part, owned), bf16), ((owned, width), f32)],
        [(channels, row_count)],
        first_parent,
        hidden_first,
        hidden_rest,
        parent_row,
        slot_row,
        own_out,
        other_out,
        out_grad,
        pool_weight,
        micros=2,
    )
    coarse_rows, spill_grad, grad_parents, grad_pooled, coarse_input, mixed, grads = call(
        coarse_both,
        [
            ((owned, width), bf16),
            ((SPILL, channels), bf16),
            ((owned, width), bf16),
            ((SLOTS // 2, channels, 2 * owned), bf16),
            ((owned, width), bf16),
            ((2, part, owned), bf16),
            ((2, 3 * part, owned), bf16),
        ],
        [
            (2, part + SPILL, coarse_heads * LANES),
            (2, part, coarse_heads * LANES),
        ],
        partial,
        upward,
        spill_in,
        pool_weight,
        own_qkv,
        other_qkv,
        own_out,
        other_out,
        out_grad,
        scalars=0,
        micros=8,
    )
    spill_back = passed_along(spill_grad, 1)
    shared = (core, first_parent, rows, grad_pooled, parent_row, slot_row, fine_qkv, fine_out)
    rest_count = row_count - LANES
    row_rest, qkv_rest, out_rest, keep, give = call(
        fine_and_weights,
        [
            ((channels, rest_count), bf16),
            ((channels, 3 * channels), f32),
            ((channels, channels), f32),
            ((coarse_count + pool_count, LANES), bf16),
            ((coarse_count + pool_count, LANES), bf16),
        ],
        [
            (3 * channels, rest_count),
            (2, channels, wide_rows),
            (SLOTS, channels, owned),
        ],
        *shared,
        *saved_rest[2:],
        saved_rest[1],
        saved_rest[0],
        grad_parents,
        children,
        spill_in,
        coarse_input,
        mixed,
        grads,
        out_grad,
        scalars=2,
        micros=5,
    )
    spill_back, give = lax.optimization_barrier((spill_back, give))
    got = swap_cores(give)
    row_grad, fine_keep, fine_give = call(
        functools.partial(fine_back, 0),
        [
            ((channels, row_count), bf16),
            ((fine_count, LANES), bf16),
            ((fine_count, LANES), bf16),
        ],
        [(3 * channels, LANES), (1, channels, wide_rows)],
        *shared,
        *saved_first[2:],
        saved_first[1],
        saved_first[0],
        spill_back,
        row_rest,
        qkv_rest,
        out_rest,
        scalars=2,
        micros=2,
    )
    fine_got = swap_cores(fine_give)
    plane = lax.axis_size("zl") * lax.axis_size("y") * lax.axis_size("x")
    count = coarse_count + pool_count + fine_count
    unit = plane * 8
    padded = -(-count // unit) * unit
    (merged,) = call(
        merge, [((padded, LANES), bf16)], [], keep, got, fine_keep, fine_got, scalars=0, micros=1
    )
    total = sum_over_chips(merged.reshape(plane, padded // plane, LANES)).reshape(padded, LANES)
    other = swap_cores(total[coarse_count:count])
    coarse_scale = (owned * devices) ** (-0.5)
    pool_shape = (SLOTS * channels, width)
    half_pool = [(SLOTS // 2 * channels, width)]
    grad_coarse_qkv, grad_coarse_out, grad_pool = call(
        functools.partial(assemble_own, coarse_scale),
        [((3, part, width), f32), ((part, width), f32), (pool_shape, f32)],
        [],
        core,
        total,
        copies=1,
        staged=half_pool,
        in_place=2,
        micros=3,
    )
    grad_pool, grad_qkv, grad_out = call(
        functools.partial(
            assemble_other, (row_count * devices) ** (-0.5), coarse_scale, coarse_count
        ),
        [(pool_shape, f32), ((channels, 3 * channels), f32), ((channels, channels), f32)],
        [],
        core,
        grad_pool,
        total,
        other,
        hbm=1,
        copies=1,
        staged=half_pool,
        in_place=0,
        micros=2,
    )
    return (
        coarse_rows,
        row_grad.T,
        grad_qkv,
        grad_out,
        grad_pool,
        grad_coarse_qkv.transpose(0, 2, 1),
        grad_coarse_out,
    )


def solution(mesh):
    torus = Mesh(mesh.devices.reshape(-1, 2, 4, 4, mesh.shape["sub"]), AXES)
    in_specs = (
        P(AXES, None),
        P(),
        P(),
        P(),
        P(None, None, "sub"),
        P("sub", None),
        P(AXES),
        P(AXES),
        P(AXES, None),
    )
    out_specs = (
        P(AXES, None),
        P(AXES, None),
        P(),
        P(),
        P(),
        P(None, None, "sub"),
        P("sub", None),
    )
    return jax.shard_map(
        on_device, mesh=torus, in_specs=in_specs, out_specs=out_specs, check_vma=False
    )
```

```python
import functools

import jax
import jax.numpy as jnp
from jax import lax
from jax.experimental import pallas as pl
from jax.experimental.pallas import tpu as pltpu
from jax.sharding import Mesh, PartitionSpec as P

HD = 16
WINDOW_OCTANTS = 32
DILATION_STRIDE = 4
SLOTS = 8
LANES = 128
SPILL = 16
EPSILON = 1e-05
NEAR = ("zl", "y", "x")
AXES = ("zh",) + NEAR + ("sub",)
VMEM_BYTES = 20 * 1024 * 1024
FAR = -1e30


def passed_along(shard, by):
    count = 1
    for name in AXES:
        count *= lax.axis_size(name)
    pairs = [(i, i + by) for i in range(count) if 0 <= i + by < count]
    return lax.ppermute(shard, AXES, pairs)


def swap_cores(shard):
    return lax.ppermute(shard, "sub", [(0, 1), (1, 0)])


def bround(value):
    return value.astype(jnp.bfloat16)


def product(left, right, left_dim, right_dim):
    return lax.dot_general(
        left, right, (((left_dim,), (right_dim,)), ((), ())), preferred_element_type=jnp.float32
    )


def nn(left, right):
    return product(left, right, 1, 0)


def nt(left, right):
    return product(left, right, 1, 1)


def tn(left, right):
    return product(left, right, 0, 0)


def indicator(condition):
    return bround(jnp.where(condition, 1.0, 0.0))


def layer_norm(value, axis):
    center = value - jnp.mean(value, axis, keepdims=True)
    inverse = lax.rsqrt(jnp.mean(center * center, axis, keepdims=True) + EPSILON)
    return (center * inverse, inverse)


def layer_norm_back(normed, inverse, upstream, axis):
    return inverse * (
        upstream
        - jnp.mean(upstream, axis, keepdims=True)
        - normed * jnp.mean(upstream * normed, axis, keepdims=True)
    )


def window_rows(window_of):
    row = lax.broadcasted_iota(jnp.int32, (SPILL, LANES), 0)
    lane = lax.broadcasted_iota(jnp.int32, (SPILL, LANES), 1)
    return indicator(window_of(lane) == row)


def mask_rows(window_of, heads):
    row = lax.broadcasted_iota(jnp.int32, (SPILL, LANES), 0)
    lane = lax.broadcasted_iota(jnp.int32, (SPILL, LANES), 1)
    other = (window_of(lane) != row) & (row < LANES // WINDOW_OCTANTS)
    return jnp.concatenate([bround(jnp.where(other, FAR, 0.0))] * heads, 1)


def fine_window(at):
    return at % DILATION_STRIDE


def coarse_window(at):
    return at // WINDOW_OCTANTS


def spread(wide, rows, heads):
    for head in range(heads):
        at = slice(head * HD, (head + 1) * HD)
        wide[at, head * LANES : (head + 1) * LANES] = rows[at]


def softmax_parts(score):
    exponent = jnp.exp(score - jnp.max(score, 0, keepdims=True))
    return (bround(exponent), 1.0 / jnp.sum(exponent, 0, keepdims=True))


def attend_back(query, key, upstream, exponent, inverse, grad_prob):
    weighted = exponent.astype(jnp.float32)
    mean = inverse * jnp.sum(weighted * grad_prob, 0, keepdims=True)
    grad_score = bround(weighted * (grad_prob - mean))
    grad_value = nt(bround(upstream.astype(jnp.float32) * inverse), exponent)
    grad_query = nn(key, grad_score)
    grad_key = nt(query, grad_score)
    return (bround(grad_query), bround(grad_key), bround(grad_value))


def scaled(value):
    return value * jnp.bfloat16(HD**-0.5)


def fine_attention(qkv, wide, classes, heads, mixed, store):
    channels = heads * HD
    spread(wide, scaled(qkv[:channels]), heads)
    keys = jnp.concatenate([qkv[channels : 2 * channels], classes], 0)
    scores = tn(keys, wide[...])
    for head in range(heads):
        exponent, inverse = softmax_parts(scores[:, head * LANES : (head + 1) * LANES])
        value = qkv[2 * channels + head * HD : 2 * channels + (head + 1) * HD]
        mixed[head * HD : (head + 1) * HD] = bround(nn(value, exponent) * inverse)
        if store is not None:
            store(head, exponent, inverse)


def clear_wide(wide, heads, window_of):
    wide[...] = jnp.zeros(wide.shape, wide.dtype)
    for slot in range(wide.shape[0]):
        wide[slot, heads * HD :] = mask_rows(window_of, heads)


def fetch(pairs, arrived):
    copies = [
        pltpu.make_async_copy(source, target, arrived.at[i])
        for i, (source, target) in enumerate(pairs)
    ]
    for copy in copies:
        copy.start()
    return copies


def fine_blocks(
    first, rows, qkv_weight, out_weight, hidden, mixed, qkv, exponents, inverses, wide, wait
):
    channels, count = hidden.shape
    heads = channels // HD
    clear_wide(wide, heads, fine_window)
    classes = window_rows(fine_window)
    wait(0)
    wait(1)
    rows_float = rows[:, first * LANES : first * LANES + count].astype(jnp.float32)
    normed, _ = layer_norm(rows_float, 0)
    qkv[...] = bround(tn(qkv_weight[...], bround(normed)))
    for block in range(count // LANES):
        lanes = slice(block * LANES, (block + 1) * LANES)

        def store(head, exponent, inverse):
            exponents[block, :, head * LANES : (head + 1) * LANES] = exponent
            at = block * heads + head
            inverses[at : at + 1] = inverse

        fine_attention(
            qkv[:, lanes],
            wide.at[block % wide.shape[0]],
            classes,
            heads,
            mixed.at[:, lanes],
            store,
        )
    wait(2)
    hidden[...] = bround(rows_float + tn(out_weight[...], mixed[...]))


def fine_first(first_parent, *refs):
    sources, targets = refs[:5], refs[5:10]
    hidden, mixed, qkv, exponents, inverses, spill, wide, arrived = refs[10:]
    rows, qkv_weight, out_weight, parent_index, child_slot = targets
    copies = fetch(tuple(zip(sources, targets)), arrived)
    fine_blocks(
        0,
        rows,
        qkv_weight,
        out_weight,
        hidden,
        mixed,
        qkv,
        exponents,
        inverses,
        wide,
        lambda i: copies[i].wait(),
    )
    copies[3].wait()
    copies[4].wait()
    spill[...] = bround(nt(leading_slots(parent_index, child_slot, first_parent), hidden[...]))


def fine_rest(*refs):
    sources, (rows, qkv_weight, out_weight) = refs[:4], refs[4:7]
    targets = refs[7:11]
    hidden, mixed, qkv, exponents, inverses, wide, arrived = refs[11:]
    copies = fetch(tuple(zip(sources, targets)), arrived)
    fine_blocks(
        1,
        rows,
        qkv_weight,
        out_weight,
        hidden,
        mixed,
        qkv,
        exponents,
        inverses,
        wide,
        lambda i: None,
    )
    for copy in copies:
        copy.wait()


def leading_slots(parent_index, child_slot, first_parent):
    slot = lax.broadcasted_iota(jnp.int32, (SPILL, LANES), 0)
    before = parent_index[:, :LANES] < first_parent[0]
    return indicator(before & (child_slot[:, :LANES] == slot))


def slot_numbers(parent_index, child_slot, first_parent, owned):
    parent = lax.broadcasted_iota(jnp.int32, (owned, parent_index.shape[1]), 0)
    mine = parent_index - first_parent[0] == parent
    return jnp.where(mine, child_slot, -1)


def pool(
    first_parent,
    first_hidden,
    rest_hidden,
    parent_index,
    child_slot,
    own_out,
    other_out,
    out_grad,
    pool_weight,
    children,
    upward,
    partial,
    hidden,
):
    owned = out_grad.shape[0]
    hidden[:, :LANES] = first_hidden[...]
    hidden[:, LANES:] = rest_hidden[...]
    slot_of = slot_numbers(parent_index[...], child_slot[...], first_parent, owned)
    for slot in range(0, SLOTS, 2):
        both = jnp.concatenate([indicator(slot_of == slot), indicator(slot_of == slot + 1)], 0)
        pair = bround(nt(hidden[...], both))
        children[slot] = pair[:, :owned]
        children[slot + 1] = pair[:, owned:]
    channels = hidden.shape[0]
    total = jnp.zeros(partial.shape, jnp.float32)
    for slot in range(SLOTS):
        total += tn(children[slot], pool_weight[slot * channels : (slot + 1) * channels])
    partial[...] = total
    for half, out_weight in enumerate((own_out, other_out)):
        upward[half] = bround(nt(out_weight[...], out_grad[...]))


def coarse_both(
    partial,
    upward,
    spill,
    pool_weight,
    own_qkv,
    other_qkv,
    out_grad,
    parents,
    spill_grad,
    grad_parents,
    grad_pooled,
    coarse_input,
    mixed,
    grads,
    wide_query,
    wide_grad,
):
    owned, width = out_grad.shape
    channels = spill.shape[1]
    part = upward.shape[1]
    heads = part // HD
    halves = range(2)
    qkv_weights = (own_qkv, other_qkv)
    for wide in (wide_query, wide_grad):
        wide[...] = jnp.zeros(wide.shape, wide.dtype)
    for half in halves:
        wide_query[half, part:] = mask_rows(coarse_window, heads)
    spill_row = lax.broadcasted_iota(jnp.int32, (SPILL, channels), 0)
    late = jnp.zeros((SPILL, width), jnp.float32)
    for slot in range(SLOTS):
        chosen = jnp.where(spill_row == slot, spill[...], jnp.zeros_like(spill))
        late += nn(chosen, pool_weight[slot * channels : (slot + 1) * channels])
    late = jnp.sum(late, 0, keepdims=True)
    at_last = lax.broadcasted_iota(jnp.int32, (owned, width), 0) == owned - 1
    parents[...] = bround(partial[...] + jnp.where(at_last, late, 0.0))
    normed, inverse = layer_norm(parents[...].astype(jnp.float32), 1)
    coarse_input[...] = bround(normed)
    upstream = out_grad[...]
    classes = window_rows(coarse_window)
    qkvs = [bround(nt(qkv_weights[half][...], coarse_input[...])) for half in halves]
    for half in halves:
        spread(wide_query.at[half], scaled(qkvs[half][:part]), heads)
    scores = [
        tn(jnp.concatenate([qkvs[half][part : 2 * part], classes], 0), wide_query[half])
        for half in halves
    ]
    parts = {}
    for half in halves:
        for head in range(heads):
            at = slice(head * HD, (head + 1) * HD)
            lanes = slice(head * LANES, (head + 1) * LANES)
            exponent, scale = softmax_parts(scores[half][:, lanes])
            parts[half, head] = (exponent, scale)
            value = qkvs[half][2 * part + head * HD : 2 * part + (head + 1) * HD]
            mixed[half, at] = bround(nn(value, exponent) * scale)
            weighted = scaled(upward[half, at]).astype(jnp.float32) * scale
            wide_grad[half, at, lanes] = bround(weighted)
    grad_probs = [tn(qkvs[half][2 * part :], wide_grad[half]) for half in halves]
    for half in halves:
        for head in range(heads):
            at = [slice(i * part + head * HD, i * part + (head + 1) * HD) for i in range(3)]
            back = attend_back(
                qkvs[half][at[0]],
                qkvs[half][at[1]],
                upward[half, at[0]],
                *parts[half, head],
                grad_probs[half][:, head * LANES : (head + 1) * LANES],
            )
            for which in range(3):
                grads[half, at[which]] = back[which]
    grad_normed = sum(tn(grads[half], qkv_weights[half][...]) for half in halves)
    upstream_total = bround(
        upstream.astype(jnp.float32) + layer_norm_back(normed, inverse, grad_normed, 1)
    )
    grad_parents[...] = upstream_total
    grad_all = bround(nt(pool_weight[...], upstream_total))
    last = lax.broadcasted_iota(jnp.int32, (SPILL, owned), 1) == owned - 1
    spill_slot = lax.broadcasted_iota(jnp.int32, (SPILL, owned), 0)
    edge_total = jnp.zeros((SPILL, channels), jnp.float32)
    for slot in range(SLOTS):
        grad_slot = grad_all[slot * channels : (slot + 1) * channels]
        grad_pooled[slot // 2, :, slot % 2 * owned : (slot % 2 + 1) * owned] = grad_slot
        edge_total += nt(indicator(last & (spill_slot == slot)), grad_slot)
    spill_grad[...] = bround(edge_total)


def coarse_weights(
    core_ref,
    grad_parents,
    children,
    spill,
    coarse_input,
    mixed,
    grads,
    out_grad,
    keep,
    give,
    pooled,
):
    core = core_ref[0]
    width = out_grad.shape[1]
    owned, channels = out_grad.shape[0], pooled.shape[1]
    part = mixed.shape[1]
    last = lax.broadcasted_iota(jnp.int32, (SPILL, owned), 1) == owned - 1
    spill_slot = lax.broadcasted_iota(jnp.int32, (SPILL, owned), 0)
    for slot in range(0, SLOTS, 2):
        edges = [indicator(last & (spill_slot == at)) for at in (slot, slot + 1)]
        edge = bround(tn(spill[...], jnp.concatenate(edges, 1)))
        pooled[slot] = children[slot] + edge[:, :owned]
        pooled[slot + 1] = children[slot + 1] + edge[:, owned:]
    panels = width // LANES

    def store(target, start, value):
        for panel in range(panels):
            at = start + panel * value.shape[0]
            target[at : at + value.shape[0]] = bround(
                value[:, panel * LANES : (panel + 1) * LANES]
            )

    for half, target in enumerate((keep, give)):
        store(target, 0, nn(grads[half], coarse_input[...]))
        store(target, 3 * part * panels, nn(mixed[half], out_grad[...]))
    base = 4 * part * panels
    for target, first in ((keep, core), (give, 1 - core)):
        for step in range(SLOTS // 2):
            grad_pool = nn(pooled[first * (SLOTS // 2) + step], grad_parents[...])
            store(target, base + step * panels * channels, grad_pool)


def fine_back(
    first_block,
    core_ref,
    first_parent,
    rows,
    grad_pooled,
    parent_index,
    child_slot,
    qkv_weight,
    out_weight,
    exponents,
    inverses,
    qkv,
    mixed,
    *rest,
):
    if first_block:
        row_grad, qkv_total, out_total, grads, wide = rest
    else:
        spill_grad, qkv_rest, out_rest = rest[:3]
        row_grad, keep, give, grads, wide = rest[3:]
    channels, count = mixed.shape
    owned = grad_pooled.shape[2] // 2
    heads = channels // HD
    span = slice(first_block * LANES, first_block * LANES + count)
    normed, inverse = layer_norm(rows[:, span].astype(jnp.float32), 0)
    slot_of = slot_numbers(parent_index[:, span], child_slot[:, span], first_parent, owned)
    upstream = jnp.zeros((channels, count), jnp.float32)
    for slot in range(0, SLOTS, 2):
        both = jnp.concatenate([indicator(slot_of == slot), indicator(slot_of == slot + 1)], 0)
        upstream += nn(grad_pooled[slot // 2], both)
    if not first_block:
        leading = leading_slots(parent_index, child_slot, first_parent)
        upstream += tn(spill_grad[...], leading)
    upstream = bround(upstream)
    upward = bround(nn(out_weight[...], upstream))
    wide[...] = jnp.zeros(wide.shape, wide.dtype)
    for block in range(count // LANES):
        lanes = slice(block * LANES, (block + 1) * LANES)
        grad_rows = wide.at[block % wide.shape[0]]
        scales = [
            inverses[block * heads + head : block * heads + head + 1] for head in range(heads)
        ]
        for head in range(heads):
            at = slice(head * HD, (head + 1) * HD)
            weighted = scaled(upward[at, lanes]).astype(jnp.float32) * scales[head]
            grad_rows[at, head * LANES : (head + 1) * LANES] = bround(weighted)
        grad_probs = tn(qkv[2 * channels :, lanes], grad_rows[...])
        for head in range(heads):
            at = [slice(i * channels + head * HD, i * channels + (head + 1) * HD) for i in range(3)]
            out = slice(head * LANES, (head + 1) * LANES)
            back = attend_back(
                qkv[at[0], lanes],
                qkv[at[1], lanes],
                upward[at[0], lanes],
                exponents[block, :, out],
                scales[head],
                grad_probs[:, out],
            )
            for which in range(3):
                grads[at[which], lanes] = back[which]
    grad_normed = nn(qkv_weight[...], grads[...])
    total = upstream.astype(jnp.float32) + layer_norm_back(normed, inverse, grad_normed, 0)
    grad_qkv = nt(bround(normed), grads[...])
    grad_out = nt(mixed[...], upstream)
    row_grad[...] = bround(total)
    if first_block:
        qkv_total[...] = grad_qkv
        out_total[...] = grad_out
        return
    grad_qkv = bround(grad_qkv + qkv_rest[...])
    grad_out = bround(grad_out + out_rest[...])
    core = core_ref[0]
    whole = 3 * channels // LANES
    panels = [grad_qkv[:, i * LANES : (i + 1) * LANES] for i in range(whole)]
    panels.append(jnp.concatenate([grad_qkv[:, whole * LANES :], grad_out[:, LANES:]], 1))
    panels.append(grad_out[:, :LANES])
    half = len(panels) // 2
    for i in range(half):
        at = slice(i * channels, (i + 1) * channels)
        keep[at] = jnp.where(core == 0, panels[i], panels[half + i])
        give[at] = jnp.where(core == 0, panels[half + i], panels[i])


def fine_and_weights(core_ref, first_parent, *refs):
    fine_in, weight_in, refs = refs[:10], refs[10:17], refs[17:]
    fine_back(1, core_ref, first_parent, *fine_in, *refs[:3], *refs[5:7])
    coarse_weights(core_ref, *weight_in, *refs[3:5], *refs[7:])


def merge(keep, got, fine_keep, fine_got, total):
    first, second = keep.shape[0], fine_keep.shape[0]
    total[:first] = keep[...] + got[...]
    total[first : first + second] = fine_keep[...] + fine_got[...]
    pad = total.shape[0] - first - second
    total[first + second :] = jnp.zeros((pad, LANES), total.dtype)


class Copies:
    def __init__(self, arrived):
        self.arrived, self.started = arrived, []

    def start(self, source, target):
        copy = pltpu.make_async_copy(source, target, self.arrived.at[len(self.started)])
        copy.start()
        self.started.append(copy)

    def finish(self):
        for copy in self.started:
            copy.wait()


def unpack_pool(copies, source, start, half, staged, target, scale):
    panels = staged.shape[1] // LANES
    channels = staged.shape[0] * 2 // SLOTS
    for step in range(SLOTS // 2):
        rows = slice(step * channels, (step + 1) * channels)
        for panel in range(panels):
            at = start + (step * panels + panel) * channels
            staged[rows, panel * LANES : (panel + 1) * LANES] = (
                source[at : at + channels].astype(jnp.float32) * scale
            )
        row = pl.multiple_of(half * staged.shape[0] + step * channels, 8)
        copies.start(staged.at[rows], target.at[pl.ds(row, channels)])


def assemble_own(
    scale,
    core_ref,
    mine,
    row_first,
    row_rest,
    parents,
    mixed,
    own_out,
    other_out,
    grad_coarse_qkv,
    grad_coarse_out,
    grad_pool,
    row_grad,
    coarse_rows,
    rows_staged,
    pool_staged,
    qkv_staged,
    out_staged,
    arrived,
):
    copies = Copies(arrived)
    copies.start(row_first, row_grad.at[:, :LANES])
    copies.start(row_rest, row_grad.at[:, LANES:])
    part, width = out_staged.shape
    panels = width // LANES
    unpack_pool(
        copies, mine, 4 * part * panels, core_ref[0], pool_staged, grad_pool, scale
    )

    def coarse(start):
        return mine[start : start + part].astype(jnp.float32) * scale

    first = 3 * part * panels
    for which in range(3):
        for panel in range(panels):
            lanes = slice(panel * LANES, (panel + 1) * LANES)
            qkv_staged[which, :, lanes] = coarse((3 * panel + which) * part)
        copies.start(qkv_staged.at[which], grad_coarse_qkv.at[which])
    for panel in range(panels):
        out_staged[:, panel * LANES : (panel + 1) * LANES] = coarse(first + panel * part)
    copies.start(out_staged, grad_coarse_out)
    summed = tn(mixed[0], own_out[...]) + tn(mixed[1], other_out[...])
    rows_staged[...] = bround(parents[...].astype(jnp.float32) + summed)
    copies.start(rows_staged, coarse_rows)
    copies.finish()


def assemble_other(
    fine_scale,
    coarse_scale,
    base,
    core_ref,
    pool_in,
    mine,
    other,
    grad_pool,
    grad_qkv,
    grad_out,
    pool_staged,
    qkv_staged,
    out_staged,
    arrived,
):
    copies = Copies(arrived)
    core = core_ref[0]
    channels = out_staged.shape[0]
    edge = channels % LANES
    skip = pool_staged.shape[0] * pool_staged.shape[1] // LANES
    fine = []
    for half in range(2):
        for i in range(3):
            at = skip + i * channels
            near = mine[base + at : base + at + channels].astype(jnp.float32)
            far = other[at : at + channels].astype(jnp.float32)
            fine.append(jnp.where(core == half, near, far) * fine_scale)
    for i in range(4):
        qkv_staged[:, i * LANES : (i + 1) * LANES] = fine[i]
    qkv_staged[:, 4 * LANES :] = fine[4][:, :edge]
    copies.start(qkv_staged, grad_qkv)
    out_staged[:, :LANES] = fine[5]
    out_staged[:, LANES:] = fine[4][:, edge:]
    copies.start(out_staged, grad_out)
    unpack_pool(copies, other, 0, 1 - core, pool_staged, grad_pool, coarse_scale)
    copies.finish()


def call(
    kernel,
    outs,
    scratch,
    *operands,
    scalars=1,
    micros=1,
    hbm=0,
    copies=0,
    staged=(),
    to_hbm=False,
    aliases=None,
):
    spaces = [pltpu.SMEM] * scalars + [pltpu.HBM] * hbm
    spaces += [pltpu.VMEM] * (len(operands) - len(spaces))
    out_spaces = [pltpu.HBM if to_hbm else pltpu.VMEM] * len(outs)
    return pl.pallas_call(
        kernel,
        out_shape=[jax.ShapeDtypeStruct(shape, dtype) for shape, dtype in outs],
        in_specs=[pl.BlockSpec(memory_space=space) for space in spaces],
        out_specs=[pl.BlockSpec(memory_space=space) for space in out_spaces],
        input_output_aliases=aliases or {},
        scratch_shapes=[pltpu.VMEM(shape, jnp.bfloat16) for shape in scratch]
        + [pltpu.VMEM(shape, jnp.float32) for shape in staged]
        + ([pltpu.SemaphoreType.DMA((copies,))] if copies else []),
        compiler_params=pltpu.CompilerParams(vmem_limit_bytes=VMEM_BYTES),
        cost_estimate=pl.CostEstimate(
            flops=int(micros * 10**9), bytes_accessed=int(micros * 10**6), transcendentals=0
        ),
    )(*operands)


def float_sum(stacked):
    return bround(jnp.sum(stacked.astype(jnp.float32), 0))


def sum_over_chips(parts):
    plane = lax.all_to_all(parts, NEAR, 0, 0, tiled=True)
    slab = float_sum(plane)
    copies = jnp.broadcast_to(slab, (lax.axis_size("zh"),) + slab.shape)
    slab = float_sum(lax.all_to_all(copies, "zh", 0, 0, tiled=True))
    copies = jnp.broadcast_to(slab, parts.shape)
    return lax.all_to_all(copies, NEAR, 0, 0, tiled=True)


def on_device(
    fine_rows,
    qkv_weight,
    out_weight,
    pool_weight,
    coarse_qkv_weight,
    coarse_out_weight,
    parent_index,
    child_slot,
    out_grad,
):
    bf16, f32 = jnp.bfloat16, jnp.float32
    devices = 1
    for name in AXES:
        devices *= lax.axis_size(name)
    row_count, channels = fine_rows.shape
    owned, width = out_grad.shape
    part = coarse_out_weight.shape[0]
    blocks = row_count // LANES
    heads = channels // HD
    coarse_heads = part // HD
    coarse_count = 4 * part * width // LANES
    pool_count = SLOTS // 2 * channels * width // LANES
    fine_count = 2 * channels * channels // LANES
    core = lax.axis_index("sub").astype(jnp.int32).reshape(1)
    first_parent = (lax.axis_index(AXES) * owned).astype(jnp.int32).reshape(1)
    rows = fine_rows.T
    parent_row = parent_index.reshape(1, row_count)
    slot_row = child_slot.reshape(1, row_count)
    own_qkv = coarse_qkv_weight.transpose(0, 2, 1).reshape(3 * part, width)
    other_qkv = swap_cores(own_qkv)
    other_out = swap_cores(coarse_out_weight)
    wide_rows = heads * LANES

    def in_hbm(*arrays):
        return [pltpu.with_memory_space_constraint(array, pltpu.HBM) for array in arrays]

    def like(*arrays):
        return [(array.shape, array.dtype) for array in arrays]

    def block_outs(count):
        return [
            ((channels, count * LANES), bf16),
            ((channels, count * LANES), bf16),
            ((3 * channels, count * LANES), bf16),
            ((count, LANES, wide_rows), bf16),
            ((count * heads, LANES), f32),
        ]

    sources = (rows, qkv_weight, out_weight, parent_row, slot_row)
    first = call(
        fine_first,
        like(*sources) + block_outs(1) + [((SPILL, channels), bf16)],
        [(1, channels + SPILL, wide_rows)],
        first_parent,
        *in_hbm(*sources),
        hbm=5,
        copies=5,
        micros=3,
    )
    rows, fine_qkv, fine_out, parent_row, slot_row = first[:5]
    hidden_first, *saved_first, spill = first[5:]
    spill_in = passed_along(spill, -1)
    sources = (pool_weight, own_qkv, coarse_out_weight, out_grad)
    second = call(
        fine_rest,
        like(*sources) + block_outs(blocks - 1),
        [(2, channels + SPILL, wide_rows)],
        *in_hbm(*sources),
        rows,
        fine_qkv,
        fine_out,
        scalars=0,
        hbm=4,
        copies=4,
        micros=2,
    )
    pool_weight, own_qkv, own_out, out_grad = second[:4]
    hidden_rest, *saved_rest = second[4:]
    children, upward, partial = call(
        pool,
        [((SLOTS, channels, owned), bf16), ((2, part, owned), bf16), ((owned, width), f32)],
        [(channels, row_count)],
        first_parent,
        hidden_first,
        hidden_rest,
        parent_row,
        slot_row,
        own_out,
        other_out,
        out_grad,
        pool_weight,
        micros=2,
    )
    parents, spill_grad, grad_parents, grad_pooled, coarse_input, mixed, grads = call(
        coarse_both,
        [
            ((owned, width), bf16),
            ((SPILL, channels), bf16),
            ((owned, width), bf16),
            ((SLOTS // 2, channels, 2 * owned), bf16),
            ((owned, width), bf16),
            ((2, part, owned), bf16),
            ((2, 3 * part, owned), bf16),
        ],
        [
            (2, part + SPILL, coarse_heads * LANES),
            (2, part, coarse_heads * LANES),
        ],
        partial,
        upward,
        spill_in,
        pool_weight,
        own_qkv,
        other_qkv,
        out_grad,
        scalars=0,
        micros=8,
    )
    spill_back = passed_along(spill_grad, 1)
    shared = (core, first_parent, rows, grad_pooled, parent_row, slot_row, fine_qkv, fine_out)
    rest_count = row_count - LANES
    row_rest, qkv_rest, out_rest, keep, give = call(
        fine_and_weights,
        [
            ((channels, rest_count), bf16),
            ((channels, 3 * channels), f32),
            ((channels, channels), f32),
            ((coarse_count + pool_count, LANES), bf16),
            ((coarse_count + pool_count, LANES), bf16),
        ],
        [
            (3 * channels, rest_count),
            (2, channels, wide_rows),
            (SLOTS, channels, owned),
        ],
        *shared,
        *saved_rest[2:],
        saved_rest[1],
        saved_rest[0],
        grad_parents,
        children,
        spill_in,
        coarse_input,
        mixed,
        grads,
        out_grad,
        scalars=2,
        micros=5,
    )
    spill_back, give = lax.optimization_barrier((spill_back, give))
    got = swap_cores(give)
    row_first, fine_keep, fine_give = call(
        functools.partial(fine_back, 0),
        [
            ((channels, LANES), bf16),
            ((fine_count, LANES), bf16),
            ((fine_count, LANES), bf16),
        ],
        [(3 * channels, LANES), (1, channels, wide_rows)],
        *shared,
        *saved_first[2:],
        saved_first[1],
        saved_first[0],
        spill_back,
        qkv_rest,
        out_rest,
        scalars=2,
        micros=2,
    )
    fine_got = swap_cores(fine_give)
    plane = lax.axis_size("zl") * lax.axis_size("y") * lax.axis_size("x")
    count = coarse_count + pool_count + fine_count
    unit = plane * 8
    padded = -(-count // unit) * unit
    (merged,) = call(
        merge, [((padded, LANES), bf16)], [], keep, got, fine_keep, fine_got, scalars=0, micros=1
    )
    total = sum_over_chips(merged.reshape(plane, padded // plane, LANES)).reshape(padded, LANES)
    other = swap_cores(total[coarse_count:count])
    coarse_scale = (owned * devices) ** (-0.5)
    pool_shape = (SLOTS * channels, width)
    half_pool = (SLOTS // 2 * channels, width)
    grad_coarse_qkv, grad_coarse_out, grad_pool, row_grad, coarse_rows = call(
        functools.partial(assemble_own, coarse_scale),
        [
            ((3, part, width), f32),
            ((part, width), f32),
            (pool_shape, f32),
            ((channels, row_count), bf16),
            ((owned, width), bf16),
        ],
        [(owned, width)],
        core,
        total,
        row_first,
        row_rest,
        parents,
        mixed,
        own_out,
        other_out,
        copies=7 + SLOTS // 2,
        staged=[half_pool, (3, part, width), (part, width)],
        to_hbm=True,
        micros=3,
    )
    grad_pool, grad_qkv, grad_out = call(
        functools.partial(
            assemble_other, (row_count * devices) ** (-0.5), coarse_scale, coarse_count
        ),
        [(pool_shape, f32), ((channels, 3 * channels), f32), ((channels, channels), f32)],
        [],
        core,
        grad_pool,
        total,
        other,
        hbm=1,
        copies=2 + SLOTS // 2,
        staged=[half_pool, (channels, 3 * channels), (channels, channels)],
        to_hbm=True,
        aliases={1: 0},
        micros=2,
    )
    return (
        coarse_rows,
        row_grad.T,
        grad_qkv,
        grad_out,
        grad_pool,
        grad_coarse_qkv.transpose(0, 2, 1),
        grad_coarse_out,
    )


def solution(mesh):
    torus = Mesh(mesh.devices.reshape(-1, 2, 4, 4, mesh.shape["sub"]), AXES)
    in_specs = (
        P(AXES, None),
        P(),
        P(),
        P(),
        P(None, None, "sub"),
        P("sub", None),
        P(AXES),
        P(AXES),
        P(AXES, None),
    )
    out_specs = (
        P(AXES, None),
        P(AXES, None),
        P(),
        P(),
        P(),
        P(None, None, "sub"),
        P("sub", None),
    )
    return jax.shard_map(
        on_device, mesh=torus, in_specs=in_specs, out_specs=out_specs, check_vma=False
    )
```

```python
import functools

import jax
import jax.numpy as jnp
from jax import lax
from jax.experimental import pallas as pl
from jax.experimental.pallas import tpu as pltpu
from jax.sharding import Mesh, PartitionSpec as P

HD = 16
WINDOW_OCTANTS = 32
DILATION_STRIDE = 4
SLOTS = 8
LANES = 128
SPILL = 16
EPSILON = 1e-05
NEAR = ("zl", "y", "x")
AXES = ("zh",) + NEAR + ("sub",)
VMEM_BYTES = 20 * 1024 * 1024
FAR = -1e30


def passed_along(shard, by):
    count = 1
    for name in AXES:
        count *= lax.axis_size(name)
    pairs = [(i, i + by) for i in range(count) if 0 <= i + by < count]
    return lax.ppermute(shard, AXES, pairs)


def swap_cores(shard):
    return lax.ppermute(shard, "sub", [(0, 1), (1, 0)])


def bround(value):
    return value.astype(jnp.bfloat16)


def product(left, right, left_dim, right_dim):
    return lax.dot_general(
        left, right, (((left_dim,), (right_dim,)), ((), ())), preferred_element_type=jnp.float32
    )


def nn(left, right):
    return product(left, right, 1, 0)


def nt(left, right):
    return product(left, right, 1, 1)


def tn(left, right):
    return product(left, right, 0, 0)


def indicator(condition):
    return bround(jnp.where(condition, 1.0, 0.0))


def layer_norm(value, axis):
    center = value - jnp.mean(value, axis, keepdims=True)
    inverse = lax.rsqrt(jnp.mean(center * center, axis, keepdims=True) + EPSILON)
    return (center * inverse, inverse)


def layer_norm_back(normed, inverse, upstream, axis):
    return inverse * (
        upstream
        - jnp.mean(upstream, axis, keepdims=True)
        - normed * jnp.mean(upstream * normed, axis, keepdims=True)
    )


def window_rows(window_of):
    row = lax.broadcasted_iota(jnp.int32, (SPILL, LANES), 0)
    lane = lax.broadcasted_iota(jnp.int32, (SPILL, LANES), 1)
    return indicator(window_of(lane) == row)


def mask_rows(window_of, heads):
    row = lax.broadcasted_iota(jnp.int32, (SPILL, LANES), 0)
    lane = lax.broadcasted_iota(jnp.int32, (SPILL, LANES), 1)
    other = (window_of(lane) != row) & (row < LANES // WINDOW_OCTANTS)
    return jnp.concatenate([bround(jnp.where(other, FAR, 0.0))] * heads, 1)


def fine_window(at):
    return at % DILATION_STRIDE


def coarse_window(at):
    return at // WINDOW_OCTANTS


def spread(wide, rows, heads):
    for head in range(heads):
        at = slice(head * HD, (head + 1) * HD)
        wide[at, head * LANES : (head + 1) * LANES] = rows[at]


def softmax_parts(score):
    exponent = jnp.exp(score - jnp.max(score, 0, keepdims=True))
    return (bround(exponent), 1.0 / jnp.sum(exponent, 0, keepdims=True))


def attend_back(query, key, upstream, exponent, inverse, grad_prob):
    weighted = exponent.astype(jnp.float32)
    mean = inverse * jnp.sum(weighted * grad_prob, 0, keepdims=True)
    grad_score = bround(weighted * (grad_prob - mean))
    grad_value = nt(bround(upstream.astype(jnp.float32) * inverse), exponent)
    grad_query = nn(key, grad_score)
    grad_key = nt(query, grad_score)
    return (bround(grad_query), bround(grad_key), bround(grad_value))


def scaled(value):
    return value * jnp.bfloat16(HD**-0.5)


def fine_attention(qkv, wide, classes, heads, mixed, store):
    channels = heads * HD
    spread(wide, scaled(qkv[:channels]), heads)
    keys = jnp.concatenate([qkv[channels : 2 * channels], classes], 0)
    scores = tn(keys, wide[...])
    for head in range(heads):
        exponent, inverse = softmax_parts(scores[:, head * LANES : (head + 1) * LANES])
        value = qkv[2 * channels + head * HD : 2 * channels + (head + 1) * HD]
        mixed[head * HD : (head + 1) * HD] = bround(nn(value, exponent) * inverse)
        if store is not None:
            store(head, exponent, inverse)


def clear_wide(wide, heads, window_of):
    wide[...] = jnp.zeros(wide.shape, wide.dtype)
    for slot in range(wide.shape[0]):
        wide[slot, heads * HD :] = mask_rows(window_of, heads)


def fetch(pairs, arrived):
    copies = [
        pltpu.make_async_copy(source, target, arrived.at[i])
        for i, (source, target) in enumerate(pairs)
    ]
    for copy in copies:
        copy.start()
    return copies


def fine_blocks(
    rows, qkv_weight, out_weight, hidden, mixed, qkv, exponents, inverses, wide
):
    channels, count = hidden.shape
    heads = channels // HD
    clear_wide(wide, heads, fine_window)
    classes = window_rows(fine_window)
    rows_float = rows[...].astype(jnp.float32)
    normed, _ = layer_norm(rows_float, 0)
    qkv[...] = bround(tn(qkv_weight[...], bround(normed)))
    for block in range(count // LANES):
        lanes = slice(block * LANES, (block + 1) * LANES)

        def store(head, exponent, inverse):
            exponents[block, :, head * LANES : (head + 1) * LANES] = exponent
            at = block * heads + head
            inverses[at : at + 1] = inverse

        fine_attention(
            qkv[:, lanes],
            wide.at[block % wide.shape[0]],
            classes,
            heads,
            mixed.at[:, lanes],
            store,
        )
    hidden[...] = bround(rows_float + tn(out_weight[...], mixed[...]))


def bring(first_parent, *refs):
    sources, targets, packed, arrived = refs[:5], refs[5:10], refs[10], refs[11]
    copies = fetch(tuple(zip(sources, targets)), arrived)
    rows, _, _, parent_index, child_slot = targets
    for i in (0, 3, 4):
        copies[i].wait()
    channels = rows.shape[0]
    packed[:channels] = rows[:, :LANES]
    packed[channels:] = leading_slots(parent_index, child_slot, first_parent)
    copies[1].wait()
    copies[2].wait()


def fine_forward(*refs):
    sources, (rows, qkv_weight, out_weight) = refs[:4], refs[4:7]
    targets, outs, wide, arrived = refs[7:11], refs[11:16], refs[16], refs[17]
    copies = fetch(tuple(zip(sources, targets)), arrived)
    fine_blocks(rows, qkv_weight, out_weight, *outs, wide)
    for copy in copies:
        copy.wait()


def leading_slots(parent_index, child_slot, first_parent):
    slot = lax.broadcasted_iota(jnp.int32, (SPILL, LANES), 0)
    before = parent_index[:, :LANES] < first_parent[0]
    return indicator(before & (child_slot[:, :LANES] == slot))


def slot_numbers(parent_index, child_slot, first_parent, owned):
    parent = lax.broadcasted_iota(jnp.int32, (owned, parent_index.shape[1]), 0)
    mine = parent_index - first_parent[0] == parent
    return jnp.where(mine, child_slot, -1)


def pool(
    first_parent,
    hidden,
    parent_index,
    child_slot,
    own_out,
    other_out,
    out_grad,
    pool_weight,
    children,
    upward,
    partial,
):
    owned = out_grad.shape[0]
    slot_of = slot_numbers(parent_index[...], child_slot[...], first_parent, owned)
    for slot in range(0, SLOTS, 2):
        both = jnp.concatenate([indicator(slot_of == slot), indicator(slot_of == slot + 1)], 0)
        pair = bround(nt(hidden[...], both))
        children[slot] = pair[:, :owned]
        children[slot + 1] = pair[:, owned:]
    channels = hidden.shape[0]
    total = jnp.zeros(partial.shape, jnp.float32)
    for slot in range(SLOTS):
        total += tn(children[slot], pool_weight[slot * channels : (slot + 1) * channels])
    partial[...] = total
    for half, out_weight in enumerate((own_out, other_out)):
        upward[half] = bround(nt(out_weight[...], out_grad[...]))


def coarse_both(
    packed,
    fine_qkv,
    fine_out,
    partial,
    upward,
    pool_weight,
    own_qkv,
    other_qkv,
    out_grad,
    parents,
    spill,
    next_upstream,
    grad_parents,
    grad_pooled,
    coarse_input,
    mixed,
    grads,
    next_mixed,
    next_qkv,
    next_exponents,
    next_inverses,
    next_hidden,
    wide_next,
    wide_query,
    wide_grad,
):
    owned, width = out_grad.shape
    channels = fine_out.shape[0]
    fine_blocks(
        packed.at[:channels],
        fine_qkv,
        fine_out,
        next_hidden,
        next_mixed,
        next_qkv,
        next_exponents,
        next_inverses,
        wide_next,
    )
    leading = packed[channels:]
    spill[...] = bround(nt(leading, next_hidden[...]))
    part = upward.shape[1]
    heads = part // HD
    halves = range(2)
    qkv_weights = (own_qkv, other_qkv)
    for wide in (wide_query, wide_grad):
        wide[...] = jnp.zeros(wide.shape, wide.dtype)
    for half in halves:
        wide_query[half, part:] = mask_rows(coarse_window, heads)
    spill_row = lax.broadcasted_iota(jnp.int32, (SPILL, channels), 0)
    late = jnp.zeros((SPILL, width), jnp.float32)
    for slot in range(SLOTS):
        chosen = jnp.where(spill_row == slot, spill[...], jnp.zeros_like(spill))
        late += nn(chosen, pool_weight[slot * channels : (slot + 1) * channels])
    late = jnp.sum(late, 0, keepdims=True)
    at_last = lax.broadcasted_iota(jnp.int32, (owned, width), 0) == owned - 1
    parents[...] = bround(partial[...] + jnp.where(at_last, late, 0.0))
    normed, inverse = layer_norm(parents[...].astype(jnp.float32), 1)
    coarse_input[...] = bround(normed)
    upstream = out_grad[...]
    classes = window_rows(coarse_window)
    qkvs = [bround(nt(qkv_weights[half][...], coarse_input[...])) for half in halves]
    for half in halves:
        spread(wide_query.at[half], scaled(qkvs[half][:part]), heads)
    scores = [
        tn(jnp.concatenate([qkvs[half][part : 2 * part], classes], 0), wide_query[half])
        for half in halves
    ]
    parts = {}
    for half in halves:
        for head in range(heads):
            at = slice(head * HD, (head + 1) * HD)
            lanes = slice(head * LANES, (head + 1) * LANES)
            exponent, scale = softmax_parts(scores[half][:, lanes])
            parts[half, head] = (exponent, scale)
            value = qkvs[half][2 * part + head * HD : 2 * part + (head + 1) * HD]
            mixed[half, at] = bround(nn(value, exponent) * scale)
            weighted = scaled(upward[half, at]).astype(jnp.float32) * scale
            wide_grad[half, at, lanes] = bround(weighted)
    grad_probs = [tn(qkvs[half][2 * part :], wide_grad[half]) for half in halves]
    for half in halves:
        for head in range(heads):
            at = [slice(i * part + head * HD, i * part + (head + 1) * HD) for i in range(3)]
            back = attend_back(
                qkvs[half][at[0]],
                qkvs[half][at[1]],
                upward[half, at[0]],
                *parts[half, head],
                grad_probs[half][:, head * LANES : (head + 1) * LANES],
            )
            for which in range(3):
                grads[half, at[which]] = back[which]
    grad_normed = sum(tn(grads[half], qkv_weights[half][...]) for half in halves)
    upstream_total = bround(
        upstream.astype(jnp.float32) + layer_norm_back(normed, inverse, grad_normed, 1)
    )
    grad_parents[...] = upstream_total
    grad_all = bround(nt(pool_weight[...], upstream_total))
    last = lax.broadcasted_iota(jnp.int32, (SPILL, owned), 1) == owned - 1
    spill_slot = lax.broadcasted_iota(jnp.int32, (SPILL, owned), 0)
    edge_total = jnp.zeros((SPILL, channels), jnp.float32)
    for slot in range(SLOTS):
        grad_slot = grad_all[slot * channels : (slot + 1) * channels]
        grad_pooled[slot // 2, :, slot % 2 * owned : (slot % 2 + 1) * owned] = grad_slot
        edge_total += nt(indicator(last & (spill_slot == slot)), grad_slot)
    next_upstream[...] = bround(tn(bround(edge_total), leading))


def coarse_weights(
    core_ref,
    grad_parents,
    children,
    spill,
    coarse_input,
    mixed,
    grads,
    out_grad,
    keep,
    give,
    pooled,
):
    core = core_ref[0]
    width = out_grad.shape[1]
    owned, channels = out_grad.shape[0], pooled.shape[1]
    part = mixed.shape[1]
    last = lax.broadcasted_iota(jnp.int32, (SPILL, owned), 1) == owned - 1
    spill_slot = lax.broadcasted_iota(jnp.int32, (SPILL, owned), 0)
    for slot in range(0, SLOTS, 2):
        edges = [indicator(last & (spill_slot == at)) for at in (slot, slot + 1)]
        edge = bround(tn(spill[...], jnp.concatenate(edges, 1)))
        pooled[slot] = children[slot] + edge[:, :owned]
        pooled[slot + 1] = children[slot + 1] + edge[:, owned:]
    panels = width // LANES

    def store(target, start, value):
        for panel in range(panels):
            at = start + panel * value.shape[0]
            target[at : at + value.shape[0]] = bround(
                value[:, panel * LANES : (panel + 1) * LANES]
            )

    for half, target in enumerate((keep, give)):
        store(target, 0, nn(grads[half], coarse_input[...]))
        store(target, 3 * part * panels, nn(mixed[half], out_grad[...]))
    base = 4 * part * panels
    for target, first in ((keep, core), (give, 1 - core)):
        for step in range(SLOTS // 2):
            grad_pool = nn(pooled[first * (SLOTS // 2) + step], grad_parents[...])
            store(target, base + step * panels * channels, grad_pool)


def fine_back(
    core_ref,
    first_parent,
    rows,
    packed,
    grad_pooled,
    next_upstream,
    parent_index,
    child_slot,
    out_weight,
    *rest,
):
    own, beyond = rest[:4], rest[4:8]
    upstreams, grads, keep, give, wide = rest[8:]
    channels, row_count = rows.shape
    owned = grad_pooled.shape[2] // 2
    heads = channels // HD
    all_rows = jnp.concatenate([rows[...], packed[:channels]], 1)
    mixed = jnp.concatenate([own[3][...], beyond[3][...]], 1)
    normed, _ = layer_norm(all_rows.astype(jnp.float32), 0)
    slot_of = slot_numbers(parent_index[...], child_slot[...], first_parent, owned)
    upstream = jnp.zeros((channels, row_count), jnp.float32)
    for slot in range(0, SLOTS, 2):
        both = jnp.concatenate([indicator(slot_of == slot), indicator(slot_of == slot + 1)], 0)
        upstream += nn(grad_pooled[slot // 2], both)
    upstream = jnp.concatenate([bround(upstream), next_upstream[...]], 1)
    upstreams[...] = upstream
    upward = bround(nn(out_weight[...], upstream))
    wide[...] = jnp.zeros(wide.shape, wide.dtype)
    blocks = row_count // LANES
    for block in range(blocks + 1):
        exponents, inverses, qkv, _ = own if block < blocks else beyond
        within = block % blocks
        lanes = slice(block * LANES, (block + 1) * LANES)
        inner = slice(within * LANES, (within + 1) * LANES)
        grad_rows = wide.at[block % wide.shape[0]]
        scales = [
            inverses[within * heads + head : within * heads + head + 1] for head in range(heads)
        ]
        for head in range(heads):
            at = slice(head * HD, (head + 1) * HD)
            weighted = scaled(upward[at, lanes]).astype(jnp.float32) * scales[head]
            grad_rows[at, head * LANES : (head + 1) * LANES] = bround(weighted)
        grad_probs = tn(qkv[2 * channels :, inner], grad_rows[...])
        for head in range(heads):
            at = [slice(i * channels + head * HD, i * channels + (head + 1) * HD) for i in range(3)]
            out = slice(head * LANES, (head + 1) * LANES)
            back = attend_back(
                qkv[at[0], inner],
                qkv[at[1], inner],
                upward[at[0], lanes],
                exponents[within, :, out],
                scales[head],
                grad_probs[:, out],
            )
            for which in range(3):
                grads[at[which], lanes] = back[which]
    grad_qkv = bround(nt(bround(normed), grads[...]))
    grad_out = bround(nt(mixed, upstream))
    core = core_ref[0]
    whole = 3 * channels // LANES
    panels = [grad_qkv[:, i * LANES : (i + 1) * LANES] for i in range(whole)]
    panels.append(jnp.concatenate([grad_qkv[:, whole * LANES :], grad_out[:, LANES:]], 1))
    panels.append(grad_out[:, :LANES])
    half = len(panels) // 2
    for i in range(half):
        at = slice(i * channels, (i + 1) * channels)
        keep[at] = jnp.where(core == 0, panels[i], panels[half + i])
        give[at] = jnp.where(core == 0, panels[half + i], panels[i])


def row_gradients(rows, packed, qkv_weight, upstream, grads, row_first, row_rest, row_next):
    channels, row_count = rows.shape
    all_rows = jnp.concatenate([rows[...], packed[:channels]], 1)
    normed, inverse = layer_norm(all_rows.astype(jnp.float32), 0)
    grad_normed = nn(qkv_weight[...], grads[...])
    total = upstream[...].astype(jnp.float32) + layer_norm_back(normed, inverse, grad_normed, 0)
    row_first[...] = total[:, :LANES]
    row_rest[...] = bround(total[:, LANES:row_count])
    row_next[...] = bround(total[:, row_count:])


def merge(keep, got, fine_keep, fine_got, total):
    first, second = keep.shape[0], fine_keep.shape[0]
    total[:first] = keep[...] + got[...]
    total[first : first + second] = fine_keep[...] + fine_got[...]
    pad = total.shape[0] - first - second
    total[first + second :] = jnp.zeros((pad, LANES), total.dtype)


class Copies:
    def __init__(self, arrived):
        self.arrived, self.started = arrived, []

    def start(self, source, target):
        copy = pltpu.make_async_copy(source, target, self.arrived.at[len(self.started)])
        copy.start()
        self.started.append(copy)

    def finish(self):
        for copy in self.started:
            copy.wait()


def unpack_pool(copies, source, start, half, staged, target, scale):
    panels = staged.shape[1] // LANES
    channels = staged.shape[0] * 2 // SLOTS
    for step in range(SLOTS // 2):
        rows = slice(step * channels, (step + 1) * channels)
        for panel in range(panels):
            at = start + (step * panels + panel) * channels
            staged[rows, panel * LANES : (panel + 1) * LANES] = (
                source[at : at + channels].astype(jnp.float32) * scale
            )
        row = pl.multiple_of(half * staged.shape[0] + step * channels, 8)
        copies.start(staged.at[rows], target.at[pl.ds(row, channels)])


def assemble_own(
    scale,
    core_ref,
    mine,
    row_first,
    row_late,
    row_rest,
    parents,
    mixed,
    own_out,
    other_out,
    grad_coarse_qkv,
    grad_coarse_out,
    grad_pool,
    row_grad,
    coarse_rows,
    rows_staged,
    first_staged,
    pool_staged,
    qkv_staged,
    out_staged,
    arrived,
):
    copies = Copies(arrived)
    first_staged[...] = bround(row_first[...] + row_late[...].astype(jnp.float32))
    copies.start(first_staged, row_grad.at[:, :LANES])
    copies.start(row_rest, row_grad.at[:, LANES:])
    part, width = out_staged.shape
    panels = width // LANES
    unpack_pool(
        copies, mine, 4 * part * panels, core_ref[0], pool_staged, grad_pool, scale
    )

    def coarse(start):
        return mine[start : start + part].astype(jnp.float32) * scale

    first = 3 * part * panels
    for which in range(3):
        for panel in range(panels):
            lanes = slice(panel * LANES, (panel + 1) * LANES)
            qkv_staged[which, :, lanes] = coarse((3 * panel + which) * part)
        copies.start(qkv_staged.at[which], grad_coarse_qkv.at[which])
    for panel in range(panels):
        out_staged[:, panel * LANES : (panel + 1) * LANES] = coarse(first + panel * part)
    copies.start(out_staged, grad_coarse_out)
    summed = tn(mixed[0], own_out[...]) + tn(mixed[1], other_out[...])
    rows_staged[...] = bround(parents[...].astype(jnp.float32) + summed)
    copies.start(rows_staged, coarse_rows)
    copies.finish()


def assemble_other(
    fine_scale,
    coarse_scale,
    base,
    core_ref,
    pool_in,
    mine,
    other,
    grad_pool,
    grad_qkv,
    grad_out,
    pool_staged,
    qkv_staged,
    out_staged,
    arrived,
):
    copies = Copies(arrived)
    core = core_ref[0]
    channels = out_staged.shape[0]
    edge = channels % LANES
    skip = pool_staged.shape[0] * pool_staged.shape[1] // LANES
    fine = []
    for half in range(2):
        for i in range(3):
            at = skip + i * channels
            near = mine[base + at : base + at + channels].astype(jnp.float32)
            far = other[at : at + channels].astype(jnp.float32)
            fine.append(jnp.where(core == half, near, far) * fine_scale)
    for i in range(4):
        qkv_staged[:, i * LANES : (i + 1) * LANES] = fine[i]
    qkv_staged[:, 4 * LANES :] = fine[4][:, :edge]
    copies.start(qkv_staged, grad_qkv)
    out_staged[:, :LANES] = fine[5]
    out_staged[:, LANES:] = fine[4][:, edge:]
    copies.start(out_staged, grad_out)
    unpack_pool(copies, other, 0, 1 - core, pool_staged, grad_pool, coarse_scale)
    copies.finish()


def call(
    kernel,
    outs,
    scratch,
    *operands,
    scalars=1,
    micros=1,
    hbm=0,
    copies=0,
    staged=(),
    to_hbm=False,
    aliases=None,
):
    spaces = [pltpu.SMEM] * scalars + [pltpu.HBM] * hbm
    spaces += [pltpu.VMEM] * (len(operands) - len(spaces))
    out_spaces = [pltpu.HBM if to_hbm else pltpu.VMEM] * len(outs)
    return pl.pallas_call(
        kernel,
        out_shape=[jax.ShapeDtypeStruct(shape, dtype) for shape, dtype in outs],
        in_specs=[pl.BlockSpec(memory_space=space) for space in spaces],
        out_specs=[pl.BlockSpec(memory_space=space) for space in out_spaces],
        input_output_aliases=aliases or {},
        scratch_shapes=[pltpu.VMEM(shape, jnp.bfloat16) for shape in scratch]
        + [pltpu.VMEM(shape, jnp.float32) for shape in staged]
        + ([pltpu.SemaphoreType.DMA((copies,))] if copies else []),
        compiler_params=pltpu.CompilerParams(vmem_limit_bytes=VMEM_BYTES),
        cost_estimate=pl.CostEstimate(
            flops=int(micros * 10**9), bytes_accessed=int(micros * 10**6), transcendentals=0
        ),
    )(*operands)


def float_sum(stacked):
    return bround(jnp.sum(stacked.astype(jnp.float32), 0))


def sum_over_chips(parts, rows_after):
    slab = float_sum(lax.all_to_all(parts, NEAR, 0, 0, tiled=True))
    copies = jnp.broadcast_to(slab, (lax.axis_size("zh"),) + slab.shape)
    slab = float_sum(lax.all_to_all(copies, "zh", 0, 0, tiled=True))
    slab, *row_parts = rows_after(slab)
    copies = jnp.broadcast_to(slab, parts.shape)
    total = lax.all_to_all(copies, NEAR, 0, 0, tiled=True)
    return lax.optimization_barrier((total, *row_parts))


def on_device(
    fine_rows,
    qkv_weight,
    out_weight,
    pool_weight,
    coarse_qkv_weight,
    coarse_out_weight,
    parent_index,
    child_slot,
    out_grad,
):
    bf16, f32 = jnp.bfloat16, jnp.float32
    devices = 1
    for name in AXES:
        devices *= lax.axis_size(name)
    row_count, channels = fine_rows.shape
    owned, width = out_grad.shape
    part = coarse_out_weight.shape[0]
    blocks = row_count // LANES
    heads = channels // HD
    coarse_heads = part // HD
    coarse_count = 4 * part * width // LANES
    pool_count = SLOTS // 2 * channels * width // LANES
    fine_count = 2 * channels * channels // LANES
    core = lax.axis_index("sub").astype(jnp.int32).reshape(1)
    first_parent = (lax.axis_index(AXES) * owned).astype(jnp.int32).reshape(1)
    rows = fine_rows.T
    parent_row = parent_index.reshape(1, row_count)
    slot_row = child_slot.reshape(1, row_count)
    own_qkv = coarse_qkv_weight.transpose(0, 2, 1).reshape(3 * part, width)
    other_qkv = swap_cores(own_qkv)
    other_out = swap_cores(coarse_out_weight)
    wide_rows = heads * LANES

    def in_hbm(*arrays):
        return [pltpu.with_memory_space_constraint(array, pltpu.HBM) for array in arrays]

    def like(*arrays):
        return [(array.shape, array.dtype) for array in arrays]

    def block_outs(count):
        return [
            ((channels, count * LANES), bf16),
            ((channels, count * LANES), bf16),
            ((3 * channels, count * LANES), bf16),
            ((count, LANES, wide_rows), bf16),
            ((count * heads, LANES), f32),
        ]

    sources = (rows, qkv_weight, out_weight, parent_row, slot_row)
    *brought, packed = call(
        bring,
        like(*sources) + [((channels + SPILL, LANES), bf16)],
        [],
        first_parent,
        *in_hbm(*sources),
        hbm=5,
        copies=5,
        micros=1,
    )
    rows, fine_qkv, fine_out, parent_row, slot_row = brought
    packed = passed_along(packed, -1)
    sources = (pool_weight, own_qkv, coarse_out_weight, out_grad)
    second = call(
        fine_forward,
        like(*sources) + block_outs(blocks),
        [(2, channels + SPILL, wide_rows)],
        *in_hbm(*sources),
        rows,
        fine_qkv,
        fine_out,
        scalars=0,
        hbm=4,
        copies=4,
        micros=4,
    )
    pool_weight, own_qkv, own_out, out_grad = second[:4]
    hidden, mixed_fine, qkv, exponents, inverses = second[4:]
    children, upward, partial = call(
        pool,
        [((SLOTS, channels, owned), bf16), ((2, part, owned), bf16), ((owned, width), f32)],
        [],
        first_parent,
        hidden,
        parent_row,
        slot_row,
        own_out,
        other_out,
        out_grad,
        pool_weight,
        micros=2,
    )
    (
        parents,
        spill,
        next_upstream,
        grad_parents,
        grad_pooled,
        coarse_input,
        mixed,
        grads,
        next_mixed,
        next_qkv,
        next_exponents,
        next_inverses,
    ) = call(
        coarse_both,
        [
            ((owned, width), bf16),
            ((SPILL, channels), bf16),
            ((channels, LANES), bf16),
            ((owned, width), bf16),
            ((SLOTS // 2, channels, 2 * owned), bf16),
            ((owned, width), bf16),
            ((2, part, owned), bf16),
            ((2, 3 * part, owned), bf16),
        ]
        + block_outs(1)[1:],
        [
            (channels, LANES),
            (1, channels + SPILL, wide_rows),
            (2, part + SPILL, coarse_heads * LANES),
            (2, part, coarse_heads * LANES),
        ],
        packed,
        fine_qkv,
        fine_out,
        partial,
        upward,
        pool_weight,
        own_qkv,
        other_qkv,
        out_grad,
        scalars=0,
        micros=8,
    )
    keep, give = call(
        coarse_weights,
        [
            ((coarse_count + pool_count, LANES), bf16),
            ((coarse_count + pool_count, LANES), bf16),
        ],
        [(SLOTS, channels, owned)],
        core,
        grad_parents,
        children,
        spill,
        coarse_input,
        mixed,
        grads,
        out_grad,
        micros=1,
    )
    got = swap_cores(give)
    upstream, fine_grads, fine_keep, fine_give = call(
        fine_back,
        [
            ((channels, row_count + LANES), bf16),
            ((3 * channels, row_count + LANES), bf16),
            ((fine_count, LANES), bf16),
            ((fine_count, LANES), bf16),
        ],
        [(2, channels, wide_rows)],
        core,
        first_parent,
        rows,
        packed,
        grad_pooled,
        next_upstream,
        parent_row,
        slot_row,
        fine_out,
        exponents,
        inverses,
        qkv,
        mixed_fine,
        next_exponents,
        next_inverses,
        next_qkv,
        next_mixed,
        scalars=2,
        micros=6,
    )

    def rows_after(dependence):
        dependence, given = lax.optimization_barrier((dependence, upstream))
        row_first, row_rest, row_next = call(
            row_gradients,
            [
                ((channels, LANES), f32),
                ((channels, row_count - LANES), bf16),
                ((channels, LANES), bf16),
            ],
            [],
            rows,
            packed,
            fine_qkv,
            given,
            fine_grads,
            scalars=0,
            micros=4,
        )
        return dependence, row_first, row_rest, passed_along(row_next, 1)

    fine_got = swap_cores(fine_give)
    plane = lax.axis_size("zl") * lax.axis_size("y") * lax.axis_size("x")
    count = coarse_count + pool_count + fine_count
    unit = plane * 8
    padded = -(-count // unit) * unit
    (merged,) = call(
        merge, [((padded, LANES), bf16)], [], keep, got, fine_keep, fine_got, scalars=0, micros=1
    )
    total, row_first, row_rest, row_late = sum_over_chips(
        merged.reshape(plane, padded // plane, LANES), rows_after
    )
    total = total.reshape(padded, LANES)
    other = swap_cores(total[coarse_count:count])
    coarse_scale = (owned * devices) ** (-0.5)
    pool_shape = (SLOTS * channels, width)
    half_pool = (SLOTS // 2 * channels, width)
    grad_coarse_qkv, grad_coarse_out, grad_pool, row_grad, coarse_rows = call(
        functools.partial(assemble_own, coarse_scale),
        [
            ((3, part, width), f32),
            ((part, width), f32),
            (pool_shape, f32),
            ((channels, row_count), bf16),
            ((owned, width), bf16),
        ],
        [(owned, width), (channels, LANES)],
        core,
        total,
        row_first,
        row_late,
        row_rest,
        parents,
        mixed,
        own_out,
        other_out,
        copies=7 + SLOTS // 2,
        staged=[half_pool, (3, part, width), (part, width)],
        to_hbm=True,
        micros=3,
    )
    grad_pool, grad_qkv, grad_out = call(
        functools.partial(
            assemble_other, (row_count * devices) ** (-0.5), coarse_scale, coarse_count
        ),
        [(pool_shape, f32), ((channels, 3 * channels), f32), ((channels, channels), f32)],
        [],
        core,
        grad_pool,
        total,
        other,
        hbm=1,
        copies=2 + SLOTS // 2,
        staged=[half_pool, (channels, 3 * channels), (channels, channels)],
        to_hbm=True,
        aliases={1: 0},
        micros=2,
    )
    return (
        coarse_rows,
        row_grad.T,
        grad_qkv,
        grad_out,
        grad_pool,
        grad_coarse_qkv.transpose(0, 2, 1),
        grad_coarse_out,
    )


def solution(mesh):
    torus = Mesh(mesh.devices.reshape(-1, 2, 4, 4, mesh.shape["sub"]), AXES)
    in_specs = (
        P(AXES, None),
        P(),
        P(),
        P(),
        P(None, None, "sub"),
        P("sub", None),
        P(AXES),
        P(AXES),
        P(AXES, None),
    )
    out_specs = (
        P(AXES, None),
        P(AXES, None),
        P(),
        P(),
        P(),
        P(None, None, "sub"),
        P("sub", None),
    )
    return jax.shard_map(
        on_device, mesh=torus, in_specs=in_specs, out_specs=out_specs, check_vma=False
    )
```

```python
import functools

import jax
import jax.numpy as jnp
from jax import lax
from jax.experimental import pallas as pl
from jax.experimental.pallas import tpu as pltpu
from jax.sharding import Mesh, PartitionSpec as P

HD = 16
WINDOW_OCTANTS = 32
DILATION_STRIDE = 4
SLOTS = 8
LANES = 128
SPILL = 16
EPSILON = 1e-05
NEAR = ("zl", "y", "x")
AXES = ("zh",) + NEAR + ("sub",)
VMEM_BYTES = 20 * 1024 * 1024
FAR = -1e30


def passed_along(shard, by):
    count = 1
    for name in AXES:
        count *= lax.axis_size(name)
    pairs = [(i, i + by) for i in range(count) if 0 <= i + by < count]
    return lax.ppermute(shard, AXES, pairs)


def swap_cores(shard):
    return lax.ppermute(shard, "sub", [(0, 1), (1, 0)])


def bround(value):
    return value.astype(jnp.bfloat16)


def product(left, right, left_dim, right_dim):
    return lax.dot_general(
        left, right, (((left_dim,), (right_dim,)), ((), ())), preferred_element_type=jnp.float32
    )


def nn(left, right):
    return product(left, right, 1, 0)


def nt(left, right):
    return product(left, right, 1, 1)


def tn(left, right):
    return product(left, right, 0, 0)


def indicator(condition):
    return bround(jnp.where(condition, 1.0, 0.0))


def layer_norm(value, axis):
    center = value - jnp.mean(value, axis, keepdims=True)
    inverse = lax.rsqrt(jnp.mean(center * center, axis, keepdims=True) + EPSILON)
    return (center * inverse, inverse)


def layer_norm_back(normed, inverse, upstream, axis):
    return inverse * (
        upstream
        - jnp.mean(upstream, axis, keepdims=True)
        - normed * jnp.mean(upstream * normed, axis, keepdims=True)
    )


def window_rows(window_of):
    row = lax.broadcasted_iota(jnp.int32, (SPILL, LANES), 0)
    lane = lax.broadcasted_iota(jnp.int32, (SPILL, LANES), 1)
    return indicator(window_of(lane) == row)


def mask_rows(window_of, heads):
    row = lax.broadcasted_iota(jnp.int32, (SPILL, LANES), 0)
    lane = lax.broadcasted_iota(jnp.int32, (SPILL, LANES), 1)
    other = (window_of(lane) != row) & (row < LANES // WINDOW_OCTANTS)
    return jnp.concatenate([bround(jnp.where(other, FAR, 0.0))] * heads, 1)


def fine_window(at):
    return at % DILATION_STRIDE


def coarse_window(at):
    return at // WINDOW_OCTANTS


def spread(wide, rows, heads):
    for head in range(heads):
        at = slice(head * HD, (head + 1) * HD)
        wide[at, head * LANES : (head + 1) * LANES] = rows[at]


def softmax_parts(score):
    exponent = jnp.exp(score - jnp.max(score, 0, keepdims=True))
    return (bround(exponent), 1.0 / jnp.sum(exponent, 0, keepdims=True))


def attend_back(query, key, upstream, exponent, inverse, grad_prob):
    weighted = exponent.astype(jnp.float32)
    mean = inverse * jnp.sum(weighted * grad_prob, 0, keepdims=True)
    grad_score = bround(weighted * (grad_prob - mean))
    grad_value = nt(bround(upstream.astype(jnp.float32) * inverse), exponent)
    grad_query = nn(key, grad_score)
    grad_key = nt(query, grad_score)
    return (bround(grad_query), bround(grad_key), bround(grad_value))


def scaled(value):
    return value * jnp.bfloat16(HD**-0.5)


def fine_attention(qkv, wide, classes, heads, mixed, store):
    channels = heads * HD
    spread(wide, scaled(qkv[:channels]), heads)
    keys = jnp.concatenate([qkv[channels : 2 * channels], classes], 0)
    scores = tn(keys, wide[...])
    for head in range(heads):
        exponent, inverse = softmax_parts(scores[:, head * LANES : (head + 1) * LANES])
        value = qkv[2 * channels + head * HD : 2 * channels + (head + 1) * HD]
        mixed[head * HD : (head + 1) * HD] = bround(nn(value, exponent) * inverse)
        if store is not None:
            store(head, exponent, inverse)


def clear_wide(wide, heads, window_of):
    wide[...] = jnp.zeros(wide.shape, wide.dtype)
    for slot in range(wide.shape[0]):
        wide[slot, heads * HD :] = mask_rows(window_of, heads)


def fetch(pairs, arrived):
    copies = [
        pltpu.make_async_copy(source, target, arrived.at[i])
        for i, (source, target) in enumerate(pairs)
    ]
    for copy in copies:
        copy.start()
    return copies


def fine_blocks(
    rows, qkv_weight, out_weight, hidden, mixed, qkv, exponents, inverses, wide
):
    channels, count = hidden.shape
    heads = channels // HD
    clear_wide(wide, heads, fine_window)
    classes = window_rows(fine_window)
    rows_float = rows[...].astype(jnp.float32)
    normed, _ = layer_norm(rows_float, 0)
    qkv[...] = bround(tn(qkv_weight[...], bround(normed)))
    for block in range(count // LANES):
        lanes = slice(block * LANES, (block + 1) * LANES)

        def store(head, exponent, inverse):
            exponents[block, :, head * LANES : (head + 1) * LANES] = exponent
            at = block * heads + head
            inverses[at : at + 1] = inverse

        fine_attention(
            qkv[:, lanes],
            wide.at[block % wide.shape[0]],
            classes,
            heads,
            mixed.at[:, lanes],
            store,
        )
    hidden[...] = bround(rows_float + tn(out_weight[...], mixed[...]))


def bring(first_parent, *refs):
    sources, targets, packed, arrived = refs[:5], refs[5:10], refs[10], refs[11]
    copies = fetch(tuple(zip(sources, targets)), arrived)
    rows, _, _, parent_index, child_slot = targets
    for i in (0, 3, 4):
        copies[i].wait()
    channels = rows.shape[0]
    packed[:channels] = rows[:, :LANES]
    packed[channels:] = leading_slots(parent_index, child_slot, first_parent)
    copies[1].wait()
    copies[2].wait()


def fine_forward(*refs):
    sources, (rows, qkv_weight, out_weight) = refs[:4], refs[4:7]
    targets, outs, wide, arrived = refs[7:11], refs[11:16], refs[16], refs[17]
    copies = fetch(tuple(zip(sources, targets)), arrived)
    fine_blocks(rows, qkv_weight, out_weight, *outs, wide)
    for copy in copies:
        copy.wait()


def leading_slots(parent_index, child_slot, first_parent):
    slot = lax.broadcasted_iota(jnp.int32, (SPILL, LANES), 0)
    before = parent_index[:, :LANES] < first_parent[0]
    return indicator(before & (child_slot[:, :LANES] == slot))


def slot_numbers(parent_index, child_slot, first_parent, owned):
    parent = lax.broadcasted_iota(jnp.int32, (owned, parent_index.shape[1]), 0)
    mine = parent_index - first_parent[0] == parent
    return jnp.where(mine, child_slot, -1)


def pool(
    first_parent,
    hidden,
    parent_index,
    child_slot,
    own_out,
    other_out,
    out_grad,
    pool_weight,
    children,
    upward,
    partial,
):
    owned = out_grad.shape[0]
    slot_of = slot_numbers(parent_index[...], child_slot[...], first_parent, owned)
    for slot in range(0, SLOTS, 2):
        both = jnp.concatenate([indicator(slot_of == slot), indicator(slot_of == slot + 1)], 0)
        pair = bround(nt(hidden[...], both))
        children[slot] = pair[:, :owned]
        children[slot + 1] = pair[:, owned:]
    channels = hidden.shape[0]
    total = jnp.zeros(partial.shape, jnp.float32)
    for slot in range(SLOTS):
        total += tn(children[slot], pool_weight[slot * channels : (slot + 1) * channels])
    partial[...] = total
    for half, out_weight in enumerate((own_out, other_out)):
        upward[half] = bround(nt(out_weight[...], out_grad[...]))


def coarse_both(
    packed,
    fine_qkv,
    fine_out,
    partial,
    upward,
    pool_weight,
    own_qkv,
    other_qkv,
    out_grad,
    parents,
    spill,
    next_upstream,
    grad_parents,
    grad_pooled,
    coarse_input,
    mixed,
    grads,
    next_mixed,
    next_qkv,
    next_exponents,
    next_inverses,
    next_hidden,
    wide_next,
    wide_query,
    wide_grad,
):
    owned, width = out_grad.shape
    channels = fine_out.shape[0]
    fine_blocks(
        packed.at[:channels],
        fine_qkv,
        fine_out,
        next_hidden,
        next_mixed,
        next_qkv,
        next_exponents,
        next_inverses,
        wide_next,
    )
    leading = packed[channels:]
    spill[...] = bround(nt(leading, next_hidden[...]))
    part = upward.shape[1]
    heads = part // HD
    halves = range(2)
    qkv_weights = (own_qkv, other_qkv)
    for wide in (wide_query, wide_grad):
        wide[...] = jnp.zeros(wide.shape, wide.dtype)
    for half in halves:
        wide_query[half, part:] = mask_rows(coarse_window, heads)
    spill_row = lax.broadcasted_iota(jnp.int32, (SPILL, channels), 0)
    late = jnp.zeros((SPILL, width), jnp.float32)
    for slot in range(SLOTS):
        chosen = jnp.where(spill_row == slot, spill[...], jnp.zeros_like(spill))
        late += nn(chosen, pool_weight[slot * channels : (slot + 1) * channels])
    late = jnp.sum(late, 0, keepdims=True)
    at_last = lax.broadcasted_iota(jnp.int32, (owned, width), 0) == owned - 1
    parents[...] = bround(partial[...] + jnp.where(at_last, late, 0.0))
    normed, inverse = layer_norm(parents[...].astype(jnp.float32), 1)
    coarse_input[...] = bround(normed)
    upstream = out_grad[...]
    classes = window_rows(coarse_window)
    qkvs = [bround(nt(qkv_weights[half][...], coarse_input[...])) for half in halves]
    for half in halves:
        spread(wide_query.at[half], scaled(qkvs[half][:part]), heads)
    scores = [
        tn(jnp.concatenate([qkvs[half][part : 2 * part], classes], 0), wide_query[half])
        for half in halves
    ]
    parts = {}
    for half in halves:
        for head in range(heads):
            at = slice(head * HD, (head + 1) * HD)
            lanes = slice(head * LANES, (head + 1) * LANES)
            exponent, scale = softmax_parts(scores[half][:, lanes])
            parts[half, head] = (exponent, scale)
            value = qkvs[half][2 * part + head * HD : 2 * part + (head + 1) * HD]
            mixed[half, at] = bround(nn(value, exponent) * scale)
            weighted = scaled(upward[half, at]).astype(jnp.float32) * scale
            wide_grad[half, at, lanes] = bround(weighted)
    grad_probs = [tn(qkvs[half][2 * part :], wide_grad[half]) for half in halves]
    for half in halves:
        for head in range(heads):
            at = [slice(i * part + head * HD, i * part + (head + 1) * HD) for i in range(3)]
            back = attend_back(
                qkvs[half][at[0]],
                qkvs[half][at[1]],
                upward[half, at[0]],
                *parts[half, head],
                grad_probs[half][:, head * LANES : (head + 1) * LANES],
            )
            for which in range(3):
                grads[half, at[which]] = back[which]
    grad_normed = sum(tn(grads[half], qkv_weights[half][...]) for half in halves)
    upstream_total = bround(
        upstream.astype(jnp.float32) + layer_norm_back(normed, inverse, grad_normed, 1)
    )
    grad_parents[...] = upstream_total
    grad_all = bround(nt(pool_weight[...], upstream_total))
    last = lax.broadcasted_iota(jnp.int32, (SPILL, owned), 1) == owned - 1
    spill_slot = lax.broadcasted_iota(jnp.int32, (SPILL, owned), 0)
    edge_total = jnp.zeros((SPILL, channels), jnp.float32)
    for slot in range(SLOTS):
        grad_slot = grad_all[slot * channels : (slot + 1) * channels]
        grad_pooled[slot // 2, :, slot % 2 * owned : (slot % 2 + 1) * owned] = grad_slot
        edge_total += nt(indicator(last & (spill_slot == slot)), grad_slot)
    next_upstream[...] = bround(tn(bround(edge_total), leading))


def coarse_weights(
    core_ref,
    grad_parents,
    children,
    spill,
    coarse_input,
    mixed,
    grads,
    out_grad,
    keep,
    give,
    pooled,
):
    core = core_ref[0]
    width = out_grad.shape[1]
    owned, channels = out_grad.shape[0], pooled.shape[1]
    part = mixed.shape[1]
    last = lax.broadcasted_iota(jnp.int32, (SPILL, owned), 1) == owned - 1
    spill_slot = lax.broadcasted_iota(jnp.int32, (SPILL, owned), 0)
    for slot in range(0, SLOTS, 2):
        edges = [indicator(last & (spill_slot == at)) for at in (slot, slot + 1)]
        edge = bround(tn(spill[...], jnp.concatenate(edges, 1)))
        pooled[slot] = children[slot] + edge[:, :owned]
        pooled[slot + 1] = children[slot + 1] + edge[:, owned:]
    panels = width // LANES

    def store(target, start, value):
        for panel in range(panels):
            at = start + panel * value.shape[0]
            target[at : at + value.shape[0]] = bround(
                value[:, panel * LANES : (panel + 1) * LANES]
            )

    for half, target in enumerate((keep, give)):
        store(target, 0, nn(grads[half], coarse_input[...]))
        store(target, 3 * part * panels, nn(mixed[half], out_grad[...]))
    base = 4 * part * panels
    for target, first in ((keep, core), (give, 1 - core)):
        for step in range(SLOTS // 2):
            grad_pool = nn(pooled[first * (SLOTS // 2) + step], grad_parents[...])
            store(target, base + step * panels * channels, grad_pool)


def fine_back(
    core_ref,
    first_parent,
    rows,
    packed,
    grad_pooled,
    next_upstream,
    parent_index,
    child_slot,
    out_weight,
    *rest,
):
    own, beyond = rest[:4], rest[4:8]
    upstreams, grads, keep, give, wide = rest[8:]
    channels, row_count = rows.shape
    owned = grad_pooled.shape[2] // 2
    heads = channels // HD
    all_rows = jnp.concatenate([rows[...], packed[:channels]], 1)
    mixed = jnp.concatenate([own[3][...], beyond[3][...]], 1)
    normed, _ = layer_norm(all_rows.astype(jnp.float32), 0)
    slot_of = slot_numbers(parent_index[...], child_slot[...], first_parent, owned)
    upstream = jnp.zeros((channels, row_count), jnp.float32)
    for slot in range(0, SLOTS, 2):
        both = jnp.concatenate([indicator(slot_of == slot), indicator(slot_of == slot + 1)], 0)
        upstream += nn(grad_pooled[slot // 2], both)
    upstream = jnp.concatenate([bround(upstream), next_upstream[...]], 1)
    upstreams[...] = upstream
    upward = bround(nn(out_weight[...], upstream))
    wide[...] = jnp.zeros(wide.shape, wide.dtype)
    blocks = row_count // LANES
    for block in range(blocks + 1):
        exponents, inverses, qkv, _ = own if block < blocks else beyond
        within = block % blocks
        lanes = slice(block * LANES, (block + 1) * LANES)
        inner = slice(within * LANES, (within + 1) * LANES)
        grad_rows = wide.at[block % wide.shape[0]]
        scales = [
            inverses[within * heads + head : within * heads + head + 1] for head in range(heads)
        ]
        for head in range(heads):
            at = slice(head * HD, (head + 1) * HD)
            weighted = scaled(upward[at, lanes]).astype(jnp.float32) * scales[head]
            grad_rows[at, head * LANES : (head + 1) * LANES] = bround(weighted)
        grad_probs = tn(qkv[2 * channels :, inner], grad_rows[...])
        for head in range(heads):
            at = [slice(i * channels + head * HD, i * channels + (head + 1) * HD) for i in range(3)]
            out = slice(head * LANES, (head + 1) * LANES)
            back = attend_back(
                qkv[at[0], inner],
                qkv[at[1], inner],
                upward[at[0], lanes],
                exponents[within, :, out],
                scales[head],
                grad_probs[:, out],
            )
            for which in range(3):
                grads[at[which], lanes] = back[which]
    grad_qkv = bround(nt(bround(normed), grads[...]))
    grad_out = bround(nt(mixed, upstream))
    core = core_ref[0]
    whole = 3 * channels // LANES
    panels = [grad_qkv[:, i * LANES : (i + 1) * LANES] for i in range(whole)]
    panels.append(jnp.concatenate([grad_qkv[:, whole * LANES :], grad_out[:, LANES:]], 1))
    panels.append(grad_out[:, :LANES])
    half = len(panels) // 2
    for i in range(half):
        at = slice(i * channels, (i + 1) * channels)
        keep[at] = jnp.where(core == 0, panels[i], panels[half + i])
        give[at] = jnp.where(core == 0, panels[half + i], panels[i])


def row_gradients(rows, packed, qkv_weight, upstream, grads, row_first, row_rest, row_next):
    channels, row_count = rows.shape
    all_rows = jnp.concatenate([rows[...], packed[:channels]], 1)
    normed, inverse = layer_norm(all_rows.astype(jnp.float32), 0)
    grad_normed = nn(qkv_weight[...], grads[...])
    total = upstream[...].astype(jnp.float32) + layer_norm_back(normed, inverse, grad_normed, 0)
    row_first[...] = total[:, :LANES]
    row_rest[...] = bround(total[:, LANES:row_count])
    row_next[...] = bround(total[:, row_count:])


def merge(keep, got, fine_keep, fine_got, total):
    first, second = keep.shape[0], fine_keep.shape[0]
    total[:first] = keep[...] + got[...]
    total[first : first + second] = fine_keep[...] + fine_got[...]
    pad = total.shape[0] - first - second
    total[first + second :] = jnp.zeros((pad, LANES), total.dtype)


class Copies:
    def __init__(self, arrived):
        self.arrived, self.started = arrived, []

    def start(self, source, target):
        copy = pltpu.make_async_copy(source, target, self.arrived.at[len(self.started)])
        copy.start()
        self.started.append(copy)

    def finish(self):
        for copy in self.started:
            copy.wait()


def unpack_pool(copies, source, start, half, staged, target, scale):
    panels = staged.shape[1] // LANES
    channels = staged.shape[0] * 2 // SLOTS
    for step in range(SLOTS // 2):
        rows = slice(step * channels, (step + 1) * channels)
        for panel in range(panels):
            at = start + (step * panels + panel) * channels
            staged[rows, panel * LANES : (panel + 1) * LANES] = (
                source[at : at + channels].astype(jnp.float32) * scale
            )
        row = pl.multiple_of(half * staged.shape[0] + step * channels, 8)
        copies.start(staged.at[rows], target.at[pl.ds(row, channels)])


def assemble_own(
    scale,
    core_ref,
    mine,
    row_first,
    row_late,
    row_rest,
    parents,
    mixed,
    own_out,
    other_out,
    grad_coarse_qkv,
    grad_coarse_out,
    grad_pool,
    row_grad,
    coarse_rows,
    rows_staged,
    first_staged,
    pool_staged,
    qkv_staged,
    out_staged,
    arrived,
):
    copies = Copies(arrived)
    first_staged[...] = bround(row_first[...] + row_late[...].astype(jnp.float32))
    copies.start(first_staged, row_grad.at[:, :LANES])
    copies.start(row_rest, row_grad.at[:, LANES:])
    part, width = out_staged.shape
    panels = width // LANES
    unpack_pool(
        copies, mine, 4 * part * panels, core_ref[0], pool_staged, grad_pool, scale
    )

    def coarse(start):
        return mine[start : start + part].astype(jnp.float32) * scale

    first = 3 * part * panels
    for which in range(3):
        for panel in range(panels):
            lanes = slice(panel * LANES, (panel + 1) * LANES)
            qkv_staged[which, :, lanes] = coarse((3 * panel + which) * part)
        copies.start(qkv_staged.at[which], grad_coarse_qkv.at[which])
    for panel in range(panels):
        out_staged[:, panel * LANES : (panel + 1) * LANES] = coarse(first + panel * part)
    copies.start(out_staged, grad_coarse_out)
    summed = tn(mixed[0], own_out[...]) + tn(mixed[1], other_out[...])
    rows_staged[...] = bround(parents[...].astype(jnp.float32) + summed)
    copies.start(rows_staged, coarse_rows)
    copies.finish()


def assemble_other(
    fine_scale,
    coarse_scale,
    base,
    core_ref,
    pool_in,
    mine,
    other,
    grad_pool,
    grad_qkv,
    grad_out,
    pool_staged,
    qkv_staged,
    out_staged,
    arrived,
):
    copies = Copies(arrived)
    core = core_ref[0]
    channels = out_staged.shape[0]
    edge = channels % LANES
    skip = pool_staged.shape[0] * pool_staged.shape[1] // LANES
    fine = []
    for half in range(2):
        for i in range(3):
            at = skip + i * channels
            near = mine[base + at : base + at + channels].astype(jnp.float32)
            far = other[at : at + channels].astype(jnp.float32)
            fine.append(jnp.where(core == half, near, far) * fine_scale)
    for i in range(4):
        qkv_staged[:, i * LANES : (i + 1) * LANES] = fine[i]
    qkv_staged[:, 4 * LANES :] = fine[4][:, :edge]
    copies.start(qkv_staged, grad_qkv)
    out_staged[:, :LANES] = fine[5]
    out_staged[:, LANES:] = fine[4][:, edge:]
    copies.start(out_staged, grad_out)
    unpack_pool(copies, other, 0, 1 - core, pool_staged, grad_pool, coarse_scale)
    copies.finish()


def call(
    kernel,
    outs,
    scratch,
    *operands,
    scalars=1,
    micros=1,
    hbm=0,
    copies=0,
    staged=(),
    to_hbm=False,
    aliases=None,
):
    spaces = [pltpu.SMEM] * scalars + [pltpu.HBM] * hbm
    spaces += [pltpu.VMEM] * (len(operands) - len(spaces))
    out_spaces = [pltpu.HBM if to_hbm else pltpu.VMEM] * len(outs)
    return pl.pallas_call(
        kernel,
        out_shape=[jax.ShapeDtypeStruct(shape, dtype) for shape, dtype in outs],
        in_specs=[pl.BlockSpec(memory_space=space) for space in spaces],
        out_specs=[pl.BlockSpec(memory_space=space) for space in out_spaces],
        input_output_aliases=aliases or {},
        scratch_shapes=[pltpu.VMEM(shape, jnp.bfloat16) for shape in scratch]
        + [pltpu.VMEM(shape, jnp.float32) for shape in staged]
        + ([pltpu.SemaphoreType.DMA((copies,))] if copies else []),
        compiler_params=pltpu.CompilerParams(vmem_limit_bytes=VMEM_BYTES),
        cost_estimate=pl.CostEstimate(
            flops=int(micros * 10**9), bytes_accessed=int(micros * 10**6), transcendentals=0
        ),
    )(*operands)


def float_sum(stacked):
    return bround(jnp.sum(stacked.astype(jnp.float32), 0))


def sum_over_chips(parts, rows_after):
    slab = float_sum(lax.all_to_all(parts, NEAR, 0, 0, tiled=True))
    copies = jnp.broadcast_to(slab, (lax.axis_size("zh"),) + slab.shape)
    slab = float_sum(lax.all_to_all(copies, "zh", 0, 0, tiled=True))
    slab, *row_parts = rows_after(slab)
    copies = jnp.broadcast_to(slab, parts.shape)
    total = lax.all_to_all(copies, NEAR, 0, 0, tiled=True)
    return lax.optimization_barrier((total, *row_parts))


def on_device(
    fine_rows,
    qkv_weight,
    out_weight,
    pool_weight,
    coarse_qkv_weight,
    coarse_out_weight,
    parent_index,
    child_slot,
    out_grad,
):
    bf16, f32 = jnp.bfloat16, jnp.float32
    devices = 1
    for name in AXES:
        devices *= lax.axis_size(name)
    row_count, channels = fine_rows.shape
    owned, width = out_grad.shape
    part = coarse_out_weight.shape[0]
    blocks = row_count // LANES
    heads = channels // HD
    coarse_heads = part // HD
    coarse_count = 4 * part * width // LANES
    pool_count = SLOTS // 2 * channels * width // LANES
    fine_count = 2 * channels * channels // LANES
    core = lax.axis_index("sub").astype(jnp.int32).reshape(1)
    first_parent = (lax.axis_index(AXES) * owned).astype(jnp.int32).reshape(1)
    rows = fine_rows.T
    parent_row = parent_index.reshape(1, row_count)
    slot_row = child_slot.reshape(1, row_count)
    own_qkv = coarse_qkv_weight.transpose(0, 2, 1).reshape(3 * part, width)
    wide_rows = heads * LANES

    def in_hbm(*arrays):
        return [pltpu.with_memory_space_constraint(array, pltpu.HBM) for array in arrays]

    def like(*arrays):
        return [(array.shape, array.dtype) for array in arrays]

    def block_outs(count):
        return [
            ((channels, count * LANES), bf16),
            ((channels, count * LANES), bf16),
            ((3 * channels, count * LANES), bf16),
            ((count, LANES, wide_rows), bf16),
            ((count * heads, LANES), f32),
        ]

    sources = (rows, qkv_weight, out_weight, parent_row, slot_row)
    *brought, packed = call(
        bring,
        like(*sources) + [((channels + SPILL, LANES), bf16)],
        [],
        first_parent,
        *in_hbm(*sources),
        hbm=5,
        copies=5,
        micros=1,
    )
    rows, fine_qkv, fine_out, parent_row, slot_row = brought
    packed, give_qkv, give_out = lax.optimization_barrier((packed, own_qkv, coarse_out_weight))
    packed = passed_along(packed, -1)
    other_qkv = swap_cores(give_qkv)
    other_out = swap_cores(give_out)
    sources = (pool_weight, own_qkv, coarse_out_weight, out_grad)
    second = call(
        fine_forward,
        like(*sources) + block_outs(blocks),
        [(2, channels + SPILL, wide_rows)],
        *in_hbm(*sources),
        rows,
        fine_qkv,
        fine_out,
        scalars=0,
        hbm=4,
        copies=4,
        micros=4,
    )
    pool_weight, own_qkv, own_out, out_grad = second[:4]
    hidden, mixed_fine, qkv, exponents, inverses = second[4:]
    children, upward, partial = call(
        pool,
        [((SLOTS, channels, owned), bf16), ((2, part, owned), bf16), ((owned, width), f32)],
        [],
        first_parent,
        hidden,
        parent_row,
        slot_row,
        own_out,
        other_out,
        out_grad,
        pool_weight,
        micros=2,
    )
    (
        parents,
        spill,
        next_upstream,
        grad_parents,
        grad_pooled,
        coarse_input,
        mixed,
        grads,
        next_mixed,
        next_qkv,
        next_exponents,
        next_inverses,
    ) = call(
        coarse_both,
        [
            ((owned, width), bf16),
            ((SPILL, channels), bf16),
            ((channels, LANES), bf16),
            ((owned, width), bf16),
            ((SLOTS // 2, channels, 2 * owned), bf16),
            ((owned, width), bf16),
            ((2, part, owned), bf16),
            ((2, 3 * part, owned), bf16),
        ]
        + block_outs(1)[1:],
        [
            (channels, LANES),
            (1, channels + SPILL, wide_rows),
            (2, part + SPILL, coarse_heads * LANES),
            (2, part, coarse_heads * LANES),
        ],
        packed,
        fine_qkv,
        fine_out,
        partial,
        upward,
        pool_weight,
        own_qkv,
        other_qkv,
        out_grad,
        scalars=0,
        micros=8,
    )
    keep, give = call(
        coarse_weights,
        [
            ((coarse_count + pool_count, LANES), bf16),
            ((coarse_count + pool_count, LANES), bf16),
        ],
        [(SLOTS, channels, owned)],
        core,
        grad_parents,
        children,
        spill,
        coarse_input,
        mixed,
        grads,
        out_grad,
        micros=1,
    )
    got = swap_cores(give)
    upstream, fine_grads, fine_keep, fine_give = call(
        fine_back,
        [
            ((channels, row_count + LANES), bf16),
            ((3 * channels, row_count + LANES), bf16),
            ((fine_count, LANES), bf16),
            ((fine_count, LANES), bf16),
        ],
        [(2, channels, wide_rows)],
        core,
        first_parent,
        rows,
        packed,
        grad_pooled,
        next_upstream,
        parent_row,
        slot_row,
        fine_out,
        exponents,
        inverses,
        qkv,
        mixed_fine,
        next_exponents,
        next_inverses,
        next_qkv,
        next_mixed,
        scalars=2,
        micros=6,
    )

    def rows_after(dependence):
        dependence, given = lax.optimization_barrier((dependence, upstream))
        row_first, row_rest, row_next = call(
            row_gradients,
            [
                ((channels, LANES), f32),
                ((channels, row_count - LANES), bf16),
                ((channels, LANES), bf16),
            ],
            [],
            rows,
            packed,
            fine_qkv,
            given,
            fine_grads,
            scalars=0,
            micros=4,
        )
        return dependence, row_first, row_rest, passed_along(row_next, 1)

    fine_got = swap_cores(fine_give)
    plane = lax.axis_size("zl") * lax.axis_size("y") * lax.axis_size("x")
    count = coarse_count + pool_count + fine_count
    unit = plane * 8
    padded = -(-count // unit) * unit
    (merged,) = call(
        merge, [((padded, LANES), bf16)], [], keep, got, fine_keep, fine_got, scalars=0, micros=1
    )
    total, row_first, row_rest, row_late = sum_over_chips(
        merged.reshape(plane, padded // plane, LANES), rows_after
    )
    total = total.reshape(padded, LANES)
    other = swap_cores(total[coarse_count:count])
    coarse_scale = (owned * devices) ** (-0.5)
    pool_shape = (SLOTS * channels, width)
    half_pool = (SLOTS // 2 * channels, width)
    grad_coarse_qkv, grad_coarse_out, grad_pool, row_grad, coarse_rows = call(
        functools.partial(assemble_own, coarse_scale),
        [
            ((3, part, width), f32),
            ((part, width), f32),
            (pool_shape, f32),
            ((channels, row_count), bf16),
            ((owned, width), bf16),
        ],
        [(owned, width), (channels, LANES)],
        core,
        total,
        row_first,
        row_late,
        row_rest,
        parents,
        mixed,
        own_out,
        other_out,
        copies=7 + SLOTS // 2,
        staged=[half_pool, (3, part, width), (part, width)],
        to_hbm=True,
        micros=3,
    )
    grad_pool, grad_qkv, grad_out = call(
        functools.partial(
            assemble_other, (row_count * devices) ** (-0.5), coarse_scale, coarse_count
        ),
        [(pool_shape, f32), ((channels, 3 * channels), f32), ((channels, channels), f32)],
        [],
        core,
        grad_pool,
        total,
        other,
        hbm=1,
        copies=2 + SLOTS // 2,
        staged=[half_pool, (channels, 3 * channels), (channels, channels)],
        to_hbm=True,
        aliases={1: 0},
        micros=2,
    )
    return (
        coarse_rows,
        row_grad.T,
        grad_qkv,
        grad_out,
        grad_pool,
        grad_coarse_qkv.transpose(0, 2, 1),
        grad_coarse_out,
    )


def solution(mesh):
    torus = Mesh(mesh.devices.reshape(-1, 2, 4, 4, mesh.shape["sub"]), AXES)
    in_specs = (
        P(AXES, None),
        P(),
        P(),
        P(),
        P(None, None, "sub"),
        P("sub", None),
        P(AXES),
        P(AXES),
        P(AXES, None),
    )
    out_specs = (
        P(AXES, None),
        P(AXES, None),
        P(),
        P(),
        P(),
        P(None, None, "sub"),
        P("sub", None),
    )
    return jax.shard_map(
        on_device, mesh=torus, in_specs=in_specs, out_specs=out_specs, check_vma=False
    )
```

```python
import functools

import jax
import jax.numpy as jnp
from jax import lax
from jax.experimental import pallas as pl
from jax.experimental.pallas import tpu as pltpu
from jax.sharding import Mesh, PartitionSpec as P

HD = 16
WINDOW_OCTANTS = 32
DILATION_STRIDE = 4
SLOTS = 8
LANES = 128
SPILL = 16
EPSILON = 1e-05
NEAR = ("zl", "y", "x")
AXES = ("zh",) + NEAR + ("sub",)
VMEM_BYTES = 20 * 1024 * 1024
FAR = -1e30


def passed_along(shard, by):
    count = 1
    for name in AXES:
        count *= lax.axis_size(name)
    pairs = [(i, i + by) for i in range(count) if 0 <= i + by < count]
    return lax.ppermute(shard, AXES, pairs)


def swap_cores(shard):
    return lax.ppermute(shard, "sub", [(0, 1), (1, 0)])


def bround(value):
    return value.astype(jnp.bfloat16)


def product(left, right, left_dim, right_dim):
    return lax.dot_general(
        left, right, (((left_dim,), (right_dim,)), ((), ())), preferred_element_type=jnp.float32
    )


def nn(left, right):
    return product(left, right, 1, 0)


def nt(left, right):
    return product(left, right, 1, 1)


def tn(left, right):
    return product(left, right, 0, 0)


def indicator(condition):
    return bround(jnp.where(condition, 1.0, 0.0))


def layer_norm(value, axis):
    center = value - jnp.mean(value, axis, keepdims=True)
    inverse = lax.rsqrt(jnp.mean(center * center, axis, keepdims=True) + EPSILON)
    return (center * inverse, inverse)


def layer_norm_back(normed, inverse, upstream, axis):
    return inverse * (
        upstream
        - jnp.mean(upstream, axis, keepdims=True)
        - normed * jnp.mean(upstream * normed, axis, keepdims=True)
    )


def window_rows(window_of):
    row = lax.broadcasted_iota(jnp.int32, (SPILL, LANES), 0)
    lane = lax.broadcasted_iota(jnp.int32, (SPILL, LANES), 1)
    return indicator(window_of(lane) == row)


def mask_rows(window_of, heads):
    row = lax.broadcasted_iota(jnp.int32, (SPILL, LANES), 0)
    lane = lax.broadcasted_iota(jnp.int32, (SPILL, LANES), 1)
    other = (window_of(lane) != row) & (row < LANES // WINDOW_OCTANTS)
    return jnp.concatenate([bround(jnp.where(other, FAR, 0.0))] * heads, 1)


def fine_window(at):
    return at % DILATION_STRIDE


def coarse_window(at):
    return at // WINDOW_OCTANTS


def spread(wide, rows, heads):
    for head in range(heads):
        at = slice(head * HD, (head + 1) * HD)
        wide[at, head * LANES : (head + 1) * LANES] = rows[at]


def softmax_parts(score):
    exponent = jnp.exp(score - jnp.max(score, 0, keepdims=True))
    return (bround(exponent), 1.0 / jnp.sum(exponent, 0, keepdims=True))


def diagonal(product):
    return jnp.concatenate([product[:HD, :LANES], product[HD:, LANES:]], 0)


def mix_pair(values, parts):
    exponents = jnp.concatenate([exponent for exponent, _ in parts], 1)
    scales = [jnp.broadcast_to(inverse, (HD, LANES)) for _, inverse in parts]
    return bround(diagonal(nn(values, exponents)) * jnp.concatenate(scales, 0))


def attend_back(query, key, upstream, parts, grad_probs):
    scores, scales = [], []
    for i, (exponent, inverse) in enumerate(parts):
        grad_prob = grad_probs[:, i * LANES : (i + 1) * LANES]
        weighted = exponent.astype(jnp.float32)
        mean = inverse * jnp.sum(weighted * grad_prob, 0, keepdims=True)
        scores.append(bround(weighted * (grad_prob - mean)))
        scales.append(jnp.broadcast_to(inverse, (HD, LANES)))
    spread_up = bround(upstream.astype(jnp.float32) * jnp.concatenate(scales, 0))
    grad_value = nt(spread_up, jnp.concatenate([exponent for exponent, _ in parts], 0))
    grad_query = nn(key, jnp.concatenate(scores, 1))
    grad_key = nt(query, jnp.concatenate(scores, 0))
    return tuple(bround(diagonal(grad)) for grad in (grad_query, grad_key, grad_value))


def scaled(value):
    return value * jnp.bfloat16(HD**-0.5)


def fine_attention(qkv, wide, classes, heads, mixed, store):
    channels = heads * HD
    spread(wide, scaled(qkv[:channels]), heads)
    keys = jnp.concatenate([qkv[channels : 2 * channels], classes], 0)
    scores = tn(keys, wide[...])
    for head in range(0, heads, 2):
        parts = [
            softmax_parts(scores[:, at * LANES : (at + 1) * LANES]) for at in (head, head + 1)
        ]
        values = qkv[2 * channels + head * HD : 2 * channels + (head + 2) * HD]
        mixed[head * HD : (head + 2) * HD] = mix_pair(values, parts)
        for i in range(2):
            store(head + i, *parts[i])


def clear_wide(wide, heads, window_of):
    wide[...] = jnp.zeros(wide.shape, wide.dtype)
    for slot in range(wide.shape[0]):
        wide[slot, heads * HD :] = mask_rows(window_of, heads)


def fetch(pairs, arrived):
    copies = [
        pltpu.make_async_copy(source, target, arrived.at[i])
        for i, (source, target) in enumerate(pairs)
    ]
    for copy in copies:
        copy.start()
    return copies


def fine_blocks(
    rows, qkv_weight, out_weight, hidden, mixed, qkv, exponents, inverses, wide
):
    channels, count = hidden.shape
    heads = channels // HD
    clear_wide(wide, heads, fine_window)
    classes = window_rows(fine_window)
    rows_float = rows[...].astype(jnp.float32)
    normed, _ = layer_norm(rows_float, 0)
    qkv[...] = bround(tn(qkv_weight[...], bround(normed)))
    for block in range(count // LANES):
        lanes = slice(block * LANES, (block + 1) * LANES)

        def store(head, exponent, inverse):
            exponents[block, :, head * LANES : (head + 1) * LANES] = exponent
            at = block * heads + head
            inverses[at : at + 1] = inverse

        fine_attention(
            qkv[:, lanes],
            wide.at[block % wide.shape[0]],
            classes,
            heads,
            mixed.at[:, lanes],
            store,
        )
    hidden[...] = bround(rows_float + tn(out_weight[...], mixed[...]))


def bring(first_parent, *refs):
    sources, targets, packed, arrived = refs[:5], refs[5:10], refs[10], refs[11]
    copies = fetch(tuple(zip(sources, targets)), arrived)
    rows, _, _, parent_index, child_slot = targets
    for i in (0, 3, 4):
        copies[i].wait()
    channels = rows.shape[0]
    packed[:channels] = rows[:, :LANES]
    packed[channels:] = leading_slots(parent_index, child_slot, first_parent)
    copies[1].wait()
    copies[2].wait()


def fine_forward(*refs):
    sources, (rows, qkv_weight, out_weight) = refs[:4], refs[4:7]
    targets, outs, wide, arrived = refs[7:11], refs[11:16], refs[16], refs[17]
    copies = fetch(tuple(zip(sources, targets)), arrived)
    fine_blocks(rows, qkv_weight, out_weight, *outs, wide)
    for copy in copies:
        copy.wait()


def leading_slots(parent_index, child_slot, first_parent):
    slot = lax.broadcasted_iota(jnp.int32, (SPILL, LANES), 0)
    before = parent_index[:, :LANES] < first_parent[0]
    return indicator(before & (child_slot[:, :LANES] == slot))


def slot_numbers(parent_index, child_slot, first_parent, owned):
    parent = lax.broadcasted_iota(jnp.int32, (owned, parent_index.shape[1]), 0)
    mine = parent_index - first_parent[0] == parent
    return jnp.where(mine, child_slot, -1)


def pool(
    first_parent,
    hidden,
    parent_index,
    child_slot,
    own_out,
    other_out,
    out_grad,
    pool_weight,
    children,
    upward,
    partial,
):
    owned = out_grad.shape[0]
    slot_of = slot_numbers(parent_index[...], child_slot[...], first_parent, owned)
    for slot in range(0, SLOTS, 2):
        both = jnp.concatenate([indicator(slot_of == slot), indicator(slot_of == slot + 1)], 0)
        pair = bround(nt(hidden[...], both))
        children[slot] = pair[:, :owned]
        children[slot + 1] = pair[:, owned:]
    channels = hidden.shape[0]
    total = jnp.zeros(partial.shape, jnp.float32)
    for slot in range(SLOTS):
        total += tn(children[slot], pool_weight[slot * channels : (slot + 1) * channels])
    partial[...] = total
    for half, out_weight in enumerate((own_out, other_out)):
        upward[half] = bround(nt(out_weight[...], out_grad[...]))


def coarse_both(
    packed,
    fine_qkv,
    fine_out,
    partial,
    upward,
    pool_weight,
    own_qkv,
    other_qkv,
    out_grad,
    parents,
    spill,
    next_upstream,
    grad_parents,
    grad_pooled,
    coarse_input,
    mixed,
    grads,
    next_mixed,
    next_qkv,
    next_exponents,
    next_inverses,
    next_hidden,
    wide_next,
    wide_query,
    wide_grad,
):
    owned, width = out_grad.shape
    channels = fine_out.shape[0]
    fine_blocks(
        packed.at[:channels],
        fine_qkv,
        fine_out,
        next_hidden,
        next_mixed,
        next_qkv,
        next_exponents,
        next_inverses,
        wide_next,
    )
    leading = packed[channels:]
    spill[...] = bround(nt(leading, next_hidden[...]))
    part = upward.shape[1]
    heads = part // HD
    halves = range(2)
    qkv_weights = (own_qkv, other_qkv)
    for wide in (wide_query, wide_grad):
        wide[...] = jnp.zeros(wide.shape, wide.dtype)
    for half in halves:
        wide_query[half, part:] = mask_rows(coarse_window, heads)
    spill_row = lax.broadcasted_iota(jnp.int32, (SPILL, channels), 0)
    late = jnp.zeros((SPILL, width), jnp.float32)
    for slot in range(SLOTS):
        chosen = jnp.where(spill_row == slot, spill[...], jnp.zeros_like(spill))
        late += nn(chosen, pool_weight[slot * channels : (slot + 1) * channels])
    late = jnp.sum(late, 0, keepdims=True)
    at_last = lax.broadcasted_iota(jnp.int32, (owned, width), 0) == owned - 1
    parents[...] = bround(partial[...] + jnp.where(at_last, late, 0.0))
    normed, inverse = layer_norm(parents[...].astype(jnp.float32), 1)
    coarse_input[...] = bround(normed)
    upstream = out_grad[...]
    classes = window_rows(coarse_window)
    qkvs = [bround(nt(qkv_weights[half][...], coarse_input[...])) for half in halves]
    for half in halves:
        spread(wide_query.at[half], scaled(qkvs[half][:part]), heads)
    scores = [
        tn(jnp.concatenate([qkvs[half][part : 2 * part], classes], 0), wide_query[half])
        for half in halves
    ]
    parts = {}
    for half in halves:
        for head in range(0, heads, 2):
            at = slice(head * HD, (head + 2) * HD)
            pair = [
                softmax_parts(scores[half][:, i * LANES : (i + 1) * LANES])
                for i in (head, head + 1)
            ]
            parts[half, head] = pair
            values = qkvs[half][2 * part + head * HD : 2 * part + (head + 2) * HD]
            mixed[half, at] = mix_pair(values, pair)
            for i in range(2):
                rows = slice((head + i) * HD, (head + i + 1) * HD)
                lanes = slice((head + i) * LANES, (head + i + 1) * LANES)
                weighted = scaled(upward[half, rows]).astype(jnp.float32) * pair[i][1]
                wide_grad[half, rows, lanes] = bround(weighted)
    grad_probs = [tn(qkvs[half][2 * part :], wide_grad[half]) for half in halves]
    for half in halves:
        for head in range(0, heads, 2):
            at = [slice(i * part + head * HD, i * part + (head + 2) * HD) for i in range(3)]
            back = attend_back(
                qkvs[half][at[0]],
                qkvs[half][at[1]],
                upward[half, at[0]],
                parts[half, head],
                grad_probs[half][:, head * LANES : (head + 2) * LANES],
            )
            for which in range(3):
                grads[half, at[which]] = back[which]
    grad_normed = sum(tn(grads[half], qkv_weights[half][...]) for half in halves)
    upstream_total = bround(
        upstream.astype(jnp.float32) + layer_norm_back(normed, inverse, grad_normed, 1)
    )
    grad_parents[...] = upstream_total
    grad_all = bround(nt(pool_weight[...], upstream_total))
    last = lax.broadcasted_iota(jnp.int32, (SPILL, owned), 1) == owned - 1
    spill_slot = lax.broadcasted_iota(jnp.int32, (SPILL, owned), 0)
    edge_total = jnp.zeros((SPILL, channels), jnp.float32)
    for slot in range(SLOTS):
        grad_slot = grad_all[slot * channels : (slot + 1) * channels]
        grad_pooled[slot // 2, :, slot % 2 * owned : (slot % 2 + 1) * owned] = grad_slot
        edge_total += nt(indicator(last & (spill_slot == slot)), grad_slot)
    next_upstream[...] = bround(tn(bround(edge_total), leading))


def coarse_weights(
    core_ref,
    grad_parents,
    children,
    spill,
    coarse_input,
    mixed,
    grads,
    out_grad,
    keep,
    give,
    pooled,
):
    core = core_ref[0]
    width = out_grad.shape[1]
    owned, channels = out_grad.shape[0], pooled.shape[1]
    part = mixed.shape[1]
    last = lax.broadcasted_iota(jnp.int32, (SPILL, owned), 1) == owned - 1
    spill_slot = lax.broadcasted_iota(jnp.int32, (SPILL, owned), 0)
    for slot in range(0, SLOTS, 2):
        edges = [indicator(last & (spill_slot == at)) for at in (slot, slot + 1)]
        edge = bround(tn(spill[...], jnp.concatenate(edges, 1)))
        pooled[slot] = children[slot] + edge[:, :owned]
        pooled[slot + 1] = children[slot + 1] + edge[:, owned:]
    panels = width // LANES

    def store(target, start, value):
        for panel in range(panels):
            at = start + panel * value.shape[0]
            target[at : at + value.shape[0]] = bround(
                value[:, panel * LANES : (panel + 1) * LANES]
            )

    for half, target in enumerate((keep, give)):
        store(target, 0, nn(grads[half], coarse_input[...]))
        store(target, 3 * part * panels, nn(mixed[half], out_grad[...]))
    base = 4 * part * panels
    for target, first in ((keep, core), (give, 1 - core)):
        for step in range(SLOTS // 2):
            grad_pool = nn(pooled[first * (SLOTS // 2) + step], grad_parents[...])
            store(target, base + step * panels * channels, grad_pool)


def fine_back(
    core_ref,
    first_parent,
    rows,
    packed,
    grad_pooled,
    next_upstream,
    parent_index,
    child_slot,
    out_weight,
    *rest,
):
    own, beyond = rest[:4], rest[4:8]
    upstreams, grads, keep, give, wide = rest[8:]
    channels, row_count = rows.shape
    owned = grad_pooled.shape[2] // 2
    heads = channels // HD
    all_rows = jnp.concatenate([rows[...], packed[:channels]], 1)
    mixed = jnp.concatenate([own[3][...], beyond[3][...]], 1)
    normed, _ = layer_norm(all_rows.astype(jnp.float32), 0)
    slot_of = slot_numbers(parent_index[...], child_slot[...], first_parent, owned)
    upstream = jnp.zeros((channels, row_count), jnp.float32)
    for slot in range(0, SLOTS, 2):
        both = jnp.concatenate([indicator(slot_of == slot), indicator(slot_of == slot + 1)], 0)
        upstream += nn(grad_pooled[slot // 2], both)
    upstream = jnp.concatenate([bround(upstream), next_upstream[...]], 1)
    upstreams[...] = upstream
    upward = bround(nn(out_weight[...], upstream))
    wide[...] = jnp.zeros(wide.shape, wide.dtype)
    blocks = row_count // LANES
    for block in range(blocks + 1):
        exponents, inverses, qkv, _ = own if block < blocks else beyond
        within = block % blocks
        lanes = slice(block * LANES, (block + 1) * LANES)
        inner = slice(within * LANES, (within + 1) * LANES)
        grad_rows = wide.at[block % wide.shape[0]]
        scales = [
            inverses[within * heads + head : within * heads + head + 1] for head in range(heads)
        ]
        for head in range(heads):
            at = slice(head * HD, (head + 1) * HD)
            weighted = scaled(upward[at, lanes]).astype(jnp.float32) * scales[head]
            grad_rows[at, head * LANES : (head + 1) * LANES] = bround(weighted)
        grad_probs = tn(qkv[2 * channels :, inner], grad_rows[...])
        for head in range(0, heads, 2):
            at = [slice(i * channels + head * HD, i * channels + (head + 2) * HD) for i in range(3)]
            parts = [
                (exponents[within, :, i * LANES : (i + 1) * LANES], scales[i])
                for i in (head, head + 1)
            ]
            back = attend_back(
                qkv[at[0], inner],
                qkv[at[1], inner],
                upward[at[0], lanes],
                parts,
                grad_probs[:, head * LANES : (head + 2) * LANES],
            )
            for which in range(3):
                grads[at[which], lanes] = back[which]
    grad_qkv = bround(nt(bround(normed), grads[...]))
    grad_out = bround(nt(mixed, upstream))
    core = core_ref[0]
    whole = 3 * channels // LANES
    panels = [grad_qkv[:, i * LANES : (i + 1) * LANES] for i in range(whole)]
    panels.append(jnp.concatenate([grad_qkv[:, whole * LANES :], grad_out[:, LANES:]], 1))
    panels.append(grad_out[:, :LANES])
    half = len(panels) // 2
    for i in range(half):
        at = slice(i * channels, (i + 1) * channels)
        keep[at] = jnp.where(core == 0, panels[i], panels[half + i])
        give[at] = jnp.where(core == 0, panels[half + i], panels[i])


def row_gradients(rows, packed, qkv_weight, upstream, grads, row_first, row_rest, row_next):
    channels, row_count = rows.shape
    all_rows = jnp.concatenate([rows[...], packed[:channels]], 1)
    normed, inverse = layer_norm(all_rows.astype(jnp.float32), 0)
    grad_normed = nn(qkv_weight[...], grads[...])
    total = upstream[...].astype(jnp.float32) + layer_norm_back(normed, inverse, grad_normed, 0)
    row_first[...] = total[:, :LANES]
    row_rest[...] = bround(total[:, LANES:row_count])
    row_next[...] = bround(total[:, row_count:])


def merge(keep, got, fine_keep, fine_got, total):
    first, second = keep.shape[0], fine_keep.shape[0]
    total[:first] = keep[...] + got[...]
    total[first : first + second] = fine_keep[...] + fine_got[...]
    pad = total.shape[0] - first - second
    total[first + second :] = jnp.zeros((pad, LANES), total.dtype)


class Copies:
    def __init__(self, arrived):
        self.arrived, self.started = arrived, []

    def start(self, source, target):
        copy = pltpu.make_async_copy(source, target, self.arrived.at[len(self.started)])
        copy.start()
        self.started.append(copy)

    def finish(self):
        for copy in self.started:
            copy.wait()


def unpack_pool(copies, source, start, half, staged, target, scale):
    panels = staged.shape[1] // LANES
    channels = staged.shape[0] * 2 // SLOTS
    for step in range(SLOTS // 2):
        rows = slice(step * channels, (step + 1) * channels)
        for panel in range(panels):
            at = start + (step * panels + panel) * channels
            staged[rows, panel * LANES : (panel + 1) * LANES] = (
                source[at : at + channels].astype(jnp.float32) * scale
            )
        row = pl.multiple_of(half * staged.shape[0] + step * channels, 8)
        copies.start(staged.at[rows], target.at[pl.ds(row, channels)])


def assemble_own(
    scale,
    core_ref,
    mine,
    row_first,
    row_late,
    row_rest,
    parents,
    mixed,
    own_out,
    other_out,
    grad_coarse_qkv,
    grad_coarse_out,
    grad_pool,
    row_grad,
    coarse_rows,
    rows_staged,
    first_staged,
    pool_staged,
    qkv_staged,
    out_staged,
    arrived,
):
    copies = Copies(arrived)
    first_staged[...] = bround(row_first[...] + row_late[...].astype(jnp.float32))
    copies.start(first_staged, row_grad.at[:, :LANES])
    copies.start(row_rest, row_grad.at[:, LANES:])
    part, width = out_staged.shape
    panels = width // LANES
    unpack_pool(
        copies, mine, 4 * part * panels, core_ref[0], pool_staged, grad_pool, scale
    )

    def coarse(start):
        return mine[start : start + part].astype(jnp.float32) * scale

    first = 3 * part * panels
    for which in range(3):
        for panel in range(panels):
            lanes = slice(panel * LANES, (panel + 1) * LANES)
            qkv_staged[which, :, lanes] = coarse((3 * panel + which) * part)
        copies.start(qkv_staged.at[which], grad_coarse_qkv.at[which])
    for panel in range(panels):
        out_staged[:, panel * LANES : (panel + 1) * LANES] = coarse(first + panel * part)
    copies.start(out_staged, grad_coarse_out)
    summed = tn(mixed[0], own_out[...]) + tn(mixed[1], other_out[...])
    rows_staged[...] = bround(parents[...].astype(jnp.float32) + summed)
    copies.start(rows_staged, coarse_rows)
    copies.finish()


def assemble_other(
    fine_scale,
    coarse_scale,
    base,
    core_ref,
    pool_in,
    mine,
    other,
    grad_pool,
    grad_qkv,
    grad_out,
    pool_staged,
    qkv_staged,
    out_staged,
    arrived,
):
    copies = Copies(arrived)
    core = core_ref[0]
    channels = out_staged.shape[0]
    edge = channels % LANES
    skip = pool_staged.shape[0] * pool_staged.shape[1] // LANES
    fine = []
    for half in range(2):
        for i in range(3):
            at = skip + i * channels
            near = mine[base + at : base + at + channels].astype(jnp.float32)
            far = other[at : at + channels].astype(jnp.float32)
            fine.append(jnp.where(core == half, near, far) * fine_scale)
    for i in range(4):
        qkv_staged[:, i * LANES : (i + 1) * LANES] = fine[i]
    qkv_staged[:, 4 * LANES :] = fine[4][:, :edge]
    copies.start(qkv_staged, grad_qkv)
    out_staged[:, :LANES] = fine[5]
    out_staged[:, LANES:] = fine[4][:, edge:]
    copies.start(out_staged, grad_out)
    unpack_pool(copies, other, 0, 1 - core, pool_staged, grad_pool, coarse_scale)
    copies.finish()


def call(
    kernel,
    outs,
    scratch,
    *operands,
    scalars=1,
    micros=1,
    hbm=0,
    copies=0,
    staged=(),
    to_hbm=False,
    aliases=None,
):
    spaces = [pltpu.SMEM] * scalars + [pltpu.HBM] * hbm
    spaces += [pltpu.VMEM] * (len(operands) - len(spaces))
    out_spaces = [pltpu.HBM if to_hbm else pltpu.VMEM] * len(outs)
    return pl.pallas_call(
        kernel,
        out_shape=[jax.ShapeDtypeStruct(shape, dtype) for shape, dtype in outs],
        in_specs=[pl.BlockSpec(memory_space=space) for space in spaces],
        out_specs=[pl.BlockSpec(memory_space=space) for space in out_spaces],
        input_output_aliases=aliases or {},
        scratch_shapes=[pltpu.VMEM(shape, jnp.bfloat16) for shape in scratch]
        + [pltpu.VMEM(shape, jnp.float32) for shape in staged]
        + ([pltpu.SemaphoreType.DMA((copies,))] if copies else []),
        compiler_params=pltpu.CompilerParams(vmem_limit_bytes=VMEM_BYTES),
        cost_estimate=pl.CostEstimate(
            flops=int(micros * 10**9), bytes_accessed=int(micros * 10**6), transcendentals=0
        ),
    )(*operands)


def float_sum(stacked):
    return bround(jnp.sum(stacked.astype(jnp.float32), 0))


def sum_over_chips(parts, rows_after):
    slab = float_sum(lax.all_to_all(parts, NEAR, 0, 0, tiled=True))
    copies = jnp.broadcast_to(slab, (lax.axis_size("zh"),) + slab.shape)
    slab = float_sum(lax.all_to_all(copies, "zh", 0, 0, tiled=True))
    slab, *row_parts = rows_after(slab)
    copies = jnp.broadcast_to(slab, parts.shape)
    total = lax.all_to_all(copies, NEAR, 0, 0, tiled=True)
    return lax.optimization_barrier((total, *row_parts))


def on_device(
    fine_rows,
    qkv_weight,
    out_weight,
    pool_weight,
    coarse_qkv_weight,
    coarse_out_weight,
    parent_index,
    child_slot,
    out_grad,
):
    bf16, f32 = jnp.bfloat16, jnp.float32
    devices = 1
    for name in AXES:
        devices *= lax.axis_size(name)
    row_count, channels = fine_rows.shape
    owned, width = out_grad.shape
    part = coarse_out_weight.shape[0]
    blocks = row_count // LANES
    heads = channels // HD
    coarse_heads = part // HD
    coarse_count = 4 * part * width // LANES
    pool_count = SLOTS // 2 * channels * width // LANES
    fine_count = 2 * channels * channels // LANES
    core = lax.axis_index("sub").astype(jnp.int32).reshape(1)
    first_parent = (lax.axis_index(AXES) * owned).astype(jnp.int32).reshape(1)
    rows = fine_rows.T
    parent_row = parent_index.reshape(1, row_count)
    slot_row = child_slot.reshape(1, row_count)
    own_qkv = coarse_qkv_weight.transpose(0, 2, 1).reshape(3 * part, width)
    wide_rows = heads * LANES

    def in_hbm(*arrays):
        return [pltpu.with_memory_space_constraint(array, pltpu.HBM) for array in arrays]

    def like(*arrays):
        return [(array.shape, array.dtype) for array in arrays]

    def block_outs(count):
        return [
            ((channels, count * LANES), bf16),
            ((channels, count * LANES), bf16),
            ((3 * channels, count * LANES), bf16),
            ((count, LANES, wide_rows), bf16),
            ((count * heads, LANES), f32),
        ]

    sources = (rows, qkv_weight, out_weight, parent_row, slot_row)
    *brought, packed = call(
        bring,
        like(*sources) + [((channels + SPILL, LANES), bf16)],
        [],
        first_parent,
        *in_hbm(*sources),
        hbm=5,
        copies=5,
        micros=1,
    )
    rows, fine_qkv, fine_out, parent_row, slot_row = brought
    packed, give_qkv, give_out = lax.optimization_barrier((packed, own_qkv, coarse_out_weight))
    packed = passed_along(packed, -1)
    other_qkv = swap_cores(give_qkv)
    other_out = swap_cores(give_out)
    sources = (pool_weight, own_qkv, coarse_out_weight, out_grad)
    second = call(
        fine_forward,
        like(*sources) + block_outs(blocks),
        [(2, channels + SPILL, wide_rows)],
        *in_hbm(*sources),
        rows,
        fine_qkv,
        fine_out,
        scalars=0,
        hbm=4,
        copies=4,
        micros=4,
    )
    pool_weight, own_qkv, own_out, out_grad = second[:4]
    hidden, mixed_fine, qkv, exponents, inverses = second[4:]
    children, upward, partial = call(
        pool,
        [((SLOTS, channels, owned), bf16), ((2, part, owned), bf16), ((owned, width), f32)],
        [],
        first_parent,
        hidden,
        parent_row,
        slot_row,
        own_out,
        other_out,
        out_grad,
        pool_weight,
        micros=2,
    )
    (
        parents,
        spill,
        next_upstream,
        grad_parents,
        grad_pooled,
        coarse_input,
        mixed,
        grads,
        next_mixed,
        next_qkv,
        next_exponents,
        next_inverses,
    ) = call(
        coarse_both,
        [
            ((owned, width), bf16),
            ((SPILL, channels), bf16),
            ((channels, LANES), bf16),
            ((owned, width), bf16),
            ((SLOTS // 2, channels, 2 * owned), bf16),
            ((owned, width), bf16),
            ((2, part, owned), bf16),
            ((2, 3 * part, owned), bf16),
        ]
        + block_outs(1)[1:],
        [
            (channels, LANES),
            (1, channels + SPILL, wide_rows),
            (2, part + SPILL, coarse_heads * LANES),
            (2, part, coarse_heads * LANES),
        ],
        packed,
        fine_qkv,
        fine_out,
        partial,
        upward,
        pool_weight,
        own_qkv,
        other_qkv,
        out_grad,
        scalars=0,
        micros=8,
    )
    keep, give = call(
        coarse_weights,
        [
            ((coarse_count + pool_count, LANES), bf16),
            ((coarse_count + pool_count, LANES), bf16),
        ],
        [(SLOTS, channels, owned)],
        core,
        grad_parents,
        children,
        spill,
        coarse_input,
        mixed,
        grads,
        out_grad,
        micros=1,
    )
    got = swap_cores(give)
    upstream, fine_grads, fine_keep, fine_give = call(
        fine_back,
        [
            ((channels, row_count + LANES), bf16),
            ((3 * channels, row_count + LANES), bf16),
            ((fine_count, LANES), bf16),
            ((fine_count, LANES), bf16),
        ],
        [(2, channels, wide_rows)],
        core,
        first_parent,
        rows,
        packed,
        grad_pooled,
        next_upstream,
        parent_row,
        slot_row,
        fine_out,
        exponents,
        inverses,
        qkv,
        mixed_fine,
        next_exponents,
        next_inverses,
        next_qkv,
        next_mixed,
        scalars=2,
        micros=6,
    )

    def rows_after(dependence):
        dependence, given = lax.optimization_barrier((dependence, upstream))
        row_first, row_rest, row_next = call(
            row_gradients,
            [
                ((channels, LANES), f32),
                ((channels, row_count - LANES), bf16),
                ((channels, LANES), bf16),
            ],
            [],
            rows,
            packed,
            fine_qkv,
            given,
            fine_grads,
            scalars=0,
            micros=4,
        )
        return dependence, row_first, row_rest, passed_along(row_next, 1)

    fine_got = swap_cores(fine_give)
    plane = lax.axis_size("zl") * lax.axis_size("y") * lax.axis_size("x")
    count = coarse_count + pool_count + fine_count
    unit = plane * 8
    padded = -(-count // unit) * unit
    (merged,) = call(
        merge, [((padded, LANES), bf16)], [], keep, got, fine_keep, fine_got, scalars=0, micros=1
    )
    total, row_first, row_rest, row_late = sum_over_chips(
        merged.reshape(plane, padded // plane, LANES), rows_after
    )
    total = total.reshape(padded, LANES)
    other = swap_cores(total[coarse_count:count])
    coarse_scale = (owned * devices) ** (-0.5)
    pool_shape = (SLOTS * channels, width)
    half_pool = (SLOTS // 2 * channels, width)
    grad_coarse_qkv, grad_coarse_out, grad_pool, row_grad, coarse_rows = call(
        functools.partial(assemble_own, coarse_scale),
        [
            ((3, part, width), f32),
            ((part, width), f32),
            (pool_shape, f32),
            ((channels, row_count), bf16),
            ((owned, width), bf16),
        ],
        [(owned, width), (channels, LANES)],
        core,
        total,
        row_first,
        row_late,
        row_rest,
        parents,
        mixed,
        own_out,
        other_out,
        copies=7 + SLOTS // 2,
        staged=[half_pool, (3, part, width), (part, width)],
        to_hbm=True,
        micros=3,
    )
    grad_pool, grad_qkv, grad_out = call(
        functools.partial(
            assemble_other, (row_count * devices) ** (-0.5), coarse_scale, coarse_count
        ),
        [(pool_shape, f32), ((channels, 3 * channels), f32), ((channels, channels), f32)],
        [],
        core,
        grad_pool,
        total,
        other,
        hbm=1,
        copies=2 + SLOTS // 2,
        staged=[half_pool, (channels, 3 * channels), (channels, channels)],
        to_hbm=True,
        aliases={1: 0},
        micros=2,
    )
    return (
        coarse_rows,
        row_grad.T,
        grad_qkv,
        grad_out,
        grad_pool,
        grad_coarse_qkv.transpose(0, 2, 1),
        grad_coarse_out,
    )


def solution(mesh):
    torus = Mesh(mesh.devices.reshape(-1, 2, 4, 4, mesh.shape["sub"]), AXES)
    in_specs = (
        P(AXES, None),
        P(),
        P(),
        P(),
        P(None, None, "sub"),
        P("sub", None),
        P(AXES),
        P(AXES),
        P(AXES, None),
    )
    out_specs = (
        P(AXES, None),
        P(AXES, None),
        P(),
        P(),
        P(),
        P(None, None, "sub"),
        P("sub", None),
    )
    return jax.shard_map(
        on_device, mesh=torus, in_specs=in_specs, out_specs=out_specs, check_vma=False
    )
```

```python
import functools

import jax
import jax.numpy as jnp
from jax import lax
from jax.experimental import pallas as pl
from jax.experimental.pallas import tpu as pltpu
from jax.sharding import Mesh, PartitionSpec as P

HD = 16
WINDOW_OCTANTS = 32
DILATION_STRIDE = 4
SLOTS = 8
LANES = 128
SPILL = 16
EPSILON = 1e-05
NEAR = ("zl", "y", "x")
AXES = ("zh",) + NEAR + ("sub",)
VMEM_BYTES = 20 * 1024 * 1024
FAR = -1e30


def passed_along(shard, by):
    count = 1
    for name in AXES:
        count *= lax.axis_size(name)
    pairs = [(i, i + by) for i in range(count) if 0 <= i + by < count]
    return lax.ppermute(shard, AXES, pairs)


def swap_cores(shard):
    return lax.ppermute(shard, "sub", [(0, 1), (1, 0)])


def bround(value):
    return value.astype(jnp.bfloat16)


def product(left, right, left_dim, right_dim):
    return lax.dot_general(
        left, right, (((left_dim,), (right_dim,)), ((), ())), preferred_element_type=jnp.float32
    )


def nn(left, right):
    return product(left, right, 1, 0)


def nt(left, right):
    return product(left, right, 1, 1)


def tn(left, right):
    return product(left, right, 0, 0)


def indicator(condition):
    return bround(jnp.where(condition, 1.0, 0.0))


def layer_norm(value, axis):
    center = value - jnp.mean(value, axis, keepdims=True)
    inverse = lax.rsqrt(jnp.mean(center * center, axis, keepdims=True) + EPSILON)
    return (center * inverse, inverse)


def layer_norm_back(normed, inverse, upstream, axis):
    return inverse * (
        upstream
        - jnp.mean(upstream, axis, keepdims=True)
        - normed * jnp.mean(upstream * normed, axis, keepdims=True)
    )


def window_rows(window_of):
    row = lax.broadcasted_iota(jnp.int32, (SPILL, LANES), 0)
    lane = lax.broadcasted_iota(jnp.int32, (SPILL, LANES), 1)
    return indicator(window_of(lane) == row)


def mask_rows(window_of, heads):
    row = lax.broadcasted_iota(jnp.int32, (SPILL, LANES), 0)
    lane = lax.broadcasted_iota(jnp.int32, (SPILL, LANES), 1)
    other = (window_of(lane) != row) & (row < LANES // WINDOW_OCTANTS)
    return jnp.concatenate([bround(jnp.where(other, FAR, 0.0))] * heads, 1)


def fine_window(at):
    return at % DILATION_STRIDE


def coarse_window(at):
    return at // WINDOW_OCTANTS


def spread(wide, rows, heads):
    for head in range(heads):
        at = slice(head * HD, (head + 1) * HD)
        wide[at, head * LANES : (head + 1) * LANES] = rows[at]


def softmax_parts(score):
    exponent = jnp.exp(score - jnp.max(score, 0, keepdims=True))
    return (bround(exponent), 1.0 / jnp.sum(exponent, 0, keepdims=True))


def diagonal(product):
    return jnp.concatenate([product[:HD, :LANES], product[HD:, LANES:]], 0)


def mix_pair(values, parts):
    mixed = [
        nn(values[i * HD : (i + 1) * HD], exponent) * inverse
        for i, (exponent, inverse) in enumerate(parts)
    ]
    return bround(jnp.concatenate(mixed, 0))


def attend_back(query, key, upstream, parts, grad_probs):
    scores, scales = [], []
    for i, (exponent, inverse) in enumerate(parts):
        grad_prob = grad_probs[:, i * LANES : (i + 1) * LANES]
        weighted = exponent.astype(jnp.float32)
        mean = inverse * jnp.sum(weighted * grad_prob, 0, keepdims=True)
        scores.append(bround(weighted * (grad_prob - mean)))
        scales.append(jnp.broadcast_to(inverse, (HD, LANES)))
    spread_up = bround(upstream.astype(jnp.float32) * jnp.concatenate(scales, 0))
    grad_value = nt(spread_up, jnp.concatenate([exponent for exponent, _ in parts], 0))
    grad_query = nn(key, jnp.concatenate(scores, 1))
    grad_key = nt(query, jnp.concatenate(scores, 0))
    return tuple(bround(diagonal(grad)) for grad in (grad_query, grad_key, grad_value))


def scaled(value):
    return value * jnp.bfloat16(HD**-0.5)


def fine_attention(qkv, wide, classes, heads, mixed, store):
    channels = heads * HD
    spread(wide, scaled(qkv[:channels]), heads)
    keys = jnp.concatenate([qkv[channels : 2 * channels], classes], 0)
    scores = tn(keys, wide[...])
    for head in range(0, heads, 2):
        parts = [
            softmax_parts(scores[:, at * LANES : (at + 1) * LANES]) for at in (head, head + 1)
        ]
        values = qkv[2 * channels + head * HD : 2 * channels + (head + 2) * HD]
        mixed[head * HD : (head + 2) * HD] = mix_pair(values, parts)
        for i in range(2):
            store(head + i, *parts[i])


def clear_wide(wide, heads, window_of):
    wide[...] = jnp.zeros(wide.shape, wide.dtype)
    for slot in range(wide.shape[0]):
        wide[slot, heads * HD :] = mask_rows(window_of, heads)


def fetch(pairs, arrived):
    copies = [
        pltpu.make_async_copy(source, target, arrived.at[i])
        for i, (source, target) in enumerate(pairs)
    ]
    for copy in copies:
        copy.start()
    return copies


def fine_blocks(
    rows, qkv_weight, out_weight, hidden, mixed, qkv, exponents, inverses, wide
):
    channels, count = hidden.shape
    heads = channels // HD
    clear_wide(wide, heads, fine_window)
    classes = window_rows(fine_window)
    rows_float = rows[...].astype(jnp.float32)
    normed, _ = layer_norm(rows_float, 0)
    qkv[...] = bround(tn(qkv_weight[...], bround(normed)))
    for block in range(count // LANES):
        lanes = slice(block * LANES, (block + 1) * LANES)

        def store(head, exponent, inverse):
            exponents[block, :, head * LANES : (head + 1) * LANES] = exponent
            at = block * heads + head
            inverses[at : at + 1] = inverse

        fine_attention(
            qkv[:, lanes],
            wide.at[block % wide.shape[0]],
            classes,
            heads,
            mixed.at[:, lanes],
            store,
        )
    hidden[...] = bround(rows_float + tn(out_weight[...], mixed[...]))


def bring(first_parent, *refs):
    sources, targets, packed, arrived = refs[:5], refs[5:10], refs[10], refs[11]
    copies = fetch(tuple(zip(sources, targets)), arrived)
    rows, _, _, parent_index, child_slot = targets
    for i in (0, 3, 4):
        copies[i].wait()
    channels = rows.shape[0]
    packed[:channels] = rows[:, :LANES]
    packed[channels:] = leading_slots(parent_index, child_slot, first_parent)
    copies[1].wait()
    copies[2].wait()


def fine_forward(*refs):
    sources, (rows, qkv_weight, out_weight) = refs[:4], refs[4:7]
    targets, outs, wide, arrived = refs[7:11], refs[11:16], refs[16], refs[17]
    copies = fetch(tuple(zip(sources, targets)), arrived)
    fine_blocks(rows, qkv_weight, out_weight, *outs, wide)
    for copy in copies:
        copy.wait()


def leading_slots(parent_index, child_slot, first_parent):
    slot = lax.broadcasted_iota(jnp.int32, (SPILL, LANES), 0)
    before = parent_index[:, :LANES] < first_parent[0]
    return indicator(before & (child_slot[:, :LANES] == slot))


def slot_numbers(parent_index, child_slot, first_parent, owned):
    parent = lax.broadcasted_iota(jnp.int32, (owned, parent_index.shape[1]), 0)
    mine = parent_index - first_parent[0] == parent
    return jnp.where(mine, child_slot, -1)


def pool(
    first_parent,
    hidden,
    parent_index,
    child_slot,
    own_out,
    other_out,
    out_grad,
    pool_weight,
    children,
    upward,
    partial,
):
    owned = out_grad.shape[0]
    slot_of = slot_numbers(parent_index[...], child_slot[...], first_parent, owned)
    for slot in range(0, SLOTS, 2):
        both = jnp.concatenate([indicator(slot_of == slot), indicator(slot_of == slot + 1)], 0)
        pair = bround(nt(hidden[...], both))
        children[slot] = pair[:, :owned]
        children[slot + 1] = pair[:, owned:]
    channels = hidden.shape[0]
    total = jnp.zeros(partial.shape, jnp.float32)
    for slot in range(SLOTS):
        total += tn(children[slot], pool_weight[slot * channels : (slot + 1) * channels])
    partial[...] = total
    for half, out_weight in enumerate((own_out, other_out)):
        upward[half] = bround(nt(out_weight[...], out_grad[...]))


def coarse_both(
    packed,
    fine_qkv,
    fine_out,
    partial,
    upward,
    pool_weight,
    own_qkv,
    other_qkv,
    out_grad,
    parents,
    spill,
    next_upstream,
    grad_parents,
    grad_pooled,
    coarse_input,
    mixed,
    grads,
    next_mixed,
    next_qkv,
    next_exponents,
    next_inverses,
    next_hidden,
    wide_next,
    wide_query,
    wide_grad,
):
    owned, width = out_grad.shape
    channels = fine_out.shape[0]
    fine_blocks(
        packed.at[:channels],
        fine_qkv,
        fine_out,
        next_hidden,
        next_mixed,
        next_qkv,
        next_exponents,
        next_inverses,
        wide_next,
    )
    leading = packed[channels:]
    spill[...] = bround(nt(leading, next_hidden[...]))
    part = upward.shape[1]
    heads = part // HD
    halves = range(2)
    qkv_weights = (own_qkv, other_qkv)
    for wide in (wide_query, wide_grad):
        wide[...] = jnp.zeros(wide.shape, wide.dtype)
    for half in halves:
        wide_query[half, part:] = mask_rows(coarse_window, heads)
    spill_row = lax.broadcasted_iota(jnp.int32, (SPILL, channels), 0)
    late = jnp.zeros((SPILL, width), jnp.float32)
    for slot in range(SLOTS):
        chosen = jnp.where(spill_row == slot, spill[...], jnp.zeros_like(spill))
        late += nn(chosen, pool_weight[slot * channels : (slot + 1) * channels])
    late = jnp.sum(late, 0, keepdims=True)
    at_last = lax.broadcasted_iota(jnp.int32, (owned, width), 0) == owned - 1
    parents[...] = bround(partial[...] + jnp.where(at_last, late, 0.0))
    normed, inverse = layer_norm(parents[...].astype(jnp.float32), 1)
    coarse_input[...] = bround(normed)
    upstream = out_grad[...]
    classes = window_rows(coarse_window)
    qkvs = [bround(nt(qkv_weights[half][...], coarse_input[...])) for half in halves]
    for half in halves:
        spread(wide_query.at[half], scaled(qkvs[half][:part]), heads)
    scores = [
        tn(jnp.concatenate([qkvs[half][part : 2 * part], classes], 0), wide_query[half])
        for half in halves
    ]
    parts = {}
    for half in halves:
        for head in range(0, heads, 2):
            at = slice(head * HD, (head + 2) * HD)
            pair = [
                softmax_parts(scores[half][:, i * LANES : (i + 1) * LANES])
                for i in (head, head + 1)
            ]
            parts[half, head] = pair
            values = qkvs[half][2 * part + head * HD : 2 * part + (head + 2) * HD]
            mixed[half, at] = mix_pair(values, pair)
            for i in range(2):
                rows = slice((head + i) * HD, (head + i + 1) * HD)
                lanes = slice((head + i) * LANES, (head + i + 1) * LANES)
                weighted = scaled(upward[half, rows]).astype(jnp.float32) * pair[i][1]
                wide_grad[half, rows, lanes] = bround(weighted)
    grad_probs = [tn(qkvs[half][2 * part :], wide_grad[half]) for half in halves]
    for half in halves:
        for head in range(0, heads, 2):
            at = [slice(i * part + head * HD, i * part + (head + 2) * HD) for i in range(3)]
            back = attend_back(
                qkvs[half][at[0]],
                qkvs[half][at[1]],
                upward[half, at[0]],
                parts[half, head],
                grad_probs[half][:, head * LANES : (head + 2) * LANES],
            )
            for which in range(3):
                grads[half, at[which]] = back[which]
    grad_normed = sum(tn(grads[half], qkv_weights[half][...]) for half in halves)
    upstream_total = bround(
        upstream.astype(jnp.float32) + layer_norm_back(normed, inverse, grad_normed, 1)
    )
    grad_parents[...] = upstream_total
    grad_all = bround(nt(pool_weight[...], upstream_total))
    last = lax.broadcasted_iota(jnp.int32, (SPILL, owned), 1) == owned - 1
    spill_slot = lax.broadcasted_iota(jnp.int32, (SPILL, owned), 0)
    edge_total = jnp.zeros((SPILL, channels), jnp.float32)
    for slot in range(SLOTS):
        grad_slot = grad_all[slot * channels : (slot + 1) * channels]
        grad_pooled[slot // 2, :, slot % 2 * owned : (slot % 2 + 1) * owned] = grad_slot
        edge_total += nt(indicator(last & (spill_slot == slot)), grad_slot)
    next_upstream[...] = bround(tn(bround(edge_total), leading))


def coarse_weights(
    core_ref,
    grad_parents,
    children,
    spill,
    coarse_input,
    mixed,
    grads,
    out_grad,
    keep,
    give,
    pooled,
):
    core = core_ref[0]
    width = out_grad.shape[1]
    owned, channels = out_grad.shape[0], pooled.shape[1]
    part = mixed.shape[1]
    last = lax.broadcasted_iota(jnp.int32, (SPILL, owned), 1) == owned - 1
    spill_slot = lax.broadcasted_iota(jnp.int32, (SPILL, owned), 0)
    for slot in range(0, SLOTS, 2):
        edges = [indicator(last & (spill_slot == at)) for at in (slot, slot + 1)]
        edge = bround(tn(spill[...], jnp.concatenate(edges, 1)))
        pooled[slot] = children[slot] + edge[:, :owned]
        pooled[slot + 1] = children[slot + 1] + edge[:, owned:]
    panels = width // LANES

    def store(target, start, value):
        for panel in range(panels):
            at = start + panel * value.shape[0]
            target[at : at + value.shape[0]] = bround(
                value[:, panel * LANES : (panel + 1) * LANES]
            )

    for half, target in enumerate((keep, give)):
        store(target, 0, nn(grads[half], coarse_input[...]))
        store(target, 3 * part * panels, nn(mixed[half], out_grad[...]))
    base = 4 * part * panels
    for target, first in ((keep, core), (give, 1 - core)):
        for step in range(SLOTS // 2):
            grad_pool = nn(pooled[first * (SLOTS // 2) + step], grad_parents[...])
            store(target, base + step * panels * channels, grad_pool)


def fine_back(
    core_ref,
    first_parent,
    rows,
    packed,
    grad_pooled,
    next_upstream,
    parent_index,
    child_slot,
    out_weight,
    *rest,
):
    own, beyond = rest[:4], rest[4:8]
    upstreams, grads, keep, give, wide = rest[8:]
    channels, row_count = rows.shape
    owned = grad_pooled.shape[2] // 2
    heads = channels // HD
    all_rows = jnp.concatenate([rows[...], packed[:channels]], 1)
    mixed = jnp.concatenate([own[3][...], beyond[3][...]], 1)
    normed, _ = layer_norm(all_rows.astype(jnp.float32), 0)
    slot_of = slot_numbers(parent_index[...], child_slot[...], first_parent, owned)
    upstream = jnp.zeros((channels, row_count), jnp.float32)
    for slot in range(0, SLOTS, 2):
        both = jnp.concatenate([indicator(slot_of == slot), indicator(slot_of == slot + 1)], 0)
        upstream += nn(grad_pooled[slot // 2], both)
    upstream = jnp.concatenate([bround(upstream), next_upstream[...]], 1)
    upstreams[...] = upstream
    upward = bround(nn(out_weight[...], upstream))
    wide[...] = jnp.zeros(wide.shape, wide.dtype)
    blocks = row_count // LANES
    for block in range(blocks + 1):
        exponents, inverses, qkv, _ = own if block < blocks else beyond
        within = block % blocks
        lanes = slice(block * LANES, (block + 1) * LANES)
        inner = slice(within * LANES, (within + 1) * LANES)
        grad_rows = wide.at[block % wide.shape[0]]
        scales = [
            inverses[within * heads + head : within * heads + head + 1] for head in range(heads)
        ]
        for head in range(heads):
            at = slice(head * HD, (head + 1) * HD)
            weighted = scaled(upward[at, lanes]).astype(jnp.float32) * scales[head]
            grad_rows[at, head * LANES : (head + 1) * LANES] = bround(weighted)
        grad_probs = tn(qkv[2 * channels :, inner], grad_rows[...])
        for head in range(0, heads, 2):
            at = [slice(i * channels + head * HD, i * channels + (head + 2) * HD) for i in range(3)]
            parts = [
                (exponents[within, :, i * LANES : (i + 1) * LANES], scales[i])
                for i in (head, head + 1)
            ]
            back = attend_back(
                qkv[at[0], inner],
                qkv[at[1], inner],
                upward[at[0], lanes],
                parts,
                grad_probs[:, head * LANES : (head + 2) * LANES],
            )
            for which in range(3):
                grads[at[which], lanes] = back[which]
    grad_qkv = bround(nt(bround(normed), grads[...]))
    grad_out = bround(nt(mixed, upstream))
    core = core_ref[0]
    whole = 3 * channels // LANES
    panels = [grad_qkv[:, i * LANES : (i + 1) * LANES] for i in range(whole)]
    panels.append(jnp.concatenate([grad_qkv[:, whole * LANES :], grad_out[:, LANES:]], 1))
    panels.append(grad_out[:, :LANES])
    half = len(panels) // 2
    for i in range(half):
        at = slice(i * channels, (i + 1) * channels)
        keep[at] = jnp.where(core == 0, panels[i], panels[half + i])
        give[at] = jnp.where(core == 0, panels[half + i], panels[i])


def row_gradients(rows, packed, qkv_weight, upstream, grads, row_first, row_rest, row_next):
    channels, row_count = rows.shape
    all_rows = jnp.concatenate([rows[...], packed[:channels]], 1)
    normed, inverse = layer_norm(all_rows.astype(jnp.float32), 0)
    grad_normed = nn(qkv_weight[...], grads[...])
    total = upstream[...].astype(jnp.float32) + layer_norm_back(normed, inverse, grad_normed, 0)
    row_first[...] = total[:, :LANES]
    row_rest[...] = bround(total[:, LANES:row_count])
    row_next[...] = bround(total[:, row_count:])


def merge(keep, got, fine_keep, fine_got, total):
    first, second = keep.shape[0], fine_keep.shape[0]
    total[:first] = keep[...] + got[...]
    total[first : first + second] = fine_keep[...] + fine_got[...]
    pad = total.shape[0] - first - second
    total[first + second :] = jnp.zeros((pad, LANES), total.dtype)


class Copies:
    def __init__(self, arrived):
        self.arrived, self.started = arrived, []

    def start(self, source, target):
        copy = pltpu.make_async_copy(source, target, self.arrived.at[len(self.started)])
        copy.start()
        self.started.append(copy)

    def finish(self):
        for copy in self.started:
            copy.wait()


def unpack_pool(copies, source, start, half, staged, target, scale):
    panels = staged.shape[1] // LANES
    channels = staged.shape[0] * 2 // SLOTS
    for step in range(SLOTS // 2):
        rows = slice(step * channels, (step + 1) * channels)
        for panel in range(panels):
            at = start + (step * panels + panel) * channels
            staged[rows, panel * LANES : (panel + 1) * LANES] = (
                source[at : at + channels].astype(jnp.float32) * scale
            )
        row = pl.multiple_of(half * staged.shape[0] + step * channels, 8)
        copies.start(staged.at[rows], target.at[pl.ds(row, channels)])


def assemble_own(
    scale,
    core_ref,
    mine,
    row_first,
    row_late,
    row_rest,
    parents,
    mixed,
    own_out,
    other_out,
    grad_coarse_qkv,
    grad_coarse_out,
    grad_pool,
    row_grad,
    coarse_rows,
    rows_staged,
    first_staged,
    pool_staged,
    qkv_staged,
    out_staged,
    arrived,
):
    copies = Copies(arrived)
    first_staged[...] = bround(row_first[...] + row_late[...].astype(jnp.float32))
    copies.start(first_staged, row_grad.at[:, :LANES])
    copies.start(row_rest, row_grad.at[:, LANES:])
    part, width = out_staged.shape
    panels = width // LANES
    unpack_pool(
        copies, mine, 4 * part * panels, core_ref[0], pool_staged, grad_pool, scale
    )

    def coarse(start):
        return mine[start : start + part].astype(jnp.float32) * scale

    first = 3 * part * panels
    for which in range(3):
        for panel in range(panels):
            lanes = slice(panel * LANES, (panel + 1) * LANES)
            qkv_staged[which, :, lanes] = coarse((3 * panel + which) * part)
        copies.start(qkv_staged.at[which], grad_coarse_qkv.at[which])
    for panel in range(panels):
        out_staged[:, panel * LANES : (panel + 1) * LANES] = coarse(first + panel * part)
    copies.start(out_staged, grad_coarse_out)
    summed = tn(mixed[0], own_out[...]) + tn(mixed[1], other_out[...])
    rows_staged[...] = bround(parents[...].astype(jnp.float32) + summed)
    copies.start(rows_staged, coarse_rows)
    copies.finish()


def assemble_other(
    fine_scale,
    coarse_scale,
    base,
    core_ref,
    pool_in,
    mine,
    other,
    grad_pool,
    grad_qkv,
    grad_out,
    pool_staged,
    qkv_staged,
    out_staged,
    arrived,
):
    copies = Copies(arrived)
    core = core_ref[0]
    channels = out_staged.shape[0]
    edge = channels % LANES
    skip = pool_staged.shape[0] * pool_staged.shape[1] // LANES
    fine = []
    for half in range(2):
        for i in range(3):
            at = skip + i * channels
            near = mine[base + at : base + at + channels].astype(jnp.float32)
            far = other[at : at + channels].astype(jnp.float32)
            fine.append(jnp.where(core == half, near, far) * fine_scale)
    for i in range(4):
        qkv_staged[:, i * LANES : (i + 1) * LANES] = fine[i]
    qkv_staged[:, 4 * LANES :] = fine[4][:, :edge]
    copies.start(qkv_staged, grad_qkv)
    out_staged[:, :LANES] = fine[5]
    out_staged[:, LANES:] = fine[4][:, edge:]
    copies.start(out_staged, grad_out)
    unpack_pool(copies, other, 0, 1 - core, pool_staged, grad_pool, coarse_scale)
    copies.finish()


def call(
    kernel,
    outs,
    scratch,
    *operands,
    scalars=1,
    micros=1,
    hbm=0,
    copies=0,
    staged=(),
    to_hbm=False,
    aliases=None,
):
    spaces = [pltpu.SMEM] * scalars + [pltpu.HBM] * hbm
    spaces += [pltpu.VMEM] * (len(operands) - len(spaces))
    out_spaces = [pltpu.HBM if to_hbm else pltpu.VMEM] * len(outs)
    return pl.pallas_call(
        kernel,
        out_shape=[jax.ShapeDtypeStruct(shape, dtype) for shape, dtype in outs],
        in_specs=[pl.BlockSpec(memory_space=space) for space in spaces],
        out_specs=[pl.BlockSpec(memory_space=space) for space in out_spaces],
        input_output_aliases=aliases or {},
        scratch_shapes=[pltpu.VMEM(shape, jnp.bfloat16) for shape in scratch]
        + [pltpu.VMEM(shape, jnp.float32) for shape in staged]
        + ([pltpu.SemaphoreType.DMA((copies,))] if copies else []),
        compiler_params=pltpu.CompilerParams(vmem_limit_bytes=VMEM_BYTES),
        cost_estimate=pl.CostEstimate(
            flops=int(micros * 10**9), bytes_accessed=int(micros * 10**6), transcendentals=0
        ),
    )(*operands)


def float_sum(stacked):
    return bround(jnp.sum(stacked.astype(jnp.float32), 0))


def sum_over_chips(parts, rows_after):
    slab = float_sum(lax.all_to_all(parts, NEAR, 0, 0, tiled=True))
    copies = jnp.broadcast_to(slab, (lax.axis_size("zh"),) + slab.shape)
    slab = float_sum(lax.all_to_all(copies, "zh", 0, 0, tiled=True))
    slab, *row_parts = rows_after(slab)
    copies = jnp.broadcast_to(slab, parts.shape)
    total = lax.all_to_all(copies, NEAR, 0, 0, tiled=True)
    return lax.optimization_barrier((total, *row_parts))


def on_device(
    fine_rows,
    qkv_weight,
    out_weight,
    pool_weight,
    coarse_qkv_weight,
    coarse_out_weight,
    parent_index,
    child_slot,
    out_grad,
):
    bf16, f32 = jnp.bfloat16, jnp.float32
    devices = 1
    for name in AXES:
        devices *= lax.axis_size(name)
    row_count, channels = fine_rows.shape
    owned, width = out_grad.shape
    part = coarse_out_weight.shape[0]
    blocks = row_count // LANES
    heads = channels // HD
    coarse_heads = part // HD
    coarse_count = 4 * part * width // LANES
    pool_count = SLOTS // 2 * channels * width // LANES
    fine_count = 2 * channels * channels // LANES
    core = lax.axis_index("sub").astype(jnp.int32).reshape(1)
    first_parent = (lax.axis_index(AXES) * owned).astype(jnp.int32).reshape(1)
    rows = fine_rows.T
    parent_row = parent_index.reshape(1, row_count)
    slot_row = child_slot.reshape(1, row_count)
    own_qkv = coarse_qkv_weight.transpose(0, 2, 1).reshape(3 * part, width)
    wide_rows = heads * LANES

    def in_hbm(*arrays):
        return [pltpu.with_memory_space_constraint(array, pltpu.HBM) for array in arrays]

    def like(*arrays):
        return [(array.shape, array.dtype) for array in arrays]

    def block_outs(count):
        return [
            ((channels, count * LANES), bf16),
            ((channels, count * LANES), bf16),
            ((3 * channels, count * LANES), bf16),
            ((count, LANES, wide_rows), bf16),
            ((count * heads, LANES), f32),
        ]

    sources = (rows, qkv_weight, out_weight, parent_row, slot_row)
    *brought, packed = call(
        bring,
        like(*sources) + [((channels + SPILL, LANES), bf16)],
        [],
        first_parent,
        *in_hbm(*sources),
        hbm=5,
        copies=5,
        micros=1,
    )
    rows, fine_qkv, fine_out, parent_row, slot_row = brought
    packed, give_qkv, give_out = lax.optimization_barrier((packed, own_qkv, coarse_out_weight))
    packed = passed_along(packed, -1)
    other_qkv = swap_cores(give_qkv)
    other_out = swap_cores(give_out)
    sources = (pool_weight, own_qkv, coarse_out_weight, out_grad)
    second = call(
        fine_forward,
        like(*sources) + block_outs(blocks),
        [(2, channels + SPILL, wide_rows)],
        *in_hbm(*sources),
        rows,
        fine_qkv,
        fine_out,
        scalars=0,
        hbm=4,
        copies=4,
        micros=4,
    )
    pool_weight, own_qkv, own_out, out_grad = second[:4]
    hidden, mixed_fine, qkv, exponents, inverses = second[4:]
    children, upward, partial = call(
        pool,
        [((SLOTS, channels, owned), bf16), ((2, part, owned), bf16), ((owned, width), f32)],
        [],
        first_parent,
        hidden,
        parent_row,
        slot_row,
        own_out,
        other_out,
        out_grad,
        pool_weight,
        micros=2,
    )
    (
        parents,
        spill,
        next_upstream,
        grad_parents,
        grad_pooled,
        coarse_input,
        mixed,
        grads,
        next_mixed,
        next_qkv,
        next_exponents,
        next_inverses,
    ) = call(
        coarse_both,
        [
            ((owned, width), bf16),
            ((SPILL, channels), bf16),
            ((channels, LANES), bf16),
            ((owned, width), bf16),
            ((SLOTS // 2, channels, 2 * owned), bf16),
            ((owned, width), bf16),
            ((2, part, owned), bf16),
            ((2, 3 * part, owned), bf16),
        ]
        + block_outs(1)[1:],
        [
            (channels, LANES),
            (1, channels + SPILL, wide_rows),
            (2, part + SPILL, coarse_heads * LANES),
            (2, part, coarse_heads * LANES),
        ],
        packed,
        fine_qkv,
        fine_out,
        partial,
        upward,
        pool_weight,
        own_qkv,
        other_qkv,
        out_grad,
        scalars=0,
        micros=8,
    )
    keep, give = call(
        coarse_weights,
        [
            ((coarse_count + pool_count, LANES), bf16),
            ((coarse_count + pool_count, LANES), bf16),
        ],
        [(SLOTS, channels, owned)],
        core,
        grad_parents,
        children,
        spill,
        coarse_input,
        mixed,
        grads,
        out_grad,
        micros=1,
    )
    got = swap_cores(give)
    upstream, fine_grads, fine_keep, fine_give = call(
        fine_back,
        [
            ((channels, row_count + LANES), bf16),
            ((3 * channels, row_count + LANES), bf16),
            ((fine_count, LANES), bf16),
            ((fine_count, LANES), bf16),
        ],
        [(2, channels, wide_rows)],
        core,
        first_parent,
        rows,
        packed,
        grad_pooled,
        next_upstream,
        parent_row,
        slot_row,
        fine_out,
        exponents,
        inverses,
        qkv,
        mixed_fine,
        next_exponents,
        next_inverses,
        next_qkv,
        next_mixed,
        scalars=2,
        micros=6,
    )

    def rows_after(dependence):
        dependence, given = lax.optimization_barrier((dependence, upstream))
        row_first, row_rest, row_next = call(
            row_gradients,
            [
                ((channels, LANES), f32),
                ((channels, row_count - LANES), bf16),
                ((channels, LANES), bf16),
            ],
            [],
            rows,
            packed,
            fine_qkv,
            given,
            fine_grads,
            scalars=0,
            micros=4,
        )
        return dependence, row_first, row_rest, passed_along(row_next, 1)

    fine_got = swap_cores(fine_give)
    plane = lax.axis_size("zl") * lax.axis_size("y") * lax.axis_size("x")
    count = coarse_count + pool_count + fine_count
    unit = plane * 8
    padded = -(-count // unit) * unit
    (merged,) = call(
        merge, [((padded, LANES), bf16)], [], keep, got, fine_keep, fine_got, scalars=0, micros=1
    )
    total, row_first, row_rest, row_late = sum_over_chips(
        merged.reshape(plane, padded // plane, LANES), rows_after
    )
    total = total.reshape(padded, LANES)
    other = swap_cores(total[coarse_count:count])
    coarse_scale = (owned * devices) ** (-0.5)
    pool_shape = (SLOTS * channels, width)
    half_pool = (SLOTS // 2 * channels, width)
    grad_coarse_qkv, grad_coarse_out, grad_pool, row_grad, coarse_rows = call(
        functools.partial(assemble_own, coarse_scale),
        [
            ((3, part, width), f32),
            ((part, width), f32),
            (pool_shape, f32),
            ((channels, row_count), bf16),
            ((owned, width), bf16),
        ],
        [(owned, width), (channels, LANES)],
        core,
        total,
        row_first,
        row_late,
        row_rest,
        parents,
        mixed,
        own_out,
        other_out,
        copies=7 + SLOTS // 2,
        staged=[half_pool, (3, part, width), (part, width)],
        to_hbm=True,
        micros=3,
    )
    grad_pool, grad_qkv, grad_out = call(
        functools.partial(
            assemble_other, (row_count * devices) ** (-0.5), coarse_scale, coarse_count
        ),
        [(pool_shape, f32), ((channels, 3 * channels), f32), ((channels, channels), f32)],
        [],
        core,
        grad_pool,
        total,
        other,
        hbm=1,
        copies=2 + SLOTS // 2,
        staged=[half_pool, (channels, 3 * channels), (channels, channels)],
        to_hbm=True,
        aliases={1: 0},
        micros=2,
    )
    return (
        coarse_rows,
        row_grad.T,
        grad_qkv,
        grad_out,
        grad_pool,
        grad_coarse_qkv.transpose(0, 2, 1),
        grad_coarse_out,
    )


def solution(mesh):
    torus = Mesh(mesh.devices.reshape(-1, 2, 4, 4, mesh.shape["sub"]), AXES)
    in_specs = (
        P(AXES, None),
        P(),
        P(),
        P(),
        P(None, None, "sub"),
        P("sub", None),
        P(AXES),
        P(AXES),
        P(AXES, None),
    )
    out_specs = (
        P(AXES, None),
        P(AXES, None),
        P(),
        P(),
        P(),
        P(None, None, "sub"),
        P("sub", None),
    )
    return jax.shard_map(
        on_device, mesh=torus, in_specs=in_specs, out_specs=out_specs, check_vma=False
    )
```

```python
import functools

import jax
import jax.numpy as jnp
from jax import lax
from jax.experimental import pallas as pl
from jax.experimental.pallas import tpu as pltpu
from jax.sharding import Mesh, PartitionSpec as P

HD = 16
WINDOW_OCTANTS = 32
DILATION_STRIDE = 4
SLOTS = 8
LANES = 128
SPILL = 16
EPSILON = 1e-05
NEAR = ("zl", "y", "x")
AXES = ("zh",) + NEAR + ("sub",)
VMEM_BYTES = 20 * 1024 * 1024
FAR = -1e30


def passed_along(shard, by):
    count = 1
    for name in AXES:
        count *= lax.axis_size(name)
    pairs = [(i, i + by) for i in range(count) if 0 <= i + by < count]
    return lax.ppermute(shard, AXES, pairs)


def swap_cores(shard):
    return lax.ppermute(shard, "sub", [(0, 1), (1, 0)])


def bround(value):
    return value.astype(jnp.bfloat16)


def product(left, right, left_dim, right_dim):
    return lax.dot_general(
        left, right, (((left_dim,), (right_dim,)), ((), ())), preferred_element_type=jnp.float32
    )


def nn(left, right):
    return product(left, right, 1, 0)


def nt(left, right):
    return product(left, right, 1, 1)


def tn(left, right):
    return product(left, right, 0, 0)


def indicator(condition):
    return bround(jnp.where(condition, 1.0, 0.0))


def layer_norm(value, axis):
    center = value - jnp.mean(value, axis, keepdims=True)
    inverse = lax.rsqrt(jnp.mean(center * center, axis, keepdims=True) + EPSILON)
    return (center * inverse, inverse)


def layer_norm_back(normed, inverse, upstream, axis):
    return inverse * (
        upstream
        - jnp.mean(upstream, axis, keepdims=True)
        - normed * jnp.mean(upstream * normed, axis, keepdims=True)
    )


def window_rows(window_of):
    row = lax.broadcasted_iota(jnp.int32, (SPILL, LANES), 0)
    lane = lax.broadcasted_iota(jnp.int32, (SPILL, LANES), 1)
    return indicator(window_of(lane) == row)


def mask_rows(window_of, heads):
    row = lax.broadcasted_iota(jnp.int32, (SPILL, LANES), 0)
    lane = lax.broadcasted_iota(jnp.int32, (SPILL, LANES), 1)
    other = (window_of(lane) != row) & (row < LANES // WINDOW_OCTANTS)
    return jnp.concatenate([bround(jnp.where(other, FAR, 0.0))] * heads, 1)


def fine_window(at):
    return at % DILATION_STRIDE


def coarse_window(at):
    return at // WINDOW_OCTANTS


def spread(wide, rows, heads):
    for head in range(heads):
        at = slice(head * HD, (head + 1) * HD)
        wide[at, head * LANES : (head + 1) * LANES] = rows[at]


def softmax_parts(score):
    exponent = jnp.exp(score - jnp.max(score, 0, keepdims=True))
    return (bround(exponent), 1.0 / jnp.sum(exponent, 0, keepdims=True))


def diagonal(product):
    return jnp.concatenate([product[:HD, :LANES], product[HD:, LANES:]], 0)


def mix_pair(values, parts):
    mixed = [
        nn(values[i * HD : (i + 1) * HD], exponent) * inverse
        for i, (exponent, inverse) in enumerate(parts)
    ]
    return bround(jnp.concatenate(mixed, 0))


def attend_back(query, key, upstream, parts, grad_probs):
    scores, scales = [], []
    for i, (exponent, inverse) in enumerate(parts):
        grad_prob = grad_probs[:, i * LANES : (i + 1) * LANES]
        weighted = exponent.astype(jnp.float32)
        mean = inverse * jnp.sum(weighted * grad_prob, 0, keepdims=True)
        scores.append(bround(weighted * (grad_prob - mean)))
        scales.append(jnp.broadcast_to(inverse, (HD, LANES)))
    spread_up = bround(upstream.astype(jnp.float32) * jnp.concatenate(scales, 0))
    grad_value = nt(spread_up, jnp.concatenate([exponent for exponent, _ in parts], 0))
    grad_query = nn(key, jnp.concatenate(scores, 1))
    grad_key = nt(query, jnp.concatenate(scores, 0))
    return tuple(bround(diagonal(grad)) for grad in (grad_query, grad_key, grad_value))


def scaled(value):
    return value * jnp.bfloat16(HD**-0.5)


def fine_attention(qkv, wide, classes, heads, mixed, store):
    channels = heads * HD
    spread(wide, scaled(qkv[:channels]), heads)
    keys = jnp.concatenate([qkv[channels : 2 * channels], classes], 0)
    scores = tn(keys, wide[...])
    for head in range(0, heads, 2):
        parts = [
            softmax_parts(scores[:, at * LANES : (at + 1) * LANES]) for at in (head, head + 1)
        ]
        values = qkv[2 * channels + head * HD : 2 * channels + (head + 2) * HD]
        mixed[head * HD : (head + 2) * HD] = mix_pair(values, parts)
        for i in range(2):
            store(head + i, *parts[i])


def clear_wide(wide, heads, window_of):
    wide[...] = jnp.zeros(wide.shape, wide.dtype)
    for slot in range(wide.shape[0]):
        wide[slot, heads * HD :] = mask_rows(window_of, heads)


def fetch(pairs, arrived):
    copies = [
        pltpu.make_async_copy(source, target, arrived.at[i])
        for i, (source, target) in enumerate(pairs)
    ]
    for copy in copies:
        copy.start()
    return copies


def fine_blocks(
    rows, qkv_weight, out_weight, hidden, mixed, qkv, exponents, inverses, wide
):
    channels, count = hidden.shape
    heads = channels // HD
    clear_wide(wide, heads, fine_window)
    classes = window_rows(fine_window)
    rows_float = rows[...].astype(jnp.float32)
    normed, _ = layer_norm(rows_float, 0)
    qkv[...] = bround(tn(qkv_weight[...], bround(normed)))
    for block in range(count // LANES):
        lanes = slice(block * LANES, (block + 1) * LANES)

        def store(head, exponent, inverse):
            exponents[block, :, head * LANES : (head + 1) * LANES] = exponent
            at = block * heads + head
            inverses[at : at + 1] = inverse

        fine_attention(
            qkv[:, lanes],
            wide.at[block % wide.shape[0]],
            classes,
            heads,
            mixed.at[:, lanes],
            store,
        )
    hidden[...] = bround(rows_float + tn(out_weight[...], mixed[...]))


def sum_and_spread(parts, spread_out, staged, arrived):
    total = jnp.zeros(parts.shape[1:], jnp.float32)
    for i in range(parts.shape[0]):
        total += parts[i].astype(jnp.float32)
    step = staged.shape[0]
    for i in range(step):
        staged[i] = bround(total)
    copies = [
        pltpu.make_async_copy(staged, spread_out.at[pl.ds(i * step, step)], arrived.at[i])
        for i in range(spread_out.shape[0] // step)
    ]
    for copy in copies:
        copy.start()
    for copy in copies:
        copy.wait()


def bring(first_parent, *refs):
    sources, targets, packed, arrived = refs[:5], refs[5:10], refs[10], refs[11]
    copies = fetch(tuple(zip(sources, targets)), arrived)
    rows, _, _, parent_index, child_slot = targets
    for i in (0, 3, 4):
        copies[i].wait()
    channels = rows.shape[0]
    packed[:channels] = rows[:, :LANES]
    packed[channels:] = leading_slots(parent_index, child_slot, first_parent)
    copies[1].wait()
    copies[2].wait()


def fine_forward(*refs):
    sources, (rows, qkv_weight, out_weight) = refs[:4], refs[4:7]
    targets, outs, wide, arrived = refs[7:11], refs[11:16], refs[16], refs[17]
    copies = fetch(tuple(zip(sources, targets)), arrived)
    fine_blocks(rows, qkv_weight, out_weight, *outs, wide)
    for copy in copies:
        copy.wait()


def leading_slots(parent_index, child_slot, first_parent):
    slot = lax.broadcasted_iota(jnp.int32, (SPILL, LANES), 0)
    before = parent_index[:, :LANES] < first_parent[0]
    return indicator(before & (child_slot[:, :LANES] == slot))


def slot_numbers(parent_index, child_slot, first_parent, owned):
    parent = lax.broadcasted_iota(jnp.int32, (owned, parent_index.shape[1]), 0)
    mine = parent_index - first_parent[0] == parent
    return jnp.where(mine, child_slot, -1)


def pool(
    first_parent,
    hidden,
    parent_index,
    child_slot,
    own_out,
    other_out,
    out_grad,
    pool_weight,
    children,
    upward,
    partial,
):
    owned = out_grad.shape[0]
    slot_of = slot_numbers(parent_index[...], child_slot[...], first_parent, owned)
    for slot in range(0, SLOTS, 2):
        both = jnp.concatenate([indicator(slot_of == slot), indicator(slot_of == slot + 1)], 0)
        pair = bround(nt(hidden[...], both))
        children[slot] = pair[:, :owned]
        children[slot + 1] = pair[:, owned:]
    channels = hidden.shape[0]
    total = jnp.zeros(partial.shape, jnp.float32)
    for slot in range(SLOTS):
        total += tn(children[slot], pool_weight[slot * channels : (slot + 1) * channels])
    partial[...] = total
    for half, out_weight in enumerate((own_out, other_out)):
        upward[half] = bround(nt(out_weight[...], out_grad[...]))


def coarse_both(
    packed,
    fine_qkv,
    fine_out,
    partial,
    upward,
    pool_weight,
    own_qkv,
    other_qkv,
    out_grad,
    parents,
    spill,
    next_upstream,
    grad_parents,
    grad_pooled,
    coarse_input,
    mixed,
    grads,
    next_mixed,
    next_qkv,
    next_exponents,
    next_inverses,
    next_hidden,
    wide_next,
    wide_query,
    wide_grad,
):
    owned, width = out_grad.shape
    channels = fine_out.shape[0]
    fine_blocks(
        packed.at[:channels],
        fine_qkv,
        fine_out,
        next_hidden,
        next_mixed,
        next_qkv,
        next_exponents,
        next_inverses,
        wide_next,
    )
    leading = packed[channels:]
    spill[...] = bround(nt(leading, next_hidden[...]))
    part = upward.shape[1]
    heads = part // HD
    halves = range(2)
    qkv_weights = (own_qkv, other_qkv)
    for wide in (wide_query, wide_grad):
        wide[...] = jnp.zeros(wide.shape, wide.dtype)
    for half in halves:
        wide_query[half, part:] = mask_rows(coarse_window, heads)
    spill_row = lax.broadcasted_iota(jnp.int32, (SPILL, channels), 0)
    late = jnp.zeros((SPILL, width), jnp.float32)
    for slot in range(SLOTS):
        chosen = jnp.where(spill_row == slot, spill[...], jnp.zeros_like(spill))
        late += nn(chosen, pool_weight[slot * channels : (slot + 1) * channels])
    late = jnp.sum(late, 0, keepdims=True)
    at_last = lax.broadcasted_iota(jnp.int32, (owned, width), 0) == owned - 1
    parents[...] = bround(partial[...] + jnp.where(at_last, late, 0.0))
    normed, inverse = layer_norm(parents[...].astype(jnp.float32), 1)
    coarse_input[...] = bround(normed)
    upstream = out_grad[...]
    classes = window_rows(coarse_window)
    qkvs = [bround(nt(qkv_weights[half][...], coarse_input[...])) for half in halves]
    for half in halves:
        spread(wide_query.at[half], scaled(qkvs[half][:part]), heads)
    scores = [
        tn(jnp.concatenate([qkvs[half][part : 2 * part], classes], 0), wide_query[half])
        for half in halves
    ]
    parts = {}
    for half in halves:
        for head in range(0, heads, 2):
            at = slice(head * HD, (head + 2) * HD)
            pair = [
                softmax_parts(scores[half][:, i * LANES : (i + 1) * LANES])
                for i in (head, head + 1)
            ]
            parts[half, head] = pair
            values = qkvs[half][2 * part + head * HD : 2 * part + (head + 2) * HD]
            mixed[half, at] = mix_pair(values, pair)
            for i in range(2):
                rows = slice((head + i) * HD, (head + i + 1) * HD)
                lanes = slice((head + i) * LANES, (head + i + 1) * LANES)
                weighted = scaled(upward[half, rows]).astype(jnp.float32) * pair[i][1]
                wide_grad[half, rows, lanes] = bround(weighted)
    grad_probs = [tn(qkvs[half][2 * part :], wide_grad[half]) for half in halves]
    for half in halves:
        for head in range(0, heads, 2):
            at = [slice(i * part + head * HD, i * part + (head + 2) * HD) for i in range(3)]
            back = attend_back(
                qkvs[half][at[0]],
                qkvs[half][at[1]],
                upward[half, at[0]],
                parts[half, head],
                grad_probs[half][:, head * LANES : (head + 2) * LANES],
            )
            for which in range(3):
                grads[half, at[which]] = back[which]
    grad_normed = sum(tn(grads[half], qkv_weights[half][...]) for half in halves)
    upstream_total = bround(
        upstream.astype(jnp.float32) + layer_norm_back(normed, inverse, grad_normed, 1)
    )
    grad_parents[...] = upstream_total
    grad_all = bround(nt(pool_weight[...], upstream_total))
    last = lax.broadcasted_iota(jnp.int32, (SPILL, owned), 1) == owned - 1
    spill_slot = lax.broadcasted_iota(jnp.int32, (SPILL, owned), 0)
    edge_total = jnp.zeros((SPILL, channels), jnp.float32)
    for slot in range(SLOTS):
        grad_slot = grad_all[slot * channels : (slot + 1) * channels]
        grad_pooled[slot // 2, :, slot % 2 * owned : (slot % 2 + 1) * owned] = grad_slot
        edge_total += nt(indicator(last & (spill_slot == slot)), grad_slot)
    next_upstream[...] = bround(tn(bround(edge_total), leading))


def coarse_weights(
    core_ref,
    grad_parents,
    children,
    spill,
    coarse_input,
    mixed,
    grads,
    out_grad,
    keep,
    give,
    pooled,
):
    core = core_ref[0]
    width = out_grad.shape[1]
    owned, channels = out_grad.shape[0], pooled.shape[1]
    part = mixed.shape[1]
    last = lax.broadcasted_iota(jnp.int32, (SPILL, owned), 1) == owned - 1
    spill_slot = lax.broadcasted_iota(jnp.int32, (SPILL, owned), 0)
    for slot in range(0, SLOTS, 2):
        edges = [indicator(last & (spill_slot == at)) for at in (slot, slot + 1)]
        edge = bround(tn(spill[...], jnp.concatenate(edges, 1)))
        pooled[slot] = children[slot] + edge[:, :owned]
        pooled[slot + 1] = children[slot + 1] + edge[:, owned:]
    panels = width // LANES

    def store(target, start, value):
        for panel in range(panels):
            at = start + panel * value.shape[0]
            target[at : at + value.shape[0]] = bround(
                value[:, panel * LANES : (panel + 1) * LANES]
            )

    for half, target in enumerate((keep, give)):
        store(target, 0, nn(grads[half], coarse_input[...]))
        store(target, 3 * part * panels, nn(mixed[half], out_grad[...]))
    base = 4 * part * panels
    for target, first in ((keep, core), (give, 1 - core)):
        for step in range(SLOTS // 2):
            grad_pool = nn(pooled[first * (SLOTS // 2) + step], grad_parents[...])
            store(target, base + step * panels * channels, grad_pool)


def fine_back(
    core_ref,
    first_parent,
    rows,
    packed,
    grad_pooled,
    next_upstream,
    parent_index,
    child_slot,
    out_weight,
    *rest,
):
    own, beyond = rest[:4], rest[4:8]
    upstreams, grads, keep, give, wide = rest[8:]
    channels, row_count = rows.shape
    owned = grad_pooled.shape[2] // 2
    heads = channels // HD
    all_rows = jnp.concatenate([rows[...], packed[:channels]], 1)
    mixed = jnp.concatenate([own[3][...], beyond[3][...]], 1)
    normed, _ = layer_norm(all_rows.astype(jnp.float32), 0)
    slot_of = slot_numbers(parent_index[...], child_slot[...], first_parent, owned)
    upstream = jnp.zeros((channels, row_count), jnp.float32)
    for slot in range(0, SLOTS, 2):
        both = jnp.concatenate([indicator(slot_of == slot), indicator(slot_of == slot + 1)], 0)
        upstream += nn(grad_pooled[slot // 2], both)
    upstream = jnp.concatenate([bround(upstream), next_upstream[...]], 1)
    upstreams[...] = upstream
    upward = bround(nn(out_weight[...], upstream))
    wide[...] = jnp.zeros(wide.shape, wide.dtype)
    blocks = row_count // LANES
    for block in range(blocks + 1):
        exponents, inverses, qkv, _ = own if block < blocks else beyond
        within = block % blocks
        lanes = slice(block * LANES, (block + 1) * LANES)
        inner = slice(within * LANES, (within + 1) * LANES)
        grad_rows = wide.at[block % wide.shape[0]]
        scales = [
            inverses[within * heads + head : within * heads + head + 1] for head in range(heads)
        ]
        for head in range(heads):
            at = slice(head * HD, (head + 1) * HD)
            weighted = scaled(upward[at, lanes]).astype(jnp.float32) * scales[head]
            grad_rows[at, head * LANES : (head + 1) * LANES] = bround(weighted)
        grad_probs = tn(qkv[2 * channels :, inner], grad_rows[...])
        for head in range(0, heads, 2):
            at = [slice(i * channels + head * HD, i * channels + (head + 2) * HD) for i in range(3)]
            parts = [
                (exponents[within, :, i * LANES : (i + 1) * LANES], scales[i])
                for i in (head, head + 1)
            ]
            back = attend_back(
                qkv[at[0], inner],
                qkv[at[1], inner],
                upward[at[0], lanes],
                parts,
                grad_probs[:, head * LANES : (head + 2) * LANES],
            )
            for which in range(3):
                grads[at[which], lanes] = back[which]
    grad_qkv = bround(nt(bround(normed), grads[...]))
    grad_out = bround(nt(mixed, upstream))
    core = core_ref[0]
    whole = 3 * channels // LANES
    panels = [grad_qkv[:, i * LANES : (i + 1) * LANES] for i in range(whole)]
    panels.append(jnp.concatenate([grad_qkv[:, whole * LANES :], grad_out[:, LANES:]], 1))
    panels.append(grad_out[:, :LANES])
    half = len(panels) // 2
    for i in range(half):
        at = slice(i * channels, (i + 1) * channels)
        keep[at] = jnp.where(core == 0, panels[i], panels[half + i])
        give[at] = jnp.where(core == 0, panels[half + i], panels[i])


def row_gradients(rows, packed, qkv_weight, upstream, grads, row_first, row_rest, row_next):
    channels, row_count = rows.shape
    all_rows = jnp.concatenate([rows[...], packed[:channels]], 1)
    normed, inverse = layer_norm(all_rows.astype(jnp.float32), 0)
    grad_normed = nn(qkv_weight[...], grads[...])
    total = upstream[...].astype(jnp.float32) + layer_norm_back(normed, inverse, grad_normed, 0)
    row_first[...] = total[:, :LANES]
    row_rest[...] = bround(total[:, LANES:row_count])
    row_next[...] = bround(total[:, row_count:])


def merge(keep, got, fine_keep, fine_got, total):
    first, second = keep.shape[0], fine_keep.shape[0]
    total[:first] = keep[...] + got[...]
    total[first : first + second] = fine_keep[...] + fine_got[...]
    pad = total.shape[0] - first - second
    total[first + second :] = jnp.zeros((pad, LANES), total.dtype)


class Copies:
    def __init__(self, arrived):
        self.arrived, self.started = arrived, []

    def start(self, source, target):
        copy = pltpu.make_async_copy(source, target, self.arrived.at[len(self.started)])
        copy.start()
        self.started.append(copy)

    def finish(self):
        for copy in self.started:
            copy.wait()


def unpack_pool(copies, source, start, half, staged, target, scale):
    panels = staged.shape[1] // LANES
    channels = staged.shape[0] * 2 // SLOTS
    for step in range(SLOTS // 2):
        rows = slice(step * channels, (step + 1) * channels)
        for panel in range(panels):
            at = start + (step * panels + panel) * channels
            staged[rows, panel * LANES : (panel + 1) * LANES] = (
                source[at : at + channels].astype(jnp.float32) * scale
            )
        row = pl.multiple_of(half * staged.shape[0] + step * channels, 8)
        copies.start(staged.at[rows], target.at[pl.ds(row, channels)])


def assemble_own(
    scale,
    core_ref,
    mine,
    row_first,
    row_late,
    row_rest,
    parents,
    mixed,
    own_out,
    other_out,
    grad_coarse_qkv,
    grad_coarse_out,
    grad_pool,
    row_grad,
    coarse_rows,
    rows_staged,
    first_staged,
    pool_staged,
    qkv_staged,
    out_staged,
    arrived,
):
    copies = Copies(arrived)
    first_staged[...] = bround(row_first[...] + row_late[...].astype(jnp.float32))
    copies.start(first_staged, row_grad.at[:, :LANES])
    copies.start(row_rest, row_grad.at[:, LANES:])
    part, width = out_staged.shape
    panels = width // LANES
    unpack_pool(
        copies, mine, 4 * part * panels, core_ref[0], pool_staged, grad_pool, scale
    )

    def coarse(start):
        return mine[start : start + part].astype(jnp.float32) * scale

    first = 3 * part * panels
    for which in range(3):
        for panel in range(panels):
            lanes = slice(panel * LANES, (panel + 1) * LANES)
            qkv_staged[which, :, lanes] = coarse((3 * panel + which) * part)
        copies.start(qkv_staged.at[which], grad_coarse_qkv.at[which])
    for panel in range(panels):
        out_staged[:, panel * LANES : (panel + 1) * LANES] = coarse(first + panel * part)
    copies.start(out_staged, grad_coarse_out)
    summed = tn(mixed[0], own_out[...]) + tn(mixed[1], other_out[...])
    rows_staged[...] = bround(parents[...].astype(jnp.float32) + summed)
    copies.start(rows_staged, coarse_rows)
    copies.finish()


def assemble_other(
    fine_scale,
    coarse_scale,
    base,
    core_ref,
    pool_in,
    mine,
    other,
    grad_pool,
    grad_qkv,
    grad_out,
    pool_staged,
    qkv_staged,
    out_staged,
    arrived,
):
    copies = Copies(arrived)
    core = core_ref[0]
    channels = out_staged.shape[0]
    edge = channels % LANES
    skip = pool_staged.shape[0] * pool_staged.shape[1] // LANES
    fine = []
    for half in range(2):
        for i in range(3):
            at = skip + i * channels
            near = mine[base + at : base + at + channels].astype(jnp.float32)
            far = other[at : at + channels].astype(jnp.float32)
            fine.append(jnp.where(core == half, near, far) * fine_scale)
    for i in range(4):
        qkv_staged[:, i * LANES : (i + 1) * LANES] = fine[i]
    qkv_staged[:, 4 * LANES :] = fine[4][:, :edge]
    copies.start(qkv_staged, grad_qkv)
    out_staged[:, :LANES] = fine[5]
    out_staged[:, LANES:] = fine[4][:, edge:]
    copies.start(out_staged, grad_out)
    unpack_pool(copies, other, 0, 1 - core, pool_staged, grad_pool, coarse_scale)
    copies.finish()


def call(
    kernel,
    outs,
    scratch,
    *operands,
    scalars=1,
    micros=1,
    hbm=0,
    copies=0,
    staged=(),
    to_hbm=False,
    aliases=None,
):
    spaces = [pltpu.SMEM] * scalars + [pltpu.HBM] * hbm
    spaces += [pltpu.VMEM] * (len(operands) - len(spaces))
    out_spaces = [pltpu.HBM if to_hbm else pltpu.VMEM] * len(outs)
    return pl.pallas_call(
        kernel,
        out_shape=[jax.ShapeDtypeStruct(shape, dtype) for shape, dtype in outs],
        in_specs=[pl.BlockSpec(memory_space=space) for space in spaces],
        out_specs=[pl.BlockSpec(memory_space=space) for space in out_spaces],
        input_output_aliases=aliases or {},
        scratch_shapes=[pltpu.VMEM(shape, jnp.bfloat16) for shape in scratch]
        + [pltpu.VMEM(shape, jnp.float32) for shape in staged]
        + ([pltpu.SemaphoreType.DMA((copies,))] if copies else []),
        compiler_params=pltpu.CompilerParams(vmem_limit_bytes=VMEM_BYTES),
        cost_estimate=pl.CostEstimate(
            flops=int(micros * 10**9), bytes_accessed=int(micros * 10**6), transcendentals=0
        ),
    )(*operands)


def float_sum(stacked):
    return bround(jnp.sum(stacked.astype(jnp.float32), 0))


def sum_over_chips(parts, rows_after):
    slab = float_sum(lax.all_to_all(parts, NEAR, 0, 0, tiled=True))
    copies = jnp.broadcast_to(slab, (lax.axis_size("zh"),) + slab.shape)
    slabs = lax.all_to_all(copies, "zh", 0, 0, tiled=True)
    slabs, *row_parts = rows_after(slabs)
    step = parts.shape[0] // 4
    (copies,) = call(
        sum_and_spread,
        [(parts.shape, parts.dtype)],
        [(step,) + slab.shape],
        slabs,
        scalars=0,
        copies=4,
        to_hbm=True,
        micros=0.5,
    )
    total = lax.all_to_all(copies, NEAR, 0, 0, tiled=True)
    return lax.optimization_barrier((total, *row_parts))


def on_device(
    fine_rows,
    qkv_weight,
    out_weight,
    pool_weight,
    coarse_qkv_weight,
    coarse_out_weight,
    parent_index,
    child_slot,
    out_grad,
):
    bf16, f32 = jnp.bfloat16, jnp.float32
    devices = 1
    for name in AXES:
        devices *= lax.axis_size(name)
    row_count, channels = fine_rows.shape
    owned, width = out_grad.shape
    part = coarse_out_weight.shape[0]
    blocks = row_count // LANES
    heads = channels // HD
    coarse_heads = part // HD
    coarse_count = 4 * part * width // LANES
    pool_count = SLOTS // 2 * channels * width // LANES
    fine_count = 2 * channels * channels // LANES
    core = lax.axis_index("sub").astype(jnp.int32).reshape(1)
    first_parent = (lax.axis_index(AXES) * owned).astype(jnp.int32).reshape(1)
    rows = fine_rows.T
    parent_row = parent_index.reshape(1, row_count)
    slot_row = child_slot.reshape(1, row_count)
    own_qkv = coarse_qkv_weight.transpose(0, 2, 1).reshape(3 * part, width)
    wide_rows = heads * LANES

    def in_hbm(*arrays):
        return [pltpu.with_memory_space_constraint(array, pltpu.HBM) for array in arrays]

    def like(*arrays):
        return [(array.shape, array.dtype) for array in arrays]

    def block_outs(count):
        return [
            ((channels, count * LANES), bf16),
            ((channels, count * LANES), bf16),
            ((3 * channels, count * LANES), bf16),
            ((count, LANES, wide_rows), bf16),
            ((count * heads, LANES), f32),
        ]

    sources = (rows, qkv_weight, out_weight, parent_row, slot_row)
    *brought, packed = call(
        bring,
        like(*sources) + [((channels + SPILL, LANES), bf16)],
        [],
        first_parent,
        *in_hbm(*sources),
        hbm=5,
        copies=5,
        micros=1,
    )
    rows, fine_qkv, fine_out, parent_row, slot_row = brought
    packed, give_qkv, give_out = lax.optimization_barrier((packed, own_qkv, coarse_out_weight))
    packed = passed_along(packed, -1)
    other_qkv = swap_cores(give_qkv)
    other_out = swap_cores(give_out)
    sources = (pool_weight, own_qkv, coarse_out_weight, out_grad)
    second = call(
        fine_forward,
        like(*sources) + block_outs(blocks),
        [(2, channels + SPILL, wide_rows)],
        *in_hbm(*sources),
        rows,
        fine_qkv,
        fine_out,
        scalars=0,
        hbm=4,
        copies=4,
        micros=4,
    )
    pool_weight, own_qkv, own_out, out_grad = second[:4]
    hidden, mixed_fine, qkv, exponents, inverses = second[4:]
    children, upward, partial = call(
        pool,
        [((SLOTS, channels, owned), bf16), ((2, part, owned), bf16), ((owned, width), f32)],
        [],
        first_parent,
        hidden,
        parent_row,
        slot_row,
        own_out,
        other_out,
        out_grad,
        pool_weight,
        micros=2,
    )
    (
        parents,
        spill,
        next_upstream,
        grad_parents,
        grad_pooled,
        coarse_input,
        mixed,
        grads,
        next_mixed,
        next_qkv,
        next_exponents,
        next_inverses,
    ) = call(
        coarse_both,
        [
            ((owned, width), bf16),
            ((SPILL, channels), bf16),
            ((channels, LANES), bf16),
            ((owned, width), bf16),
            ((SLOTS // 2, channels, 2 * owned), bf16),
            ((owned, width), bf16),
            ((2, part, owned), bf16),
            ((2, 3 * part, owned), bf16),
        ]
        + block_outs(1)[1:],
        [
            (channels, LANES),
            (1, channels + SPILL, wide_rows),
            (2, part + SPILL, coarse_heads * LANES),
            (2, part, coarse_heads * LANES),
        ],
        packed,
        fine_qkv,
        fine_out,
        partial,
        upward,
        pool_weight,
        own_qkv,
        other_qkv,
        out_grad,
        scalars=0,
        micros=8,
    )
    keep, give = call(
        coarse_weights,
        [
            ((coarse_count + pool_count, LANES), bf16),
            ((coarse_count + pool_count, LANES), bf16),
        ],
        [(SLOTS, channels, owned)],
        core,
        grad_parents,
        children,
        spill,
        coarse_input,
        mixed,
        grads,
        out_grad,
        micros=1,
    )
    got = swap_cores(give)
    upstream, fine_grads, fine_keep, fine_give = call(
        fine_back,
        [
            ((channels, row_count + LANES), bf16),
            ((3 * channels, row_count + LANES), bf16),
            ((fine_count, LANES), bf16),
            ((fine_count, LANES), bf16),
        ],
        [(2, channels, wide_rows)],
        core,
        first_parent,
        rows,
        packed,
        grad_pooled,
        next_upstream,
        parent_row,
        slot_row,
        fine_out,
        exponents,
        inverses,
        qkv,
        mixed_fine,
        next_exponents,
        next_inverses,
        next_qkv,
        next_mixed,
        scalars=2,
        micros=6,
    )

    def rows_after(dependence):
        dependence, given = lax.optimization_barrier((dependence, upstream))
        row_first, row_rest, row_next = call(
            row_gradients,
            [
                ((channels, LANES), f32),
                ((channels, row_count - LANES), bf16),
                ((channels, LANES), bf16),
            ],
            [],
            rows,
            packed,
            fine_qkv,
            given,
            fine_grads,
            scalars=0,
            micros=4,
        )
        return dependence, row_first, row_rest, passed_along(row_next, 1)

    fine_got = swap_cores(fine_give)
    plane = lax.axis_size("zl") * lax.axis_size("y") * lax.axis_size("x")
    count = coarse_count + pool_count + fine_count
    unit = plane * 8
    padded = -(-count // unit) * unit
    (merged,) = call(
        merge, [((padded, LANES), bf16)], [], keep, got, fine_keep, fine_got, scalars=0, micros=1
    )
    total, row_first, row_rest, row_late = sum_over_chips(
        merged.reshape(plane, padded // plane, LANES), rows_after
    )
    total = total.reshape(padded, LANES)
    other = swap_cores(total[coarse_count:count])
    coarse_scale = (owned * devices) ** (-0.5)
    pool_shape = (SLOTS * channels, width)
    half_pool = (SLOTS // 2 * channels, width)
    grad_coarse_qkv, grad_coarse_out, grad_pool, row_grad, coarse_rows = call(
        functools.partial(assemble_own, coarse_scale),
        [
            ((3, part, width), f32),
            ((part, width), f32),
            (pool_shape, f32),
            ((channels, row_count), bf16),
            ((owned, width), bf16),
        ],
        [(owned, width), (channels, LANES)],
        core,
        total,
        row_first,
        row_late,
        row_rest,
        parents,
        mixed,
        own_out,
        other_out,
        copies=7 + SLOTS // 2,
        staged=[half_pool, (3, part, width), (part, width)],
        to_hbm=True,
        micros=3,
    )
    grad_pool, grad_qkv, grad_out = call(
        functools.partial(
            assemble_other, (row_count * devices) ** (-0.5), coarse_scale, coarse_count
        ),
        [(pool_shape, f32), ((channels, 3 * channels), f32), ((channels, channels), f32)],
        [],
        core,
        grad_pool,
        total,
        other,
        hbm=1,
        copies=2 + SLOTS // 2,
        staged=[half_pool, (channels, 3 * channels), (channels, channels)],
        to_hbm=True,
        aliases={1: 0},
        micros=2,
    )
    return (
        coarse_rows,
        row_grad.T,
        grad_qkv,
        grad_out,
        grad_pool,
        grad_coarse_qkv.transpose(0, 2, 1),
        grad_coarse_out,
    )


def solution(mesh):
    torus = Mesh(mesh.devices.reshape(-1, 2, 4, 4, mesh.shape["sub"]), AXES)
    in_specs = (
        P(AXES, None),
        P(),
        P(),
        P(),
        P(None, None, "sub"),
        P("sub", None),
        P(AXES),
        P(AXES),
        P(AXES, None),
    )
    out_specs = (
        P(AXES, None),
        P(AXES, None),
        P(),
        P(),
        P(),
        P(None, None, "sub"),
        P("sub", None),
    )
    return jax.shard_map(
        on_device, mesh=torus, in_specs=in_specs, out_specs=out_specs, check_vma=False
    )
```

```python
import functools

import jax
import jax.numpy as jnp
from jax import lax
from jax.experimental import pallas as pl
from jax.experimental.pallas import tpu as pltpu
from jax.sharding import Mesh, PartitionSpec as P

HD = 16
WINDOW_OCTANTS = 32
DILATION_STRIDE = 4
SLOTS = 8
LANES = 128
SPILL = 16
EPSILON = 1e-05
NEAR = ("zl", "y", "x")
AXES = ("zh",) + NEAR + ("sub",)
VMEM_BYTES = 20 * 1024 * 1024
FAR = -1e30


def passed_along(shard, by):
    count = 1
    for name in AXES:
        count *= lax.axis_size(name)
    pairs = [(i, i + by) for i in range(count) if 0 <= i + by < count]
    return lax.ppermute(shard, AXES, pairs)


def swap_cores(shard):
    return lax.ppermute(shard, "sub", [(0, 1), (1, 0)])


def bround(value):
    return value.astype(jnp.bfloat16)


def product(left, right, left_dim, right_dim):
    return lax.dot_general(
        left, right, (((left_dim,), (right_dim,)), ((), ())), preferred_element_type=jnp.float32
    )


def nn(left, right):
    return product(left, right, 1, 0)


def nt(left, right):
    return product(left, right, 1, 1)


def tn(left, right):
    return product(left, right, 0, 0)


def indicator(condition):
    return bround(jnp.where(condition, 1.0, 0.0))


def layer_norm(value, axis):
    center = value - jnp.mean(value, axis, keepdims=True)
    inverse = lax.rsqrt(jnp.mean(center * center, axis, keepdims=True) + EPSILON)
    return (center * inverse, inverse)


def layer_norm_back(normed, inverse, upstream, axis):
    return inverse * (
        upstream
        - jnp.mean(upstream, axis, keepdims=True)
        - normed * jnp.mean(upstream * normed, axis, keepdims=True)
    )


def window_rows(window_of):
    row = lax.broadcasted_iota(jnp.int32, (SPILL, LANES), 0)
    lane = lax.broadcasted_iota(jnp.int32, (SPILL, LANES), 1)
    return indicator(window_of(lane) == row)


def mask_rows(window_of, heads):
    row = lax.broadcasted_iota(jnp.int32, (SPILL, LANES), 0)
    lane = lax.broadcasted_iota(jnp.int32, (SPILL, LANES), 1)
    other = (window_of(lane) != row) & (row < LANES // WINDOW_OCTANTS)
    return jnp.concatenate([bround(jnp.where(other, FAR, 0.0))] * heads, 1)


def fine_window(at):
    return at % DILATION_STRIDE


def coarse_window(at):
    return at // WINDOW_OCTANTS


def spread(wide, rows, heads):
    for head in range(heads):
        at = slice(head * HD, (head + 1) * HD)
        wide[at, head * LANES : (head + 1) * LANES] = rows[at]


def softmax_parts(score):
    exponent = jnp.exp(score - jnp.max(score, 0, keepdims=True))
    return (bround(exponent), 1.0 / jnp.sum(exponent, 0, keepdims=True))


def diagonal(product):
    return jnp.concatenate([product[:HD, :LANES], product[HD:, LANES:]], 0)


def mix_pair(values, parts):
    mixed = [
        nn(values[i * HD : (i + 1) * HD], exponent) * inverse
        for i, (exponent, inverse) in enumerate(parts)
    ]
    return bround(jnp.concatenate(mixed, 0))


def attend_back(query, key, upstream, mixed, parts, grad_probs):
    scales = [jnp.broadcast_to(inverse, (HD, LANES)) for _, inverse in parts]
    upward = upstream.astype(jnp.float32) * jnp.concatenate(scales, 0)
    overlap = upward * mixed.astype(jnp.float32) * HD**-0.5
    scores = []
    for i, (exponent, _) in enumerate(parts):
        grad_prob = grad_probs[:, i * LANES : (i + 1) * LANES]
        mean = jnp.sum(overlap[i * HD : (i + 1) * HD], 0, keepdims=True)
        scores.append(bround(exponent.astype(jnp.float32) * (grad_prob - mean)))
    spread_up = bround(upward)
    grad_value = nt(spread_up, jnp.concatenate([exponent for exponent, _ in parts], 0))
    grad_query = nn(key, jnp.concatenate(scores, 1))
    grad_key = nt(query, jnp.concatenate(scores, 0))
    return tuple(bround(diagonal(grad)) for grad in (grad_query, grad_key, grad_value))


def scaled(value):
    return value * jnp.bfloat16(HD**-0.5)


def fine_attention(qkv, wide, classes, heads, mixed, store):
    channels = heads * HD
    spread(wide, scaled(qkv[:channels]), heads)
    keys = jnp.concatenate([qkv[channels : 2 * channels], classes], 0)
    scores = tn(keys, wide[...])
    for head in range(0, heads, 2):
        parts = [
            softmax_parts(scores[:, at * LANES : (at + 1) * LANES]) for at in (head, head + 1)
        ]
        values = qkv[2 * channels + head * HD : 2 * channels + (head + 2) * HD]
        mixed[head * HD : (head + 2) * HD] = mix_pair(values, parts)
        for i in range(2):
            store(head + i, *parts[i])


def clear_wide(wide, heads, window_of):
    wide[...] = jnp.zeros(wide.shape, wide.dtype)
    for slot in range(wide.shape[0]):
        wide[slot, heads * HD :] = mask_rows(window_of, heads)


def fetch(pairs, arrived):
    copies = [
        pltpu.make_async_copy(source, target, arrived.at[i])
        for i, (source, target) in enumerate(pairs)
    ]
    for copy in copies:
        copy.start()
    return copies


def fine_blocks(
    rows, qkv_weight, out_weight, hidden, mixed, qkv, exponents, inverses, wide
):
    channels, count = hidden.shape
    heads = channels // HD
    clear_wide(wide, heads, fine_window)
    classes = window_rows(fine_window)
    rows_float = rows[...].astype(jnp.float32)
    normed, _ = layer_norm(rows_float, 0)
    qkv[...] = bround(tn(qkv_weight[...], bround(normed)))
    for block in range(count // LANES):
        lanes = slice(block * LANES, (block + 1) * LANES)

        def store(head, exponent, inverse):
            exponents[block, :, head * LANES : (head + 1) * LANES] = exponent
            at = block * heads + head
            inverses[at : at + 1] = inverse

        fine_attention(
            qkv[:, lanes],
            wide.at[block % wide.shape[0]],
            classes,
            heads,
            mixed.at[:, lanes],
            store,
        )
    hidden[...] = bround(rows_float + tn(out_weight[...], mixed[...]))


def sum_and_spread(parts, spread_out, staged, arrived):
    total = jnp.zeros(parts.shape[1:], jnp.float32)
    for i in range(parts.shape[0]):
        total += parts[i].astype(jnp.float32)
    step = staged.shape[0]
    for i in range(step):
        staged[i] = bround(total)
    copies = [
        pltpu.make_async_copy(staged, spread_out.at[pl.ds(i * step, step)], arrived.at[i])
        for i in range(spread_out.shape[0] // step)
    ]
    for copy in copies:
        copy.start()
    for copy in copies:
        copy.wait()


def bring(first_parent, *refs):
    sources, targets, packed, arrived = refs[:5], refs[5:10], refs[10], refs[11]
    copies = fetch(tuple(zip(sources, targets)), arrived)
    rows, _, _, parent_index, child_slot = targets
    for i in (0, 3, 4):
        copies[i].wait()
    channels = rows.shape[0]
    packed[:channels] = rows[:, :LANES]
    packed[channels:] = leading_slots(parent_index, child_slot, first_parent)
    copies[1].wait()
    copies[2].wait()


def fine_forward(*refs):
    sources, (rows, qkv_weight, out_weight) = refs[:4], refs[4:7]
    targets, outs, wide, arrived = refs[7:11], refs[11:16], refs[16], refs[17]
    copies = fetch(tuple(zip(sources, targets)), arrived)
    fine_blocks(rows, qkv_weight, out_weight, *outs, wide)
    for copy in copies:
        copy.wait()


def leading_slots(parent_index, child_slot, first_parent):
    slot = lax.broadcasted_iota(jnp.int32, (SPILL, LANES), 0)
    before = parent_index[:, :LANES] < first_parent[0]
    return indicator(before & (child_slot[:, :LANES] == slot))


def slot_numbers(parent_index, child_slot, first_parent, owned):
    parent = lax.broadcasted_iota(jnp.int32, (owned, parent_index.shape[1]), 0)
    mine = parent_index - first_parent[0] == parent
    return jnp.where(mine, child_slot, -1)


def pool(
    first_parent,
    hidden,
    parent_index,
    child_slot,
    own_out,
    other_out,
    out_grad,
    pool_weight,
    children,
    upward,
    partial,
):
    owned = out_grad.shape[0]
    slot_of = slot_numbers(parent_index[...], child_slot[...], first_parent, owned)
    for slot in range(0, SLOTS, 2):
        both = jnp.concatenate([indicator(slot_of == slot), indicator(slot_of == slot + 1)], 0)
        pair = bround(nt(hidden[...], both))
        children[slot] = pair[:, :owned]
        children[slot + 1] = pair[:, owned:]
    channels = hidden.shape[0]
    total = jnp.zeros(partial.shape, jnp.float32)
    for slot in range(SLOTS):
        total += tn(children[slot], pool_weight[slot * channels : (slot + 1) * channels])
    partial[...] = total
    for half, out_weight in enumerate((own_out, other_out)):
        upward[half] = bround(nt(out_weight[...], out_grad[...]))


def coarse_both(
    packed,
    fine_qkv,
    fine_out,
    partial,
    upward,
    pool_weight,
    own_qkv,
    other_qkv,
    out_grad,
    parents,
    spill,
    next_upstream,
    grad_parents,
    grad_pooled,
    coarse_input,
    mixed,
    grads,
    next_mixed,
    next_qkv,
    next_exponents,
    next_inverses,
    next_hidden,
    wide_next,
    wide_query,
    wide_grad,
):
    owned, width = out_grad.shape
    channels = fine_out.shape[0]
    fine_blocks(
        packed.at[:channels],
        fine_qkv,
        fine_out,
        next_hidden,
        next_mixed,
        next_qkv,
        next_exponents,
        next_inverses,
        wide_next,
    )
    leading = packed[channels:]
    spill[...] = bround(nt(leading, next_hidden[...]))
    part = upward.shape[1]
    heads = part // HD
    halves = range(2)
    qkv_weights = (own_qkv, other_qkv)
    for wide in (wide_query, wide_grad):
        wide[...] = jnp.zeros(wide.shape, wide.dtype)
    for half in halves:
        wide_query[half, part:] = mask_rows(coarse_window, heads)
    spill_row = lax.broadcasted_iota(jnp.int32, (SPILL, channels), 0)
    late = jnp.zeros((SPILL, width), jnp.float32)
    for slot in range(SLOTS):
        chosen = jnp.where(spill_row == slot, spill[...], jnp.zeros_like(spill))
        late += nn(chosen, pool_weight[slot * channels : (slot + 1) * channels])
    late = jnp.sum(late, 0, keepdims=True)
    at_last = lax.broadcasted_iota(jnp.int32, (owned, width), 0) == owned - 1
    parents[...] = bround(partial[...] + jnp.where(at_last, late, 0.0))
    normed, inverse = layer_norm(parents[...].astype(jnp.float32), 1)
    coarse_input[...] = bround(normed)
    upstream = out_grad[...]
    classes = window_rows(coarse_window)
    qkvs = [bround(nt(qkv_weights[half][...], coarse_input[...])) for half in halves]
    for half in halves:
        spread(wide_query.at[half], scaled(qkvs[half][:part]), heads)
    scores = [
        tn(jnp.concatenate([qkvs[half][part : 2 * part], classes], 0), wide_query[half])
        for half in halves
    ]
    parts = {}
    for half in halves:
        for head in range(0, heads, 2):
            at = slice(head * HD, (head + 2) * HD)
            pair = [
                softmax_parts(scores[half][:, i * LANES : (i + 1) * LANES])
                for i in (head, head + 1)
            ]
            parts[half, head] = pair
            values = qkvs[half][2 * part + head * HD : 2 * part + (head + 2) * HD]
            mixed[half, at] = mix_pair(values, pair)
            for i in range(2):
                rows = slice((head + i) * HD, (head + i + 1) * HD)
                lanes = slice((head + i) * LANES, (head + i + 1) * LANES)
                weighted = scaled(upward[half, rows]).astype(jnp.float32) * pair[i][1]
                wide_grad[half, rows, lanes] = bround(weighted)
    grad_probs = [tn(qkvs[half][2 * part :], wide_grad[half]) for half in halves]
    for half in halves:
        for head in range(0, heads, 2):
            at = [slice(i * part + head * HD, i * part + (head + 2) * HD) for i in range(3)]
            back = attend_back(
                qkvs[half][at[0]],
                qkvs[half][at[1]],
                upward[half, at[0]],
                mixed[half, at[0]],
                parts[half, head],
                grad_probs[half][:, head * LANES : (head + 2) * LANES],
            )
            for which in range(3):
                grads[half, at[which]] = back[which]
    grad_normed = sum(tn(grads[half], qkv_weights[half][...]) for half in halves)
    upstream_total = bround(
        upstream.astype(jnp.float32) + layer_norm_back(normed, inverse, grad_normed, 1)
    )
    grad_parents[...] = upstream_total
    grad_all = bround(nt(pool_weight[...], upstream_total))
    last = lax.broadcasted_iota(jnp.int32, (SPILL, owned), 1) == owned - 1
    spill_slot = lax.broadcasted_iota(jnp.int32, (SPILL, owned), 0)
    edge_total = jnp.zeros((SPILL, channels), jnp.float32)
    for slot in range(SLOTS):
        grad_slot = grad_all[slot * channels : (slot + 1) * channels]
        grad_pooled[slot // 2, :, slot % 2 * owned : (slot % 2 + 1) * owned] = grad_slot
        edge_total += nt(indicator(last & (spill_slot == slot)), grad_slot)
    next_upstream[...] = bround(tn(bround(edge_total), leading))


def coarse_weights(
    core_ref,
    grad_parents,
    children,
    spill,
    coarse_input,
    mixed,
    grads,
    out_grad,
    keep,
    give,
    pooled,
):
    core = core_ref[0]
    width = out_grad.shape[1]
    owned, channels = out_grad.shape[0], pooled.shape[1]
    part = mixed.shape[1]
    last = lax.broadcasted_iota(jnp.int32, (SPILL, owned), 1) == owned - 1
    spill_slot = lax.broadcasted_iota(jnp.int32, (SPILL, owned), 0)
    for slot in range(0, SLOTS, 2):
        edges = [indicator(last & (spill_slot == at)) for at in (slot, slot + 1)]
        edge = bround(tn(spill[...], jnp.concatenate(edges, 1)))
        pooled[slot] = children[slot] + edge[:, :owned]
        pooled[slot + 1] = children[slot + 1] + edge[:, owned:]
    panels = width // LANES

    def store(target, start, value):
        for panel in range(panels):
            at = start + panel * value.shape[0]
            target[at : at + value.shape[0]] = bround(
                value[:, panel * LANES : (panel + 1) * LANES]
            )

    for half, target in enumerate((keep, give)):
        store(target, 0, nn(grads[half], coarse_input[...]))
        store(target, 3 * part * panels, nn(mixed[half], out_grad[...]))
    base = 4 * part * panels
    for target, first in ((keep, core), (give, 1 - core)):
        for step in range(SLOTS // 2):
            grad_pool = nn(pooled[first * (SLOTS // 2) + step], grad_parents[...])
            store(target, base + step * panels * channels, grad_pool)


def fine_back(
    core_ref,
    first_parent,
    rows,
    packed,
    grad_pooled,
    next_upstream,
    parent_index,
    child_slot,
    out_weight,
    *rest,
):
    own, beyond = rest[:4], rest[4:8]
    upstreams, grads, keep, give, wide = rest[8:]
    channels, row_count = rows.shape
    owned = grad_pooled.shape[2] // 2
    heads = channels // HD
    all_rows = jnp.concatenate([rows[...], packed[:channels]], 1)
    mixed = jnp.concatenate([own[3][...], beyond[3][...]], 1)
    normed, _ = layer_norm(all_rows.astype(jnp.float32), 0)
    slot_of = slot_numbers(parent_index[...], child_slot[...], first_parent, owned)
    upstream = jnp.zeros((channels, row_count), jnp.float32)
    for slot in range(0, SLOTS, 2):
        both = jnp.concatenate([indicator(slot_of == slot), indicator(slot_of == slot + 1)], 0)
        upstream += nn(grad_pooled[slot // 2], both)
    upstream = jnp.concatenate([bround(upstream), next_upstream[...]], 1)
    upstreams[...] = upstream
    upward = bround(nn(out_weight[...], upstream))
    wide[...] = jnp.zeros(wide.shape, wide.dtype)
    blocks = row_count // LANES
    for block in range(blocks + 1):
        exponents, inverses, qkv, _ = own if block < blocks else beyond
        within = block % blocks
        lanes = slice(block * LANES, (block + 1) * LANES)
        inner = slice(within * LANES, (within + 1) * LANES)
        grad_rows = wide.at[block % wide.shape[0]]
        scales = [
            inverses[within * heads + head : within * heads + head + 1] for head in range(heads)
        ]
        for head in range(heads):
            at = slice(head * HD, (head + 1) * HD)
            weighted = scaled(upward[at, lanes]).astype(jnp.float32) * scales[head]
            grad_rows[at, head * LANES : (head + 1) * LANES] = bround(weighted)
        grad_probs = tn(qkv[2 * channels :, inner], grad_rows[...])
        for head in range(0, heads, 2):
            at = [slice(i * channels + head * HD, i * channels + (head + 2) * HD) for i in range(3)]
            parts = [
                (exponents[within, :, i * LANES : (i + 1) * LANES], scales[i])
                for i in (head, head + 1)
            ]
            back = attend_back(
                qkv[at[0], inner],
                qkv[at[1], inner],
                upward[at[0], lanes],
                mixed[at[0], lanes],
                parts,
                grad_probs[:, head * LANES : (head + 2) * LANES],
            )
            for which in range(3):
                grads[at[which], lanes] = back[which]
    grad_qkv = bround(nt(bround(normed), grads[...]))
    grad_out = bround(nt(mixed, upstream))
    core = core_ref[0]
    whole = 3 * channels // LANES
    panels = [grad_qkv[:, i * LANES : (i + 1) * LANES] for i in range(whole)]
    panels.append(jnp.concatenate([grad_qkv[:, whole * LANES :], grad_out[:, LANES:]], 1))
    panels.append(grad_out[:, :LANES])
    half = len(panels) // 2
    for i in range(half):
        at = slice(i * channels, (i + 1) * channels)
        keep[at] = jnp.where(core == 0, panels[i], panels[half + i])
        give[at] = jnp.where(core == 0, panels[half + i], panels[i])


def row_gradients(rows, packed, qkv_weight, upstream, grads, row_first, row_rest, row_next):
    channels, row_count = rows.shape
    all_rows = jnp.concatenate([rows[...], packed[:channels]], 1)
    normed, inverse = layer_norm(all_rows.astype(jnp.float32), 0)
    grad_normed = nn(qkv_weight[...], grads[...])
    total = upstream[...].astype(jnp.float32) + layer_norm_back(normed, inverse, grad_normed, 0)
    row_first[...] = total[:, :LANES]
    row_rest[...] = bround(total[:, LANES:row_count])
    row_next[...] = bround(total[:, row_count:])


def merge(keep, got, fine_keep, fine_got, total):
    first, second = keep.shape[0], fine_keep.shape[0]
    total[:first] = keep[...] + got[...]
    total[first : first + second] = fine_keep[...] + fine_got[...]
    pad = total.shape[0] - first - second
    total[first + second :] = jnp.zeros((pad, LANES), total.dtype)


class Copies:
    def __init__(self, arrived):
        self.arrived, self.started = arrived, []

    def start(self, source, target):
        copy = pltpu.make_async_copy(source, target, self.arrived.at[len(self.started)])
        copy.start()
        self.started.append(copy)

    def finish(self):
        for copy in self.started:
            copy.wait()


def unpack_pool(copies, source, start, half, staged, target, scale):
    panels = staged.shape[1] // LANES
    channels = staged.shape[0] * 2 // SLOTS
    for step in range(SLOTS // 2):
        rows = slice(step * channels, (step + 1) * channels)
        for panel in range(panels):
            at = start + (step * panels + panel) * channels
            staged[rows, panel * LANES : (panel + 1) * LANES] = (
                source[at : at + channels].astype(jnp.float32) * scale
            )
        row = pl.multiple_of(half * staged.shape[0] + step * channels, 8)
        copies.start(staged.at[rows], target.at[pl.ds(row, channels)])


def assemble_own(
    scale,
    core_ref,
    mine,
    row_first,
    row_late,
    row_rest,
    parents,
    mixed,
    own_out,
    other_out,
    grad_coarse_qkv,
    grad_coarse_out,
    grad_pool,
    row_grad,
    coarse_rows,
    rows_staged,
    first_staged,
    pool_staged,
    qkv_staged,
    out_staged,
    arrived,
):
    copies = Copies(arrived)
    first_staged[...] = bround(row_first[...] + row_late[...].astype(jnp.float32))
    copies.start(first_staged, row_grad.at[:, :LANES])
    copies.start(row_rest, row_grad.at[:, LANES:])
    part, width = out_staged.shape
    panels = width // LANES
    unpack_pool(
        copies, mine, 4 * part * panels, core_ref[0], pool_staged, grad_pool, scale
    )

    def coarse(start):
        return mine[start : start + part].astype(jnp.float32) * scale

    first = 3 * part * panels
    for which in range(3):
        for panel in range(panels):
            lanes = slice(panel * LANES, (panel + 1) * LANES)
            qkv_staged[which, :, lanes] = coarse((3 * panel + which) * part)
        copies.start(qkv_staged.at[which], grad_coarse_qkv.at[which])
    for panel in range(panels):
        out_staged[:, panel * LANES : (panel + 1) * LANES] = coarse(first + panel * part)
    copies.start(out_staged, grad_coarse_out)
    summed = tn(mixed[0], own_out[...]) + tn(mixed[1], other_out[...])
    rows_staged[...] = bround(parents[...].astype(jnp.float32) + summed)
    copies.start(rows_staged, coarse_rows)
    copies.finish()


def assemble_other(
    fine_scale,
    coarse_scale,
    base,
    core_ref,
    pool_in,
    mine,
    other,
    grad_pool,
    grad_qkv,
    grad_out,
    pool_staged,
    qkv_staged,
    out_staged,
    arrived,
):
    copies = Copies(arrived)
    core = core_ref[0]
    channels = out_staged.shape[0]
    edge = channels % LANES
    skip = pool_staged.shape[0] * pool_staged.shape[1] // LANES
    fine = []
    for half in range(2):
        for i in range(3):
            at = skip + i * channels
            near = mine[base + at : base + at + channels].astype(jnp.float32)
            far = other[at : at + channels].astype(jnp.float32)
            fine.append(jnp.where(core == half, near, far) * fine_scale)
    for i in range(4):
        qkv_staged[:, i * LANES : (i + 1) * LANES] = fine[i]
    qkv_staged[:, 4 * LANES :] = fine[4][:, :edge]
    copies.start(qkv_staged, grad_qkv)
    out_staged[:, :LANES] = fine[5]
    out_staged[:, LANES:] = fine[4][:, edge:]
    copies.start(out_staged, grad_out)
    unpack_pool(copies, other, 0, 1 - core, pool_staged, grad_pool, coarse_scale)
    copies.finish()


def call(
    kernel,
    outs,
    scratch,
    *operands,
    scalars=1,
    micros=1,
    hbm=0,
    copies=0,
    staged=(),
    to_hbm=False,
    aliases=None,
):
    spaces = [pltpu.SMEM] * scalars + [pltpu.HBM] * hbm
    spaces += [pltpu.VMEM] * (len(operands) - len(spaces))
    out_spaces = [pltpu.HBM if to_hbm else pltpu.VMEM] * len(outs)
    return pl.pallas_call(
        kernel,
        out_shape=[jax.ShapeDtypeStruct(shape, dtype) for shape, dtype in outs],
        in_specs=[pl.BlockSpec(memory_space=space) for space in spaces],
        out_specs=[pl.BlockSpec(memory_space=space) for space in out_spaces],
        input_output_aliases=aliases or {},
        scratch_shapes=[pltpu.VMEM(shape, jnp.bfloat16) for shape in scratch]
        + [pltpu.VMEM(shape, jnp.float32) for shape in staged]
        + ([pltpu.SemaphoreType.DMA((copies,))] if copies else []),
        compiler_params=pltpu.CompilerParams(vmem_limit_bytes=VMEM_BYTES),
        cost_estimate=pl.CostEstimate(
            flops=int(micros * 10**9), bytes_accessed=int(micros * 10**6), transcendentals=0
        ),
    )(*operands)


def float_sum(stacked):
    return bround(jnp.sum(stacked.astype(jnp.float32), 0))


def sum_over_chips(parts, rows_after):
    slab = float_sum(lax.all_to_all(parts, NEAR, 0, 0, tiled=True))
    copies = jnp.broadcast_to(slab, (lax.axis_size("zh"),) + slab.shape)
    slabs = lax.all_to_all(copies, "zh", 0, 0, tiled=True)
    slabs, *row_parts = rows_after(slabs)
    step = parts.shape[0] // 4
    (copies,) = call(
        sum_and_spread,
        [(parts.shape, parts.dtype)],
        [(step,) + slab.shape],
        slabs,
        scalars=0,
        copies=4,
        to_hbm=True,
        micros=0.5,
    )
    total = lax.all_to_all(copies, NEAR, 0, 0, tiled=True)
    return lax.optimization_barrier((total, *row_parts))


def on_device(
    fine_rows,
    qkv_weight,
    out_weight,
    pool_weight,
    coarse_qkv_weight,
    coarse_out_weight,
    parent_index,
    child_slot,
    out_grad,
):
    bf16, f32 = jnp.bfloat16, jnp.float32
    devices = 1
    for name in AXES:
        devices *= lax.axis_size(name)
    row_count, channels = fine_rows.shape
    owned, width = out_grad.shape
    part = coarse_out_weight.shape[0]
    blocks = row_count // LANES
    heads = channels // HD
    coarse_heads = part // HD
    coarse_count = 4 * part * width // LANES
    pool_count = SLOTS // 2 * channels * width // LANES
    fine_count = 2 * channels * channels // LANES
    core = lax.axis_index("sub").astype(jnp.int32).reshape(1)
    first_parent = (lax.axis_index(AXES) * owned).astype(jnp.int32).reshape(1)
    rows = fine_rows.T
    parent_row = parent_index.reshape(1, row_count)
    slot_row = child_slot.reshape(1, row_count)
    own_qkv = coarse_qkv_weight.transpose(0, 2, 1).reshape(3 * part, width)
    wide_rows = heads * LANES

    def in_hbm(*arrays):
        return [pltpu.with_memory_space_constraint(array, pltpu.HBM) for array in arrays]

    def like(*arrays):
        return [(array.shape, array.dtype) for array in arrays]

    def block_outs(count):
        return [
            ((channels, count * LANES), bf16),
            ((channels, count * LANES), bf16),
            ((3 * channels, count * LANES), bf16),
            ((count, LANES, wide_rows), bf16),
            ((count * heads, LANES), f32),
        ]

    sources = (rows, qkv_weight, out_weight, parent_row, slot_row)
    *brought, packed = call(
        bring,
        like(*sources) + [((channels + SPILL, LANES), bf16)],
        [],
        first_parent,
        *in_hbm(*sources),
        hbm=5,
        copies=5,
        micros=1,
    )
    rows, fine_qkv, fine_out, parent_row, slot_row = brought
    packed, give_qkv, give_out = lax.optimization_barrier((packed, own_qkv, coarse_out_weight))
    packed = passed_along(packed, -1)
    other_qkv = swap_cores(give_qkv)
    other_out = swap_cores(give_out)
    sources = (pool_weight, own_qkv, coarse_out_weight, out_grad)
    second = call(
        fine_forward,
        like(*sources) + block_outs(blocks),
        [(2, channels + SPILL, wide_rows)],
        *in_hbm(*sources),
        rows,
        fine_qkv,
        fine_out,
        scalars=0,
        hbm=4,
        copies=4,
        micros=4,
    )
    pool_weight, own_qkv, own_out, out_grad = second[:4]
    hidden, mixed_fine, qkv, exponents, inverses = second[4:]
    children, upward, partial = call(
        pool,
        [((SLOTS, channels, owned), bf16), ((2, part, owned), bf16), ((owned, width), f32)],
        [],
        first_parent,
        hidden,
        parent_row,
        slot_row,
        own_out,
        other_out,
        out_grad,
        pool_weight,
        micros=2,
    )
    (
        parents,
        spill,
        next_upstream,
        grad_parents,
        grad_pooled,
        coarse_input,
        mixed,
        grads,
        next_mixed,
        next_qkv,
        next_exponents,
        next_inverses,
    ) = call(
        coarse_both,
        [
            ((owned, width), bf16),
            ((SPILL, channels), bf16),
            ((channels, LANES), bf16),
            ((owned, width), bf16),
            ((SLOTS // 2, channels, 2 * owned), bf16),
            ((owned, width), bf16),
            ((2, part, owned), bf16),
            ((2, 3 * part, owned), bf16),
        ]
        + block_outs(1)[1:],
        [
            (channels, LANES),
            (1, channels + SPILL, wide_rows),
            (2, part + SPILL, coarse_heads * LANES),
            (2, part, coarse_heads * LANES),
        ],
        packed,
        fine_qkv,
        fine_out,
        partial,
        upward,
        pool_weight,
        own_qkv,
        other_qkv,
        out_grad,
        scalars=0,
        micros=8,
    )
    keep, give = call(
        coarse_weights,
        [
            ((coarse_count + pool_count, LANES), bf16),
            ((coarse_count + pool_count, LANES), bf16),
        ],
        [(SLOTS, channels, owned)],
        core,
        grad_parents,
        children,
        spill,
        coarse_input,
        mixed,
        grads,
        out_grad,
        micros=1,
    )
    got = swap_cores(give)
    upstream, fine_grads, fine_keep, fine_give = call(
        fine_back,
        [
            ((channels, row_count + LANES), bf16),
            ((3 * channels, row_count + LANES), bf16),
            ((fine_count, LANES), bf16),
            ((fine_count, LANES), bf16),
        ],
        [(2, channels, wide_rows)],
        core,
        first_parent,
        rows,
        packed,
        grad_pooled,
        next_upstream,
        parent_row,
        slot_row,
        fine_out,
        exponents,
        inverses,
        qkv,
        mixed_fine,
        next_exponents,
        next_inverses,
        next_qkv,
        next_mixed,
        scalars=2,
        micros=6,
    )

    def rows_after(dependence):
        dependence, given = lax.optimization_barrier((dependence, upstream))
        row_first, row_rest, row_next = call(
            row_gradients,
            [
                ((channels, LANES), f32),
                ((channels, row_count - LANES), bf16),
                ((channels, LANES), bf16),
            ],
            [],
            rows,
            packed,
            fine_qkv,
            given,
            fine_grads,
            scalars=0,
            micros=4,
        )
        return dependence, row_first, row_rest, passed_along(row_next, 1)

    fine_got = swap_cores(fine_give)
    plane = lax.axis_size("zl") * lax.axis_size("y") * lax.axis_size("x")
    count = coarse_count + pool_count + fine_count
    unit = plane * 8
    padded = -(-count // unit) * unit
    (merged,) = call(
        merge, [((padded, LANES), bf16)], [], keep, got, fine_keep, fine_got, scalars=0, micros=1
    )
    total, row_first, row_rest, row_late = sum_over_chips(
        merged.reshape(plane, padded // plane, LANES), rows_after
    )
    total = total.reshape(padded, LANES)
    other = swap_cores(total[coarse_count:count])
    coarse_scale = (owned * devices) ** (-0.5)
    pool_shape = (SLOTS * channels, width)
    half_pool = (SLOTS // 2 * channels, width)
    grad_coarse_qkv, grad_coarse_out, grad_pool, row_grad, coarse_rows = call(
        functools.partial(assemble_own, coarse_scale),
        [
            ((3, part, width), f32),
            ((part, width), f32),
            (pool_shape, f32),
            ((channels, row_count), bf16),
            ((owned, width), bf16),
        ],
        [(owned, width), (channels, LANES)],
        core,
        total,
        row_first,
        row_late,
        row_rest,
        parents,
        mixed,
        own_out,
        other_out,
        copies=7 + SLOTS // 2,
        staged=[half_pool, (3, part, width), (part, width)],
        to_hbm=True,
        micros=3,
    )
    grad_pool, grad_qkv, grad_out = call(
        functools.partial(
            assemble_other, (row_count * devices) ** (-0.5), coarse_scale, coarse_count
        ),
        [(pool_shape, f32), ((channels, 3 * channels), f32), ((channels, channels), f32)],
        [],
        core,
        grad_pool,
        total,
        other,
        hbm=1,
        copies=2 + SLOTS // 2,
        staged=[half_pool, (channels, 3 * channels), (channels, channels)],
        to_hbm=True,
        aliases={1: 0},
        micros=2,
    )
    return (
        coarse_rows,
        row_grad.T,
        grad_qkv,
        grad_out,
        grad_pool,
        grad_coarse_qkv.transpose(0, 2, 1),
        grad_coarse_out,
    )


def solution(mesh):
    torus = Mesh(mesh.devices.reshape(-1, 2, 4, 4, mesh.shape["sub"]), AXES)
    in_specs = (
        P(AXES, None),
        P(),
        P(),
        P(),
        P(None, None, "sub"),
        P("sub", None),
        P(AXES),
        P(AXES),
        P(AXES, None),
    )
    out_specs = (
        P(AXES, None),
        P(AXES, None),
        P(),
        P(),
        P(),
        P(None, None, "sub"),
        P("sub", None),
    )
    return jax.shard_map(
        on_device, mesh=torus, in_specs=in_specs, out_specs=out_specs, check_vma=False
    )
```
